128 devices in a mesh: gx: 16 (over y_lo, z, core), gy: 8 (over y_hi, x).
Axes of the slice: x: 4, y: 4 (y_hi: 2, y_lo: 2; y = y_hi * 2 + y_lo), z: 4, core: 2. Of those that a mesh axis runs over, the one named last changes fastest.
Arguments:
- populations: float32 [19, 256, 128, 512], P(None, 'gx', 'gy'), may hold values from 0.001 to 1.3
- solid: int32 [256, 128, 512], P('gx', 'gy'), may hold values from 0 to 1
- counts: float32 [64, 32, 16, 64], P(None, 'gx', None, 'gy'), may hold values from 0.02 to 45
- breakage: float32 [64, 64], replicated, may hold values from 0 to 4, as said below
- selection: float32 [64], replicated, may hold values from 0.05 to 1
Outputs:
- read: float32 [19, 256, 128, 512], P(None, 'gx', 'gy')
- counts_next: float32 [64, 32, 16, 64], P(None, 'gx', None, 'gy')
The draws below stay inside these ranges and needn't reach their ends.
Inputs may be any that keep to these rules, and one draw needn't show every extreme that they name: breakage is zero on and below the diagonal.
All inputs are finite; a program needn't handle non-finite values.
Results may differ from the reference program's by a relative error of at most 0.0001.
Values sent between devices are 32-bit elements; how exact they have to be, the bound alone decides.
A program may use at most 192 MiB of HBM per device.

```python
import math
import jax
import jax.numpy as jnp
from jax import lax

NZ = 512
K = 64
SUB = 4
NX = 256
NY = 128
NXC = 32
NYC = 16
NZC = 64


def draw_populations(key, part):
    key = jax.random.fold_in(key, 11)
    first, second = jax.random.split(key)
    density = jnp.exp(jax.random.uniform(first, (NX, NY, NZ), jnp.float32, -0.7, 0.7))
    noise = jax.random.uniform(second, (19, NX, NY, NZ), jnp.float32, -1.0, 1.0)
    amplitude = 0.6
    table = jnp.array([1.0 / 3.0] + [1.0 / 18.0] * 6 + [1.0 / 36.0] * 12, jnp.float32)
    return table[:, None, None, None] * density[None] * (1.0 + amplitude * noise)


def draw_solid(key, part):
    key = jax.random.fold_in(key, 12)
    first, second = jax.random.split(key)
    level = jax.random.randint(first, (NX // 8, NY // 8, NZ // 8), 0, 90)
    level = jnp.repeat(jnp.repeat(jnp.repeat(level, 8, 0), 8, 1), 8, 2)
    dice_values = jax.random.randint(second, (NX, NY, NZ), 0, 100)
    return (dice_values < level).astype(jnp.int32)


def draw_counts(key, part):
    key = jax.random.fold_in(key, 13)
    first, second = jax.random.split(key)
    overall = jax.random.uniform(first, (1, NXC, NYC, NZC), jnp.float32, -2.3, 2.3)
    spread = jax.random.uniform(second, (K, NXC, NYC, NZC), jnp.float32, -1.5, 1.5)
    return jnp.exp(overall + spread)


def draw_breakage(key, part):
    key = jax.random.fold_in(key, 14)
    values = jax.random.uniform(key, (K, K), jnp.float32, 0.0, 1.0)
    rows = jnp.arange(K)[:, None]
    cols = jnp.arange(K)[None, :]
    above = (rows < cols).astype(jnp.float32)
    return values * above * 4.0 / (cols.astype(jnp.float32) + 1.0)


def setup_inputs(seed: int = 0) -> dict:
    key_list = jax.random.split(jax.random.key(seed), 6)
    return {
        "populations": draw_populations(jax.random.fold_in(key_list[5], 71), 0),
        "solid": draw_solid(jax.random.fold_in(key_list[5], 71), 0),
        "counts": draw_counts(jax.random.fold_in(key_list[5], 71), 0),
        "breakage": draw_breakage(jax.random.fold_in(key_list[5], 71), 0),
        "selection": jnp.clip(jnp.exp(jax.random.uniform(key_list[4], (K,), jnp.float32, math.log(0.05), math.log(1.0))), 0.05, 1.0),
    }


velocities = ((0, 0, 0), (1, 0, 0), (-1, 0, 0), (0, 1, 0), (0, -1, 0), (0, 0, 1), (0, 0, -1), (1, 1, 0), (-1, -1, 0), (1, -1, 0), (-1, 1, 0), (1, 0, 1), (-1, 0, -1), (1, 0, -1), (-1, 0, 1), (0, 1, 1), (0, -1, -1), (0, 1, -1), (0, -1, 1))
lattice_weights = (1.0 / 3.0,) + (1.0 / 18.0,) * 6 + (1.0 / 36.0,) * 12
opposite = (0, 2, 1, 4, 3, 6, 5, 8, 7, 10, 9, 12, 11, 14, 13, 16, 15, 18, 17)

def expand(coarse):
    a, b, c = coarse.shape
    return jnp.broadcast_to(coarse[:, None, :, None, :, None], (a, 8, b, 8, c, 8)).reshape(a * 8, b * 8, c * 8)

def block_mean(field):
    a, b, c = field.shape
    return field.reshape(a // 8, 8, b // 8, 8, c // 8, 8).sum(axis=(1, 3, 5)) / 512.0

def relax_time(counts):
    classes = counts.shape[0]
    volume = (jnp.arange(classes).astype(jnp.float32) + 1.0) / classes
    load = lax.optimization_barrier(jnp.sum(volume[:, None, None, None] * counts, axis=0))
    packed = 0.5 * load / (1.0 + load)
    thinned = 1.0 - packed / 0.64
    return 0.5 + 3.0 * (0.04 / (thinned * thinned))

def heat_factor(tau):
    return (tau - 0.5) / (3.0 * tau * tau)

def collide(populations, tau_fine, fluid):
    rho = populations[0]
    for index in range(1, 19):
        rho = rho + populations[index]
    moments = [jnp.zeros_like(rho), jnp.zeros_like(rho), jnp.zeros_like(rho)]
    for index, vector in enumerate(velocities):
        for axis_num in range(3):
            if vector[axis_num] != 0:
                moments[axis_num] = moments[axis_num] + vector[axis_num] * populations[index]
    vel_x = moments[0] / rho
    vel_y = moments[1] / rho
    vel_z = moments[2] / rho
    speed_sq = vel_x * vel_x + vel_y * vel_y + vel_z * vel_z
    stress = [jnp.zeros_like(rho) for slot in range(6)]
    pairs = ((0, 0), (1, 1), (2, 2), (0, 1), (0, 2), (1, 2))
    posted = []
    for index, vector in enumerate(velocities):
        along = vector[0] * vel_x + vector[1] * vel_y + vector[2] * vel_z
        equil = lattice_weights[index] * rho * (1.0 + 3.0 * along + 4.5 * along * along - 1.5 * speed_sq)
        noneq = populations[index] - equil
        for slot, pair in enumerate(pairs):
            factor = vector[pair[0]] * vector[pair[1]]
            if factor != 0:
                stress[slot] = stress[slot] + factor * noneq
        posted.append(populations[index] - noneq / tau_fine)
    post = jnp.stack([jnp.where(fluid, posted[index], populations[opposite[index]]) for index in range(19)])
    square = stress[0] * stress[0] + stress[1] * stress[1] + stress[2] * stress[2]
    square = square + 2.0 * (stress[3] * stress[3] + stress[4] * stress[4] + stress[5] * stress[5])
    heat = jnp.where(fluid, 4.5 * square / (rho * rho), 0.0)
    return (post, heat)

def breakup(counts, eps, breakage, selection):
    strength = jnp.sqrt(50.0 * eps + 1e-06)
    rate = selection[:, None, None, None] * (strength / (1.0 + strength))[None]
    current = counts
    for step in range(SUB):
        lost = rate * current
        born = jnp.einsum('ij,jxyz->ixyz', breakage, lost, precision=lax.Precision.HIGHEST)
        current = current + 0.25 * (born - lost)
    return current

def reference(populations, solid, counts, breakage, selection):
    tau = relax_time(counts)
    tau_fine = expand(tau)
    post, heat = collide(populations, tau_fine, solid == 0)
    read = jnp.stack([jnp.roll(post[index], velocities[index], axis=(0, 1, 2)) for index in range(19)])
    eps = block_mean(heat * heat_factor(tau_fine))
    return (read, breakup(counts, eps, breakage, selection))
```

```python
import functools

import jax
import jax.numpy as jnp
from jax import lax
from jax.experimental import pallas as pl
from jax.experimental.pallas import tpu as pltpu
from jax.sharding import PartitionSpec as P

SUB = 4
MESH = pl.DeviceIdType.MESH
F32 = jnp.float32
HIGH = lax.Precision.HIGHEST

velocities = (
    (0, 0, 0),
    (1, 0, 0),
    (-1, 0, 0),
    (0, 1, 0),
    (0, -1, 0),
    (0, 0, 1),
    (0, 0, -1),
    (1, 1, 0),
    (-1, -1, 0),
    (1, -1, 0),
    (-1, 1, 0),
    (1, 0, 1),
    (-1, 0, -1),
    (1, 0, -1),
    (-1, 0, 1),
    (0, 1, 1),
    (0, -1, -1),
    (0, 1, -1),
    (0, -1, 1),
)
opposite = (0, 2, 1, 4, 3, 6, 5, 8, 7, 10, 9, 12, 11, 14, 13, 16, 15, 18, 17)

LEAVE_X = ((1, 7, 9, 11, 13), (2, 8, 10, 12, 14))
LEAVE_Y = ((3, 7, 10, 15, 17), (4, 8, 9, 16, 18))
LEAVE_Z = (5, 6, 11, 12, 13, 14, 15, 16, 17, 18)
CORNERS = ((7, 0, 1), (10, 0, -1), (9, 1, 1), (8, 1, -1))
TILES = tuple(slice(128 * t, 128 * t + 128) for t in range(4))


def iota(shape, axis):
    return lax.broadcasted_iota(jnp.int32, shape, axis)


def class_load(counts, lanes):
    volume = (iota((64, lanes), 0).astype(F32) + 1.0) / 64.0
    return jnp.dot(counts, volume, precision=HIGH, preferred_element_type=F32)


def relax_time(load):
    packed = 0.5 * load / (1.0 + load)
    thinned = 1.0 - packed / 0.64
    return 0.5 + 3.0 * (0.04 / (thinned * thinned))


def moments_of(f):
    even = {i: f[i] + f[i + 1] for i in range(1, 19, 2)}
    odd = {i: f[i] - f[i + 1] for i in range(1, 19, 2)}
    xy, xz, yz = even[7] + even[9], even[11] + even[13], even[15] + even[17]
    rho = f[0] + (even[1] + xy) + (even[3] + yz) + (even[5] + xz)
    jx = odd[1] + (odd[7] + odd[9]) + (odd[11] + odd[13])
    jy = odd[3] + (odd[7] - odd[9]) + (odd[15] + odd[17])
    jz = odd[5] + (odd[11] - odd[13]) + (odd[15] - odd[17])
    return even, (xy, xz, yz), rho, (jx, jy, jz)


def equilibrium(eighth, ux, uy, uz):
    tx, ty, tz = eighth * ux, eighth * uy, eighth * uz
    xx, yy, zz = tx * ux, ty * uy, tz * uz
    tx2, ty2 = tx + tx, ty + ty
    cross = (tx2 * uy, tx2 * uz, ty2 * uz)
    base = eighth * (8.0 / 36.0) - (xx + yy + zz) * (1.0 / 3.0)
    bx, by, bz = base + xx, base + yy, base + zz
    sums = (bx + yy, bx + zz, by + zz)
    return base, (bx, by, bz), sums, cross, (tx * (2.0 / 3.0), ty * (2.0 / 3.0), tz * (2.0 / 3.0))


def equilibrium_of(index, terms):
    base, axes, sums, cross, flow = terms
    c = velocities[index]
    nonzero = [a for a in range(3) if c[a] != 0]
    if not nonzero:
        return 12.0 * base
    if len(nonzero) == 1:
        (a,) = nonzero
        even = axes[a] + axes[a]
        odd = flow[a] + flow[a]
        return even + odd if c[a] > 0 else even - odd
    a, b = nonzero
    slot = {(0, 1): 0, (0, 2): 1, (1, 2): 2}[(a, b)]
    even = sums[slot] + cross[slot] if c[a] * c[b] > 0 else sums[slot] - cross[slot]
    odd = flow[a] + flow[b] if c[a] == c[b] else flow[a] - flow[b]
    return even + odd if c[a] > 0 else even - odd


def along_lanes(tiles, step):
    if step == 0:
        return tiles
    lane = iota((8, 128), 1)
    if step > 0:
        moved = [pltpu.roll(v, 1, 1) for v in tiles]
        return [jnp.where(lane == 0, moved[(t + 3) % 4], moved[t]) for t in range(4)]
    moved = [pltpu.roll(v, 127, 1) for v in tiles]
    return [jnp.where(lane == 127, moved[(t + 1) % 4], moved[t]) for t in range(4)]


def along_rows(low, high, step):
    if step == 0:
        return low, high
    row = iota((8, 128), 0)
    if step > 0:
        low, high = pltpu.roll(low, 1, 0), pltpu.roll(high, 1, 0)
        return jnp.where(row == 0, high, low), jnp.where(row == 0, low, high)
    low, high = pltpu.roll(low, 7, 0), pltpu.roll(high, 7, 0)
    return jnp.where(row == 7, high, low), jnp.where(row == 7, low, high)


def step_kernel(
    nx,
    ny,
    pop_hbm,
    solid_hbm,
    counts_hbm,
    moved,
    sums_in,
    pops,
    solid,
    counts,
    moments,
    heat_acc,
    sums_out,
    rate_out,
    rate_in,
    rates,
    staged,
    row_pops,
    row_solid,
    start_out,
    gain_out,
    edge_out,
    corner_in,
    corner_own,
    pop_sem,
    solid_sem,
    counts_sem,
    row_sem,
    rate_send,
    rate_recv,
    sums_send,
    sums_recv,
    edge_send,
    edge_recv,
    corner_send,
    corner_recv,
    onward_send,
    onward_recv,
):
    gx = lax.axis_index("gx")
    gy = lax.axis_index("gy")
    right, left = lax.rem(gx + 1, nx), lax.rem(gx + nx - 1, nx)
    up, down = lax.rem(gy + 1, ny), lax.rem(gy + ny - 1, ny)
    peers = [lax.rem(gy + d, ny) for d in range(ny)]

    counts_copy = pltpu.make_async_copy(counts_hbm, counts, counts_sem)
    counts_copy.start()
    barrier = pltpu.get_barrier_semaphore()
    partners = [(gx, peers[d]) for d in range(1, ny)] + [(left, gy), (right, gy)]
    for partner in partners:
        pl.semaphore_signal(barrier, inc=1, device_id=partner, device_id_type=MESH)

    def chunk_copy(chunk):
        rows = pl.ds(2 * chunk, 2)
        return pltpu.make_async_copy(pop_hbm.at[:, rows], pops.at[:, rows], pop_sem.at[chunk])

    def row_copies(side):
        y = 15 if side == 0 else 0
        return (
            pltpu.make_async_copy(solid_hbm.at[:, y], row_solid.at[side], row_sem.at[side, 0]),
            pltpu.make_async_copy(pop_hbm.at[:, :, y], row_pops.at[side], row_sem.at[side, 1]),
        )

    solid_copy = pltpu.make_async_copy(solid_hbm, solid, solid_sem)
    for side in range(2):
        for copy in row_copies(side):
            copy.start()
    solid_copy.start()
    for chunk in (0, 7, 1, 2, 3, 4, 5, 6):
        chunk_copy(chunk).start()

    counts_copy.wait()
    row, lane = iota((256, 128), 0), iota((256, 128), 1)
    load = class_load(counts[...], 128)
    load = jnp.where(row % 8 == (lane % 64) // 8, load, 0.0)
    slot, cell = iota((64, 256), 0), iota((64, 256), 1)
    wanted = ((slot % 8) // 2) * 16 + 2 * (slot // 8) + slot % 2
    pick = jnp.where((slot % 8 < 4) & (cell // 8 == wanted), 1.0, 0.0)
    load = jnp.dot(pick, load, precision=HIGH, preferred_element_type=F32)
    rate_out[...] = (1.0 / relax_time(load)).reshape(8, 8, 128)
    rate_in[pl.ds(gy, 1)] = rate_out[pl.ds(gy, 1)]

    pl.semaphore_wait(barrier, len(partners))

    def rate_copy(d):
        return pltpu.make_async_remote_copy(
            src_ref=rate_out.at[peers[d]],
            dst_ref=rate_in.at[gy],
            send_sem=rate_send.at[d],
            recv_sem=rate_recv.at[d],
            device_id=(gx, peers[d]),
            device_id_type=MESH,
        )

    for d in range(1, ny):
        rate_copy(d).start()

    heat_acc[...] = jnp.zeros_like(heat_acc)
    sums_out[...] = jnp.zeros_like(sums_out)

    def prepare(kind, side, tile):
        lanes = pl.ds(pl.multiple_of(tile * 128, 128), 128)
        leave = (LEAVE_X if kind == 0 else LEAVE_Y)[side]
        plane = 15 if side == 0 else 0
        for part in range(2):
            rows = slice(8 * part, 8 * part + 8)
            if kind == 0:
                f = [pops[index, plane, rows, lanes] for index in range(19)]
                fluid = solid[plane, rows, lanes] == 0
            else:
                f = [row_pops[side, index, rows, lanes] for index in range(19)]
                fluid = row_solid[side, rows, lanes] == 0
            _, _, rho, (jx, jy, jz) = moments_of(f)
            inverse = 1.0 / rho
            terms = equilibrium(rho * 0.125, jx * inverse, jy * inverse, jz * inverse)
            for place, index in enumerate(leave):
                start_out[kind, side, place, rows, lanes] = jnp.where(
                    fluid, f[index], f[opposite[index]]
                )
                gain_out[kind, side, place, rows, lanes] = jnp.where(
                    fluid, equilibrium_of(index, terms) - f[index], 0.0
                )

    for side in range(2):
        for copy in row_copies(side):
            copy.wait()

    def prepare_y(tile, carry):
        for side in range(2):
            prepare(1, side, tile)
        return carry

    lax.fori_loop(0, 4, prepare_y, 0)

    solid_copy.wait()
    for chunk in (0, 7):
        chunk_copy(chunk).wait()

    def prepare_x(tile, carry):
        for side in range(2):
            prepare(0, side, tile)
        return carry

    lax.fori_loop(0, 4, prepare_x, 0)

    def first_pass(chunk):
        half = chunk // 4

        def one_tile(tile, carry):
            lanes = pl.ds(pl.multiple_of(tile * 128, 128), 128)
            heats = []
            for part in range(4):
                plane, rows = 2 * chunk + part // 2, slice(8 * (part % 2), 8 * (part % 2) + 8)
                f = [pops[index, plane, rows, lanes] for index in range(19)]
                even, (xy, xz, yz), rho, (jx, jy, jz) = moments_of(f)
                inverse = 1.0 / rho
                ux, uy, uz = jx * inverse, jy * inverse, jz * inverse
                third = rho * (1.0 / 3.0)
                pxx = even[1] + (xy + xz) - third - jx * ux
                pyy = even[3] + (xy + yz) - third - jy * uy
                pzz = even[5] + (xz + yz) - third - jz * uz
                pxy = even[7] - even[9] - jx * uy
                pxz = even[11] - even[13] - jx * uz
                pyz = even[15] - even[17] - jy * uz
                off = pxy * pxy + pxz * pxz + pyz * pyz
                square = pxx * pxx + pyy * pyy + pzz * pzz + (off + off)
                heat = square * (inverse * inverse)
                heats.append(jnp.where(solid[plane, rows, lanes] == 0, heat, 0.0))
                for slot, value in enumerate((rho, ux, uy, uz)):
                    moments[slot, plane, rows, lanes] = value
            heat_acc[half * 2, tile] += heats[0] + heats[2]
            heat_acc[half * 2 + 1, tile] += heats[1] + heats[3]
            return carry

        lax.fori_loop(0, 4, one_tile, 0)

    def outer_chunks(step, carry):
        first_pass(step * 7)
        return carry

    def inner_chunks(chunk, carry):
        chunk_copy(chunk).wait()
        first_pass(chunk)
        return carry

    lax.fori_loop(0, 2, outer_chunks, 0)
    lax.fori_loop(1, 7, inner_chunks, 0)

    for d in range(1, ny):
        rate_copy(d).wait_recv()
    lane = iota((8, 128), 1)
    for tile in range(4):
        owned = jnp.where(lane < 64, rate_in[2 * tile], rate_in[2 * tile + 1])
        for block in range(4):
            rates[block, tile] = jnp.broadcast_to(owned[block : block + 1], (8, 128))

    def edge_copy(kind, side, place):
        index = (LEAVE_X if kind == 0 else LEAVE_Y)[side][place]
        source = edge_out.at[kind, side, place]
        if kind == 0:
            target = moved.at[index, 1 if side == 0 else 16]
            device = (right if side == 0 else left, gy)
        else:
            first = 1 + velocities[index][0]
            target = moved.at[index, first : first + 16, 0 if side == 0 else 15]
            device = (gx, up if side == 0 else down)
        return pltpu.make_async_remote_copy(
            src_ref=source,
            dst_ref=target,
            send_sem=edge_send.at[kind, side, place],
            recv_sem=edge_recv.at[kind, side, place],
            device_id=device,
            device_id_type=MESH,
        )

    def corner_copy(slot):
        index, side, step = CORNERS[slot]
        return pltpu.make_async_remote_copy(
            src_ref=edge_out.at[1, side, LEAVE_Y[side].index(index), 15 if step > 0 else 0],
            dst_ref=corner_in.at[slot, 0],
            send_sem=corner_send.at[slot],
            recv_sem=corner_recv.at[slot],
            device_id=(right if step > 0 else left, gy),
            device_id_type=MESH,
        )

    def onward_copy(slot):
        _, side, _ = CORNERS[slot]
        return pltpu.make_async_remote_copy(
            src_ref=corner_in.at[slot, 0],
            dst_ref=corner_own.at[slot, 0],
            send_sem=onward_send.at[slot],
            recv_sem=onward_recv.at[slot],
            device_id=(gx, up if side == 0 else down),
            device_id_type=MESH,
        )

    def leave(kind, side):
        for place, index in enumerate((LEAVE_X if kind == 0 else LEAVE_Y)[side]):
            c = velocities[index]
            values = []
            for part in range(2):
                rows = slice(8 * part, 8 * part + 8)
                far = 1 - side
                blocks = far * 2 + part if kind == 0 else part * 2 + far
                tiles = [
                    start_out[kind, side, place, rows, TILES[t]]
                    + rates[blocks, t] * gain_out[kind, side, place, rows, TILES[t]]
                    for t in range(4)
                ]
                values.append(along_lanes(tiles, c[2]))
            for t in range(4):
                low, high = along_rows(values[0][t], values[1][t], c[1] if kind == 0 else 0)
                edge_out[kind, side, place, 0:8, TILES[t]] = low
                edge_out[kind, side, place, 8:16, TILES[t]] = high
            edge_copy(kind, side, place).start()

    for kind in (1, 0):
        for side in range(2):
            leave(kind, side)
    for slot in range(4):
        corner_copy(slot).start()

    for tile in range(4):
        sums_out[tile, 0:4, :] = jnp.sum(heat_acc[:, tile], axis=1)
    sums_in[pl.ds(gy, 1)] = sums_out[pl.ds(gy // 2, 1)]

    def sums_copy(d):
        return pltpu.make_async_remote_copy(
            src_ref=sums_out.at[peers[d] // 2],
            dst_ref=sums_in.at[gy],
            send_sem=sums_send.at[d],
            recv_sem=sums_recv.at[d],
            device_id=(gx, peers[d]),
            device_id_type=MESH,
        )

    for d in range(1, ny):
        sums_copy(d).start()

    def put(index, plane, tile, low, high):
        c = velocities[index]
        place, lanes = plane + 1 + c[0], TILES[tile]
        low, high = along_rows(low, high, c[1])
        if c[1] > 0:
            moved[index, place, 1:8, lanes] = low[1:8]
        else:
            moved[index, place, 0:8, lanes] = low
        if c[1] < 0:
            moved[index, place, 8:15, lanes] = high[0:7]
        else:
            moved[index, place, 8:16, lanes] = high

    def collide(plane):
        half = plane // 8
        for tile in range(4):
            lanes = TILES[tile]
            found = []
            for part in range(2):
                rows = slice(8 * part, 8 * part + 8)
                rho, ux, uy, uz = [moments[slot, plane, rows, lanes] for slot in range(4)]
                rate = rates[half * 2 + part, tile]
                terms = equilibrium((rate * 0.125) * rho, ux, uy, uz)
                fluid = solid[plane, rows, lanes] == 0
                kept = 1.0 - rate
                f = [pops[index, plane, rows, lanes] for index in range(19)]
                found.append(
                    [
                        jnp.where(
                            fluid, kept * f[index] + equilibrium_of(index, terms), f[opposite[index]]
                        )
                        for index in range(19)
                    ]
                )
            for index in range(19):
                low, high = found[0][index], found[1][index]
                if index in LEAVE_Z:
                    staged[LEAVE_Z.index(index), 0:8, lanes] = low
                    staged[LEAVE_Z.index(index), 8:16, lanes] = high
                else:
                    put(index, plane, tile, low, high)

    def run_z(plane):
        for place, index in enumerate(LEAVE_Z):
            low = along_lanes([staged[place, 0:8, TILES[t]] for t in range(4)], velocities[index][2])
            high = along_lanes([staged[place, 8:16, TILES[t]] for t in range(4)], velocities[index][2])
            for t in range(4):
                put(index, plane, t, low[t], high[t])

    collide(0)

    def planes(plane, carry):
        run_z(plane - 1)
        collide(plane)
        return carry

    lax.fori_loop(1, 16, planes, 0)
    run_z(15)

    for slot in range(4):
        corner_copy(slot).wait_recv()
        onward_copy(slot).start()

    for kind in range(2):
        for side in range(2):
            for place in range(5):
                edge_copy(kind, side, place).wait_recv()
    for slot, (index, side, step) in enumerate(CORNERS):
        onward_copy(slot).wait_recv()
        row = 0 if side == 0 else 15
        moved[index, 1 if step > 0 else 16, row : row + 1, :] = corner_own[slot, 0:1, :]
    for d in range(1, ny):
        sums_copy(d).wait_recv()

    for d in range(1, ny):
        rate_copy(d).wait_send()
        sums_copy(d).wait_send()
    for kind in range(2):
        for side in range(2):
            for place in range(5):
                edge_copy(kind, side, place).wait_send()
    for slot in range(4):
        corner_copy(slot).wait_send()
        onward_copy(slot).wait_send()


def finish_kernel(
    moved,
    sums_in,
    counts_hbm,
    breakage_hbm,
    selection_hbm,
    read_hbm,
    next_hbm,
    counts,
    breakage,
    selection,
    result,
    small_sem,
    read_sem,
    next_sem,
):
    copies = [
        pltpu.make_async_copy(moved.at[index, 1:17], read_hbm.at[index], read_sem.at[index])
        for index in range(19)
    ]
    loads = [
        pltpu.make_async_copy(counts_hbm, counts, small_sem.at[0]),
        pltpu.make_async_copy(breakage_hbm, breakage, small_sem.at[1]),
        pltpu.make_async_copy(selection_hbm, selection, small_sem.at[2]),
    ]
    for copy in loads + copies:
        copy.start()
    for copy in loads:
        copy.wait()

    gy = lax.axis_index("gy")
    current = counts[...]
    tau = relax_time(class_load(current, 128))
    factor = (tau - 0.5) / (3.0 * tau * tau)
    row, slot = iota((256, 64), 0), iota((256, 64), 1)
    wanted = ((row // 8) % 16 // 2) * 8 + (row // 128) * 2 + (row // 8) % 2
    pick = jnp.where(slot == wanted, 1.0, 0.0)
    sums = jnp.dot(
        pick, sums_in[...].reshape(64, 128), precision=HIGH, preferred_element_type=F32
    )
    row, lane = iota((256, 128), 0), iota((256, 128), 1)
    sums = jnp.where(lane // 8 == row % 8 + 8 * lax.rem(gy, 2), sums, 0.0)
    sums = jnp.dot(sums, jnp.ones((128, 128), F32), precision=HIGH, preferred_element_type=F32)
    eps = sums * (4.5 / 512.0) * factor
    strength = jnp.sqrt(50.0 * eps + 1e-06)
    gain = strength / (1.0 + strength)
    rate = gain[:, :64] * selection[...][None, :]
    for step in range(SUB):
        lost = rate * current
        born = lax.dot_general(
            lost,
            breakage[...],
            (((1,), (1,)), ((), ())),
            precision=HIGH,
            preferred_element_type=F32,
        )
        current = current + 0.25 * (born - lost)
    result[...] = current
    last = pltpu.make_async_copy(result, next_hbm, next_sem)
    last.start()
    last.wait()
    for copy in copies:
        copy.wait()


def per_device(nx, ny, populations, solid, counts, breakage, selection):
    cells = counts.transpose(1, 2, 3, 0).reshape(256, 64)
    any_space = pl.BlockSpec(memory_space=pl.ANY)
    vmem = pl.BlockSpec(memory_space=pltpu.VMEM)
    dma = pltpu.SemaphoreType.DMA
    moved, sums = pl.pallas_call(
        functools.partial(step_kernel, nx, ny),
        out_shape=(
            pltpu.VMEM((19, 18, 16, 512), F32),
            pltpu.VMEM((8, 8, 128), F32),
        ),
        in_specs=[any_space] * 3,
        out_specs=(vmem, vmem),
        scratch_shapes=[
            pltpu.VMEM((19, 16, 16, 512), F32),
            pltpu.VMEM((16, 16, 512), jnp.int32),
            pltpu.VMEM((256, 64), F32),
            pltpu.VMEM((4, 16, 16, 512), F32),
            pltpu.VMEM((4, 4, 8, 128), F32),
            pltpu.VMEM((4, 8, 128), F32),
            pltpu.VMEM((8, 8, 128), F32),
            pltpu.VMEM((8, 8, 128), F32),
            pltpu.VMEM((4, 4, 8, 128), F32),
            pltpu.VMEM((10, 16, 512), F32),
            pltpu.VMEM((2, 19, 16, 512), F32),
            pltpu.VMEM((2, 16, 512), jnp.int32),
            pltpu.VMEM((2, 2, 5, 16, 512), F32),
            pltpu.VMEM((2, 2, 5, 16, 512), F32),
            pltpu.VMEM((2, 2, 5, 16, 512), F32),
            pltpu.VMEM((4, 8, 512), F32),
            pltpu.VMEM((4, 8, 512), F32),
            dma((8,)),
            dma,
            dma,
            dma((2, 2)),
            dma((8,)),
            dma((8,)),
            dma((8,)),
            dma((8,)),
            dma((2, 2, 5)),
            dma((2, 2, 5)),
            dma((4,)),
            dma((4,)),
            dma((4,)),
            dma((4,)),
        ],
        compiler_params=pltpu.CompilerParams(
            collective_id=0, has_side_effects=True, vmem_limit_bytes=40 * 1024 * 1024
        ),
        name="collide",
    )(*[pltpu.with_memory_space_constraint(x, pltpu.HBM) for x in (populations, solid, cells)])
    read, after = pl.pallas_call(
        finish_kernel,
        out_shape=(
            jax.ShapeDtypeStruct(populations.shape, F32),
            jax.ShapeDtypeStruct(cells.shape, F32),
        ),
        in_specs=[vmem] * 2 + [any_space] * 3,
        out_specs=(any_space, any_space),
        scratch_shapes=[
            pltpu.VMEM((256, 64), F32),
            pltpu.VMEM((64, 64), F32),
            pltpu.VMEM((64,), F32),
            pltpu.VMEM((256, 64), F32),
            dma((3,)),
            dma((19,)),
            dma,
        ],
        compiler_params=pltpu.CompilerParams(vmem_limit_bytes=24 * 1024 * 1024),
        name="finish",
    )(moved, sums, cells, breakage, selection)
    return (read, after.reshape(2, 16, 8, 64).transpose(3, 0, 1, 2))


def solution(mesh):
    in_specs = (P(None, "gx", "gy", None), P("gx", "gy", None), P(None, "gx", None, "gy"), P(), P())
    out_specs = (P(None, "gx", "gy", None), P(None, "gx", None, "gy"))
    return jax.shard_map(
        functools.partial(per_device, mesh.shape["gx"], mesh.shape["gy"]),
        mesh=mesh,
        in_specs=in_specs,
        out_specs=out_specs,
        check_vma=False,
    )
```

```python
import functools

import jax
import jax.numpy as jnp
from jax import lax
from jax.experimental import pallas as pl
from jax.experimental.pallas import tpu as pltpu
from jax.sharding import PartitionSpec as P

SUB = 4
MESH = pl.DeviceIdType.MESH
F32 = jnp.float32
HIGH = lax.Precision.HIGHEST

velocities = (
    (0, 0, 0),
    (1, 0, 0),
    (-1, 0, 0),
    (0, 1, 0),
    (0, -1, 0),
    (0, 0, 1),
    (0, 0, -1),
    (1, 1, 0),
    (-1, -1, 0),
    (1, -1, 0),
    (-1, 1, 0),
    (1, 0, 1),
    (-1, 0, -1),
    (1, 0, -1),
    (-1, 0, 1),
    (0, 1, 1),
    (0, -1, -1),
    (0, 1, -1),
    (0, -1, 1),
)
opposite = (0, 2, 1, 4, 3, 6, 5, 8, 7, 10, 9, 12, 11, 14, 13, 16, 15, 18, 17)

LEAVE_X = ((1, 7, 9, 11, 13), (2, 8, 10, 12, 14))
LEAVE_Y = ((3, 7, 10, 15, 17), (4, 8, 9, 16, 18))
LEAVE_Z = (5, 6, 11, 12, 13, 14, 15, 16, 17, 18)
CORNERS = ((7, 0, 1), (10, 0, -1), (9, 1, 1), (8, 1, -1))
TILES = tuple(slice(128 * t, 128 * t + 128) for t in range(4))


def iota(shape, axis):
    return lax.broadcasted_iota(jnp.int32, shape, axis)


def class_load(counts, lanes):
    volume = (iota((64, lanes), 0).astype(F32) + 1.0) / 64.0
    return jnp.dot(counts, volume, precision=HIGH, preferred_element_type=F32)


def relax_time(load):
    packed = 0.5 * load / (1.0 + load)
    thinned = 1.0 - packed / 0.64
    return 0.5 + 3.0 * (0.04 / (thinned * thinned))


def moments_of(f):
    even = {i: f[i] + f[i + 1] for i in range(1, 19, 2)}
    odd = {i: f[i] - f[i + 1] for i in range(1, 19, 2)}
    xy, xz, yz = even[7] + even[9], even[11] + even[13], even[15] + even[17]
    rho = f[0] + (even[1] + xy) + (even[3] + yz) + (even[5] + xz)
    jx = odd[1] + (odd[7] + odd[9]) + (odd[11] + odd[13])
    jy = odd[3] + (odd[7] - odd[9]) + (odd[15] + odd[17])
    jz = odd[5] + (odd[11] - odd[13]) + (odd[15] - odd[17])
    return even, (xy, xz, yz), rho, (jx, jy, jz)


def equilibrium(eighth, ux, uy, uz):
    tx, ty, tz = eighth * ux, eighth * uy, eighth * uz
    xx, yy, zz = tx * ux, ty * uy, tz * uz
    tx2, ty2 = tx + tx, ty + ty
    cross = (tx2 * uy, tx2 * uz, ty2 * uz)
    base = eighth * (8.0 / 36.0) - (xx + yy + zz) * (1.0 / 3.0)
    bx, by, bz = base + xx, base + yy, base + zz
    sums = (bx + yy, bx + zz, by + zz)
    return base, (bx, by, bz), sums, cross, (tx * (2.0 / 3.0), ty * (2.0 / 3.0), tz * (2.0 / 3.0))


def equilibrium_of(index, terms):
    base, axes, sums, cross, flow = terms
    c = velocities[index]
    nonzero = [a for a in range(3) if c[a] != 0]
    if not nonzero:
        return 12.0 * base
    if len(nonzero) == 1:
        (a,) = nonzero
        even = axes[a] + axes[a]
        odd = flow[a] + flow[a]
        return even + odd if c[a] > 0 else even - odd
    a, b = nonzero
    slot = {(0, 1): 0, (0, 2): 1, (1, 2): 2}[(a, b)]
    even = sums[slot] + cross[slot] if c[a] * c[b] > 0 else sums[slot] - cross[slot]
    odd = flow[a] + flow[b] if c[a] == c[b] else flow[a] - flow[b]
    return even + odd if c[a] > 0 else even - odd


def along_lanes(tiles, step):
    if step == 0:
        return tiles
    lane = iota((8, 128), 1)
    if step > 0:
        moved = [pltpu.roll(v, 1, 1) for v in tiles]
        return [jnp.where(lane == 0, moved[(t + 3) % 4], moved[t]) for t in range(4)]
    moved = [pltpu.roll(v, 127, 1) for v in tiles]
    return [jnp.where(lane == 127, moved[(t + 1) % 4], moved[t]) for t in range(4)]


def along_rows(low, high, step):
    if step == 0:
        return low, high
    row = iota((8, 128), 0)
    if step > 0:
        low, high = pltpu.roll(low, 1, 0), pltpu.roll(high, 1, 0)
        return jnp.where(row == 0, high, low), jnp.where(row == 0, low, high)
    low, high = pltpu.roll(low, 7, 0), pltpu.roll(high, 7, 0)
    return jnp.where(row == 7, high, low), jnp.where(row == 7, low, high)


def step_kernel(
    nx,
    ny,
    pop_hbm,
    solid_hbm,
    counts_hbm,
    moved,
    sums_in,
    pops,
    solid,
    counts,
    moments,
    heat_acc,
    sums_out,
    rate_out,
    rate_in,
    rates,
    staged,
    row_pops,
    row_solid,
    start_out,
    gain_out,
    edge_out,
    corner_in,
    corner_own,
    pop_sem,
    solid_sem,
    counts_sem,
    row_sem,
    rate_send,
    rate_recv,
    sums_send,
    sums_recv,
    edge_send,
    edge_recv,
    corner_send,
    corner_recv,
    onward_send,
    onward_recv,
):
    gx = lax.axis_index("gx")
    gy = lax.axis_index("gy")
    right, left = lax.rem(gx + 1, nx), lax.rem(gx + nx - 1, nx)
    up, down = lax.rem(gy + 1, ny), lax.rem(gy + ny - 1, ny)
    peers = [lax.rem(gy + d, ny) for d in range(ny)]

    counts_copy = pltpu.make_async_copy(counts_hbm, counts, counts_sem)
    counts_copy.start()
    barrier = pltpu.get_barrier_semaphore()
    partners = [(gx, peers[d]) for d in range(1, ny)] + [(left, gy), (right, gy)]
    for partner in partners:
        pl.semaphore_signal(barrier, inc=1, device_id=partner, device_id_type=MESH)

    def chunk_copy(chunk):
        rows = pl.ds(2 * chunk, 2)
        return pltpu.make_async_copy(pop_hbm.at[:, rows], pops.at[:, rows], pop_sem.at[chunk])

    def row_copies(side):
        y = 15 if side == 0 else 0
        return (
            pltpu.make_async_copy(solid_hbm.at[:, y], row_solid.at[side], row_sem.at[side, 0]),
            pltpu.make_async_copy(pop_hbm.at[:, :, y], row_pops.at[side], row_sem.at[side, 1]),
        )

    solid_copy = pltpu.make_async_copy(solid_hbm, solid, solid_sem)
    for side in range(2):
        for copy in row_copies(side):
            copy.start()
    solid_copy.start()
    for chunk in (0, 7, 1, 2):
        chunk_copy(chunk).start()

    counts_copy.wait()
    row, lane = iota((256, 128), 0), iota((256, 128), 1)
    load = class_load(counts[...], 128)
    load = jnp.where(row % 8 == (lane % 64) // 8, load, 0.0)
    slot, cell = iota((64, 256), 0), iota((64, 256), 1)
    wanted = ((slot % 8) // 2) * 16 + 2 * (slot // 8) + slot % 2
    pick = jnp.where((slot % 8 < 4) & (cell // 8 == wanted), 1.0, 0.0)
    load = jnp.dot(pick, load, precision=HIGH, preferred_element_type=F32)
    rate_out[...] = (1.0 / relax_time(load)).reshape(8, 8, 128)
    rate_in[pl.ds(gy, 1)] = rate_out[pl.ds(gy, 1)]

    pl.semaphore_wait(barrier, len(partners))

    def rate_copy(d):
        return pltpu.make_async_remote_copy(
            src_ref=rate_out.at[peers[d]],
            dst_ref=rate_in.at[gy],
            send_sem=rate_send.at[d],
            recv_sem=rate_recv.at[d],
            device_id=(gx, peers[d]),
            device_id_type=MESH,
        )

    for d in range(1, ny):
        rate_copy(d).start()

    heat_acc[...] = jnp.zeros_like(heat_acc)
    sums_out[...] = jnp.zeros_like(sums_out)

    def prepare(kind, side, tile):
        lanes = pl.ds(pl.multiple_of(tile * 128, 128), 128)
        leave = (LEAVE_X if kind == 0 else LEAVE_Y)[side]
        plane = 15 if side == 0 else 0
        for part in range(2):
            rows = slice(8 * part, 8 * part + 8)
            if kind == 0:
                f = [pops[index, plane, rows, lanes] for index in range(19)]
                fluid = solid[plane, rows, lanes] == 0
            else:
                f = [row_pops[side, index, rows, lanes] for index in range(19)]
                fluid = row_solid[side, rows, lanes] == 0
            _, _, rho, (jx, jy, jz) = moments_of(f)
            inverse = 1.0 / rho
            terms = equilibrium(rho * 0.125, jx * inverse, jy * inverse, jz * inverse)
            for place, index in enumerate(leave):
                start_out[kind, side, place, rows, lanes] = jnp.where(
                    fluid, f[index], f[opposite[index]]
                )
                gain_out[kind, side, place, rows, lanes] = jnp.where(
                    fluid, equilibrium_of(index, terms) - f[index], 0.0
                )

    for side in range(2):
        for copy in row_copies(side):
            copy.wait()

    def prepare_y(tile, carry):
        for side in range(2):
            prepare(1, side, tile)
        return carry

    lax.fori_loop(0, 4, prepare_y, 0)

    solid_copy.wait()
    for chunk in (0, 7):
        chunk_copy(chunk).wait()

    def prepare_x(tile, carry):
        for side in range(2):
            prepare(0, side, tile)
        return carry

    lax.fori_loop(0, 4, prepare_x, 0)

    def first_pass(chunk):
        half = chunk // 4

        def one_tile(tile, carry):
            lanes = pl.ds(pl.multiple_of(tile * 128, 128), 128)
            heats = []
            for part in range(4):
                plane, rows = 2 * chunk + part // 2, slice(8 * (part % 2), 8 * (part % 2) + 8)
                f = [pops[index, plane, rows, lanes] for index in range(19)]
                even, (xy, xz, yz), rho, (jx, jy, jz) = moments_of(f)
                inverse = 1.0 / rho
                ux, uy, uz = jx * inverse, jy * inverse, jz * inverse
                third = rho * (1.0 / 3.0)
                pxx = even[1] + (xy + xz) - third - jx * ux
                pyy = even[3] + (xy + yz) - third - jy * uy
                pzz = even[5] + (xz + yz) - third - jz * uz
                pxy = even[7] - even[9] - jx * uy
                pxz = even[11] - even[13] - jx * uz
                pyz = even[15] - even[17] - jy * uz
                off = pxy * pxy + pxz * pxz + pyz * pyz
                square = pxx * pxx + pyy * pyy + pzz * pzz + (off + off)
                heat = square * (inverse * inverse)
                heats.append(jnp.where(solid[plane, rows, lanes] == 0, heat, 0.0))
                for slot, value in enumerate((rho, ux, uy, uz)):
                    moments[slot, plane, rows, lanes] = value
            heat_acc[half * 2, tile] += heats[0] + heats[2]
            heat_acc[half * 2 + 1, tile] += heats[1] + heats[3]
            return carry

        lax.fori_loop(0, 4, one_tile, 0)

    def outer_chunks(step, carry):
        first_pass(step * 7)
        return carry

    def inner_chunks(chunk, carry):
        chunk_copy(chunk).wait()

        @pl.when(chunk < 5)
        def _():
            chunk_copy(chunk + 2).start()

        first_pass(chunk)
        return carry

    lax.fori_loop(0, 2, outer_chunks, 0)
    lax.fori_loop(1, 7, inner_chunks, 0)

    for d in range(1, ny):
        rate_copy(d).wait_recv()
    lane = iota((8, 128), 1)
    for tile in range(4):
        owned = jnp.where(lane < 64, rate_in[2 * tile], rate_in[2 * tile + 1])
        for block in range(4):
            rates[block, tile] = jnp.broadcast_to(owned[block : block + 1], (8, 128))

    def edge_copy(kind, side, place):
        index = (LEAVE_X if kind == 0 else LEAVE_Y)[side][place]
        source = edge_out.at[kind, side, place]
        if kind == 0:
            target = moved.at[index, 1 if side == 0 else 16]
            device = (right if side == 0 else left, gy)
        else:
            first = 1 + velocities[index][0]
            target = moved.at[index, first : first + 16, 0 if side == 0 else 15]
            device = (gx, up if side == 0 else down)
        return pltpu.make_async_remote_copy(
            src_ref=source,
            dst_ref=target,
            send_sem=edge_send.at[kind, side, place],
            recv_sem=edge_recv.at[kind, side, place],
            device_id=device,
            device_id_type=MESH,
        )

    def corner_copy(slot):
        index, side, step = CORNERS[slot]
        return pltpu.make_async_remote_copy(
            src_ref=edge_out.at[1, side, LEAVE_Y[side].index(index), 15 if step > 0 else 0],
            dst_ref=corner_in.at[slot, 0],
            send_sem=corner_send.at[slot],
            recv_sem=corner_recv.at[slot],
            device_id=(right if step > 0 else left, gy),
            device_id_type=MESH,
        )

    def onward_copy(slot):
        _, side, _ = CORNERS[slot]
        return pltpu.make_async_remote_copy(
            src_ref=corner_in.at[slot, 0],
            dst_ref=corner_own.at[slot, 0],
            send_sem=onward_send.at[slot],
            recv_sem=onward_recv.at[slot],
            device_id=(gx, up if side == 0 else down),
            device_id_type=MESH,
        )

    def leave(kind, side, place):
        index = (LEAVE_X if kind == 0 else LEAVE_Y)[side][place]
        c = velocities[index]
        values = []
        for part in range(2):
            rows = slice(8 * part, 8 * part + 8)
            far = 1 - side
            blocks = far * 2 + part if kind == 0 else part * 2 + far
            tiles = [
                start_out[kind, side, place, rows, TILES[t]]
                + rates[blocks, t] * gain_out[kind, side, place, rows, TILES[t]]
                for t in range(4)
            ]
            values.append(along_lanes(tiles, c[2]))
        for t in range(4):
            low, high = along_rows(values[0][t], values[1][t], c[1] if kind == 0 else 0)
            edge_out[kind, side, place, 0:8, TILES[t]] = low
            edge_out[kind, side, place, 8:16, TILES[t]] = high

    for slot, (index, side, _) in enumerate(CORNERS):
        leave(1, side, LEAVE_Y[side].index(index))
        corner_copy(slot).start()
    for place in range(5):
        for side in range(2):
            leave(0, side, place)
            edge_copy(0, side, place).start()
    for place in (1, 2, 0, 3, 4):
        for side in range(2):
            if (LEAVE_Y[side][place], side) not in [corner[:2] for corner in CORNERS]:
                leave(1, side, place)
            edge_copy(1, side, place).start()

    for tile in range(4):
        sums_out[tile, 0:4, :] = jnp.sum(heat_acc[:, tile], axis=1)
    sums_in[pl.ds(gy, 1)] = sums_out[pl.ds(gy // 2, 1)]

    def sums_copy(d):
        return pltpu.make_async_remote_copy(
            src_ref=sums_out.at[peers[d] // 2],
            dst_ref=sums_in.at[gy],
            send_sem=sums_send.at[d],
            recv_sem=sums_recv.at[d],
            device_id=(gx, peers[d]),
            device_id_type=MESH,
        )

    for d in range(1, ny):
        sums_copy(d).start()

    def put(index, plane, tile, low, high):
        c = velocities[index]
        place, lanes = plane + 1 + c[0], TILES[tile]
        low, high = along_rows(low, high, c[1])
        if c[1] > 0:
            moved[index, place, 1:8, lanes] = low[1:8]
        else:
            moved[index, place, 0:8, lanes] = low
        if c[1] < 0:
            moved[index, place, 8:15, lanes] = high[0:7]
        else:
            moved[index, place, 8:16, lanes] = high

    def collide(plane):
        half = plane // 8
        for tile in range(4):
            lanes = TILES[tile]
            found = []
            for part in range(2):
                rows = slice(8 * part, 8 * part + 8)
                rho, ux, uy, uz = [moments[slot, plane, rows, lanes] for slot in range(4)]
                rate = rates[half * 2 + part, tile]
                terms = equilibrium((rate * 0.125) * rho, ux, uy, uz)
                fluid = solid[plane, rows, lanes] == 0
                kept = 1.0 - rate
                f = [pops[index, plane, rows, lanes] for index in range(19)]
                found.append(
                    [
                        jnp.where(
                            fluid, kept * f[index] + equilibrium_of(index, terms), f[opposite[index]]
                        )
                        for index in range(19)
                    ]
                )
            for index in range(19):
                low, high = found[0][index], found[1][index]
                if index in LEAVE_Z:
                    staged[LEAVE_Z.index(index), 0:8, lanes] = low
                    staged[LEAVE_Z.index(index), 8:16, lanes] = high
                else:
                    put(index, plane, tile, low, high)

    def run_z(plane):
        for place, index in enumerate(LEAVE_Z):
            low = along_lanes([staged[place, 0:8, TILES[t]] for t in range(4)], velocities[index][2])
            high = along_lanes([staged[place, 8:16, TILES[t]] for t in range(4)], velocities[index][2])
            for t in range(4):
                put(index, plane, t, low[t], high[t])

    collide(0)

    def planes(plane, carry):
        run_z(plane - 1)
        collide(plane)
        return carry

    def some_planes(half, carry):
        lax.fori_loop(1 + 8 * half, 9 + 7 * half, planes, 0)

        @pl.when(half == 0)
        def _():
            for slot in range(4):
                corner_copy(slot).wait_recv()
                onward_copy(slot).start()

        return carry

    lax.fori_loop(0, 2, some_planes, 0)
    run_z(15)

    for kind in range(2):
        for side in range(2):
            for place in range(5):
                edge_copy(kind, side, place).wait_recv()
    for slot, (index, side, step) in enumerate(CORNERS):
        onward_copy(slot).wait_recv()
        row = 0 if side == 0 else 15
        moved[index, 1 if step > 0 else 16, row : row + 1, :] = corner_own[slot, 0:1, :]
    for d in range(1, ny):
        sums_copy(d).wait_recv()

    for d in range(1, ny):
        rate_copy(d).wait_send()
        sums_copy(d).wait_send()
    for kind in range(2):
        for side in range(2):
            for place in range(5):
                edge_copy(kind, side, place).wait_send()
    for slot in range(4):
        corner_copy(slot).wait_send()
        onward_copy(slot).wait_send()


def finish_kernel(
    moved,
    sums_in,
    counts_hbm,
    breakage_hbm,
    selection_hbm,
    read_hbm,
    next_hbm,
    counts,
    breakage,
    selection,
    result,
    small_sem,
    read_sem,
    next_sem,
):
    copies = [
        pltpu.make_async_copy(moved.at[index, 1:17], read_hbm.at[index], read_sem.at[index])
        for index in range(19)
    ]
    loads = [
        pltpu.make_async_copy(counts_hbm, counts, small_sem.at[0]),
        pltpu.make_async_copy(breakage_hbm, breakage, small_sem.at[1]),
        pltpu.make_async_copy(selection_hbm, selection, small_sem.at[2]),
    ]
    for copy in copies + loads:
        copy.start()
    for copy in loads:
        copy.wait()

    gy = lax.axis_index("gy")
    current = counts[...]
    tau = relax_time(class_load(current, 128))
    factor = (tau - 0.5) / (3.0 * tau * tau)
    row, slot = iota((256, 64), 0), iota((256, 64), 1)
    wanted = ((row // 8) % 16 // 2) * 8 + (row // 128) * 2 + (row // 8) % 2
    pick = jnp.where(slot == wanted, 1.0, 0.0)
    sums = jnp.dot(
        pick, sums_in[...].reshape(64, 128), precision=HIGH, preferred_element_type=F32
    )
    row, lane = iota((256, 128), 0), iota((256, 128), 1)
    sums = jnp.where(lane // 8 == row % 8 + 8 * lax.rem(gy, 2), sums, 0.0)
    sums = jnp.dot(sums, jnp.ones((128, 128), F32), precision=HIGH, preferred_element_type=F32)
    eps = sums * (4.5 / 512.0) * factor
    strength = jnp.sqrt(50.0 * eps + 1e-06)
    gain = strength / (1.0 + strength)
    rate = gain[:, :64] * selection[...][None, :]
    for step in range(SUB):
        lost = rate * current
        born = lax.dot_general(
            lost,
            breakage[...],
            (((1,), (1,)), ((), ())),
            precision=HIGH,
            preferred_element_type=F32,
        )
        current = current + 0.25 * (born - lost)
    result[...] = current
    last = pltpu.make_async_copy(result, next_hbm, next_sem)
    last.start()
    last.wait()
    for copy in copies:
        copy.wait()


def per_device(nx, ny, populations, solid, counts, breakage, selection):
    cells = counts.transpose(1, 2, 3, 0).reshape(256, 64)
    any_space = pl.BlockSpec(memory_space=pl.ANY)
    vmem = pl.BlockSpec(memory_space=pltpu.VMEM)
    dma = pltpu.SemaphoreType.DMA
    moved, sums = pl.pallas_call(
        functools.partial(step_kernel, nx, ny),
        out_shape=(
            pltpu.VMEM((19, 18, 16, 512), F32),
            pltpu.VMEM((8, 8, 128), F32),
        ),
        in_specs=[any_space] * 3,
        out_specs=(vmem, vmem),
        scratch_shapes=[
            pltpu.VMEM((19, 16, 16, 512), F32),
            pltpu.VMEM((16, 16, 512), jnp.int32),
            pltpu.VMEM((256, 64), F32),
            pltpu.VMEM((4, 16, 16, 512), F32),
            pltpu.VMEM((4, 4, 8, 128), F32),
            pltpu.VMEM((4, 8, 128), F32),
            pltpu.VMEM((8, 8, 128), F32),
            pltpu.VMEM((8, 8, 128), F32),
            pltpu.VMEM((4, 4, 8, 128), F32),
            pltpu.VMEM((10, 16, 512), F32),
            pltpu.VMEM((2, 19, 16, 512), F32),
            pltpu.VMEM((2, 16, 512), jnp.int32),
            pltpu.VMEM((2, 2, 5, 16, 512), F32),
            pltpu.VMEM((2, 2, 5, 16, 512), F32),
            pltpu.VMEM((2, 2, 5, 16, 512), F32),
            pltpu.VMEM((4, 8, 512), F32),
            pltpu.VMEM((4, 8, 512), F32),
            dma((8,)),
            dma,
            dma,
            dma((2, 2)),
            dma((8,)),
            dma((8,)),
            dma((8,)),
            dma((8,)),
            dma((2, 2, 5)),
            dma((2, 2, 5)),
            dma((4,)),
            dma((4,)),
            dma((4,)),
            dma((4,)),
        ],
        compiler_params=pltpu.CompilerParams(
            collective_id=0, has_side_effects=True, vmem_limit_bytes=40 * 1024 * 1024
        ),
        name="collide",
    )(*[pltpu.with_memory_space_constraint(x, pltpu.HBM) for x in (populations, solid, cells)])
    read, after = pl.pallas_call(
        finish_kernel,
        out_shape=(
            jax.ShapeDtypeStruct(populations.shape, F32),
            jax.ShapeDtypeStruct(cells.shape, F32),
        ),
        in_specs=[vmem] * 2 + [any_space] * 3,
        out_specs=(any_space, any_space),
        scratch_shapes=[
            pltpu.VMEM((256, 64), F32),
            pltpu.VMEM((64, 64), F32),
            pltpu.VMEM((64,), F32),
            pltpu.VMEM((256, 64), F32),
            dma((3,)),
            dma((19,)),
            dma,
        ],
        compiler_params=pltpu.CompilerParams(vmem_limit_bytes=24 * 1024 * 1024),
        name="finish",
    )(moved, sums, cells, breakage, selection)
    return (read, after.reshape(2, 16, 8, 64).transpose(3, 0, 1, 2))


def solution(mesh):
    in_specs = (P(None, "gx", "gy", None), P("gx", "gy", None), P(None, "gx", None, "gy"), P(), P())
    out_specs = (P(None, "gx", "gy", None), P(None, "gx", None, "gy"))
    return jax.shard_map(
        functools.partial(per_device, mesh.shape["gx"], mesh.shape["gy"]),
        mesh=mesh,
        in_specs=in_specs,
        out_specs=out_specs,
        check_vma=False,
    )
```

```python
import functools

import jax
import jax.numpy as jnp
from jax import lax
from jax.experimental import pallas as pl
from jax.experimental.pallas import tpu as pltpu
from jax.sharding import PartitionSpec as P

SUB = 4
MESH = pl.DeviceIdType.MESH
F32 = jnp.float32
HIGH = lax.Precision.HIGHEST

velocities = (
    (0, 0, 0),
    (1, 0, 0),
    (-1, 0, 0),
    (0, 1, 0),
    (0, -1, 0),
    (0, 0, 1),
    (0, 0, -1),
    (1, 1, 0),
    (-1, -1, 0),
    (1, -1, 0),
    (-1, 1, 0),
    (1, 0, 1),
    (-1, 0, -1),
    (1, 0, -1),
    (-1, 0, 1),
    (0, 1, 1),
    (0, -1, -1),
    (0, 1, -1),
    (0, -1, 1),
)
opposite = (0, 2, 1, 4, 3, 6, 5, 8, 7, 10, 9, 12, 11, 14, 13, 16, 15, 18, 17)

LEAVE_X = ((1, 7, 9, 11, 13), (2, 8, 10, 12, 14))
LEAVE_Y = ((3, 7, 10, 15, 17), (4, 8, 9, 16, 18))
LEAVE_Z = (5, 6, 11, 12, 13, 14, 15, 16, 17, 18)
CORNERS = ((7, 1, 1), (10, -1, 1), (9, 1, -1), (8, -1, -1))
FLAT = tuple(i for i in range(19) if velocities[i][1] == 0)
TILES = tuple(slice(128 * t, 128 * t + 128) for t in range(4))


def iota(shape, axis):
    return lax.broadcasted_iota(jnp.int32, shape, axis)


def class_load(counts, lanes):
    volume = (iota((64, lanes), 0).astype(F32) + 1.0) / 64.0
    return jnp.dot(counts, volume, precision=HIGH, preferred_element_type=F32)


def relax_time(load):
    packed = 0.5 * load / (1.0 + load)
    thinned = 1.0 - packed / 0.64
    return 0.5 + 3.0 * (0.04 / (thinned * thinned))


def moments_of(f):
    even = {i: f[i] + f[i + 1] for i in range(1, 19, 2)}
    odd = {i: f[i] - f[i + 1] for i in range(1, 19, 2)}
    xy, xz, yz = even[7] + even[9], even[11] + even[13], even[15] + even[17]
    rho = f[0] + (even[1] + xy) + (even[3] + yz) + (even[5] + xz)
    jx = odd[1] + (odd[7] + odd[9]) + (odd[11] + odd[13])
    jy = odd[3] + (odd[7] - odd[9]) + (odd[15] + odd[17])
    jz = odd[5] + (odd[11] - odd[13]) + (odd[15] - odd[17])
    return even, (xy, xz, yz), rho, (jx, jy, jz)


def equilibrium(eighth, ux, uy, uz):
    tx, ty, tz = eighth * ux, eighth * uy, eighth * uz
    xx, yy, zz = tx * ux, ty * uy, tz * uz
    tx2, ty2 = tx + tx, ty + ty
    cross = (tx2 * uy, tx2 * uz, ty2 * uz)
    base = eighth * (8.0 / 36.0) - (xx + yy + zz) * (1.0 / 3.0)
    bx, by, bz = base + xx, base + yy, base + zz
    sums = (bx + yy, bx + zz, by + zz)
    return base, (bx, by, bz), sums, cross, (tx * (2.0 / 3.0), ty * (2.0 / 3.0), tz * (2.0 / 3.0))


def equilibrium_of(index, terms):
    base, axes, sums, cross, flow = terms
    c = velocities[index]
    nonzero = [a for a in range(3) if c[a] != 0]
    if not nonzero:
        return 12.0 * base
    if len(nonzero) == 1:
        (a,) = nonzero
        even = axes[a] + axes[a]
        odd = flow[a] + flow[a]
        return even + odd if c[a] > 0 else even - odd
    a, b = nonzero
    slot = {(0, 1): 0, (0, 2): 1, (1, 2): 2}[(a, b)]
    even = sums[slot] + cross[slot] if c[a] * c[b] > 0 else sums[slot] - cross[slot]
    odd = flow[a] + flow[b] if c[a] == c[b] else flow[a] - flow[b]
    return even + odd if c[a] > 0 else even - odd


def along_lanes(tiles, step):
    if step == 0:
        return tiles
    lane = iota((8, 128), 1)
    if step > 0:
        moved = [pltpu.roll(v, 1, 1) for v in tiles]
        return [jnp.where(lane == 0, moved[(t + 3) % 4], moved[t]) for t in range(4)]
    moved = [pltpu.roll(v, 127, 1) for v in tiles]
    return [jnp.where(lane == 127, moved[(t + 1) % 4], moved[t]) for t in range(4)]


def along_rows(low, high, step):
    if step == 0:
        return low, high
    row = iota((8, 128), 0)
    if step > 0:
        low, high = pltpu.roll(low, 1, 0), pltpu.roll(high, 1, 0)
        return jnp.where(row == 0, high, low), jnp.where(row == 0, low, high)
    low, high = pltpu.roll(low, 7, 0), pltpu.roll(high, 7, 0)
    return jnp.where(row == 7, high, low), jnp.where(row == 7, low, high)


def step_kernel(
    nx,
    ny,
    pop_hbm,
    solid_hbm,
    counts_hbm,
    moved,
    y_rows,
    sums_in,
    pops,
    solid,
    counts,
    moments,
    heat_acc,
    sums_out,
    rate_out,
    rate_in,
    rates,
    staged,
    row_pops,
    row_solid,
    start_out,
    gain_out,
    edge_out,
    y_out,
    y_in,
    corner_in,
    pop_sem,
    solid_sem,
    counts_sem,
    row_sem,
    rate_send,
    rate_recv,
    sums_send,
    sums_recv,
    edge_send,
    edge_recv,
    y_send,
    y_recv,
    corner_send,
    corner_recv,
):
    gx = lax.axis_index("gx")
    gy = lax.axis_index("gy")
    right, left = lax.rem(gx + 1, nx), lax.rem(gx + nx - 1, nx)
    up, down = lax.rem(gy + 1, ny), lax.rem(gy + ny - 1, ny)
    peers = [lax.rem(gy + d, ny) for d in range(ny)]

    counts_copy = pltpu.make_async_copy(counts_hbm, counts, counts_sem)
    counts_copy.start()
    barrier = pltpu.get_barrier_semaphore()
    partners = [(gx, peers[d]) for d in range(1, ny)]
    partners += [(x, y) for x in (left, right) for y in (gy, up, down)]
    for partner in partners:
        pl.semaphore_signal(barrier, inc=1, device_id=partner, device_id_type=MESH)

    def chunk_copy(chunk):
        rows = pl.ds(2 * chunk, 2)
        return pltpu.make_async_copy(pop_hbm.at[:, rows], pops.at[:, rows], pop_sem.at[chunk])

    def row_copies(side):
        y = 15 if side == 0 else 0
        return (
            pltpu.make_async_copy(solid_hbm.at[:, y], row_solid.at[side], row_sem.at[side, 0]),
            pltpu.make_async_copy(pop_hbm.at[:, :, y], row_pops.at[side], row_sem.at[side, 1]),
        )

    solid_copy = pltpu.make_async_copy(solid_hbm, solid, solid_sem)
    for side in range(2):
        for copy in row_copies(side):
            copy.start()
    solid_copy.start()
    for chunk in (0, 7, 1, 2):
        chunk_copy(chunk).start()

    counts_copy.wait()
    row, lane = iota((256, 128), 0), iota((256, 128), 1)
    load = class_load(counts[...], 128)
    load = jnp.where(row % 8 == (lane % 64) // 8, load, 0.0)
    slot, cell = iota((64, 256), 0), iota((64, 256), 1)
    wanted = ((slot % 8) // 4) * 16 + (2 * (slot // 8) + 15 + slot % 4) % 16
    pick = jnp.where(cell // 8 == wanted, 1.0, 0.0)
    load = jnp.dot(pick, load, precision=HIGH, preferred_element_type=F32)
    rate_out[...] = (1.0 / relax_time(load)).reshape(8, 8, 128)
    rate_in[pl.ds(gy, 1)] = rate_out[pl.ds(gy, 1)]

    pl.semaphore_wait(barrier, len(partners))

    def rate_copy(d):
        return pltpu.make_async_remote_copy(
            src_ref=rate_out.at[peers[d]],
            dst_ref=rate_in.at[gy],
            send_sem=rate_send.at[d],
            recv_sem=rate_recv.at[d],
            device_id=(gx, peers[d]),
            device_id_type=MESH,
        )

    for d in range(1, ny):
        rate_copy(d).start()

    heat_acc[...] = jnp.zeros_like(heat_acc)
    sums_out[...] = jnp.zeros_like(sums_out)

    def prepare_y(tile, carry):
        lanes = pl.ds(pl.multiple_of(tile * 128, 128), 128)
        for side in range(2):
            for part in range(2):
                rows = slice(8 * part, 8 * part + 8)
                f = [row_pops[side, index, rows, lanes] for index in range(19)]
                fluid = row_solid[side, rows, lanes] == 0
                _, _, rho, flow = moments_of(f)
                inverse = 1.0 / rho
                for place, index in enumerate(LEAVE_Y[side]):
                    y_out[side, place, rows, lanes] = jnp.where(fluid, f[index], f[opposite[index]])
                y_out[side, 5, rows, lanes] = jnp.where(fluid, rho, 0.0)
                for axis in range(3):
                    y_out[side, 6 + axis, rows, lanes] = flow[axis] * inverse
        return carry

    def y_copy(side):
        return pltpu.make_async_remote_copy(
            src_ref=y_out.at[side],
            dst_ref=y_in.at[side],
            send_sem=y_send.at[side],
            recv_sem=y_recv.at[side],
            device_id=(gx, up if side == 0 else down),
            device_id_type=MESH,
        )

    for side in range(2):
        for copy in row_copies(side):
            copy.wait()
    lax.fori_loop(0, 4, prepare_y, 0)
    for side in range(2):
        y_copy(side).start()

    def prepare_x(tile, carry):
        lanes = pl.ds(pl.multiple_of(tile * 128, 128), 128)
        for side in range(2):
            plane = 15 if side == 0 else 0
            for part in range(2):
                rows = slice(8 * part, 8 * part + 8)
                f = [pops[index, plane, rows, lanes] for index in range(19)]
                fluid = solid[plane, rows, lanes] == 0
                _, _, rho, (jx, jy, jz) = moments_of(f)
                inverse = 1.0 / rho
                terms = equilibrium(rho * 0.125, jx * inverse, jy * inverse, jz * inverse)
                for place, index in enumerate(LEAVE_X[side]):
                    start_out[side, place, rows, lanes] = jnp.where(
                        fluid, f[index], f[opposite[index]]
                    )
                    gain_out[side, place, rows, lanes] = jnp.where(
                        fluid, equilibrium_of(index, terms) - f[index], 0.0
                    )
        return carry

    solid_copy.wait()
    for chunk in (0, 7):
        chunk_copy(chunk).wait()

    lax.fori_loop(0, 4, prepare_x, 0)

    def first_pass(chunk):
        half = chunk // 4

        def one_tile(tile, carry):
            lanes = pl.ds(pl.multiple_of(tile * 128, 128), 128)
            heats = []
            for part in range(4):
                plane, rows = 2 * chunk + part // 2, slice(8 * (part % 2), 8 * (part % 2) + 8)
                f = [pops[index, plane, rows, lanes] for index in range(19)]
                even, (xy, xz, yz), rho, (jx, jy, jz) = moments_of(f)
                inverse = 1.0 / rho
                ux, uy, uz = jx * inverse, jy * inverse, jz * inverse
                third = rho * (1.0 / 3.0)
                pxx = even[1] + (xy + xz) - third - jx * ux
                pyy = even[3] + (xy + yz) - third - jy * uy
                pzz = even[5] + (xz + yz) - third - jz * uz
                pxy = even[7] - even[9] - jx * uy
                pxz = even[11] - even[13] - jx * uz
                pyz = even[15] - even[17] - jy * uz
                off = pxy * pxy + pxz * pxz + pyz * pyz
                square = pxx * pxx + pyy * pyy + pzz * pzz + (off + off)
                heat = square * (inverse * inverse)
                heats.append(jnp.where(solid[plane, rows, lanes] == 0, heat, 0.0))
                for slot, value in enumerate((rho, ux, uy, uz)):
                    moments[slot, plane, rows, lanes] = value
            heat_acc[half * 2, tile] += heats[0] + heats[2]
            heat_acc[half * 2 + 1, tile] += heats[1] + heats[3]
            return carry

        lax.fori_loop(0, 4, one_tile, 0)

    def outer_chunks(step, carry):
        first_pass(step * 7)
        return carry

    def inner_chunks(chunk, carry):
        chunk_copy(chunk).wait()

        @pl.when(chunk < 5)
        def _():
            chunk_copy(chunk + 2).start()

        first_pass(chunk)
        return carry

    lax.fori_loop(0, 2, outer_chunks, 0)
    lax.fori_loop(1, 7, inner_chunks, 0)

    for d in range(1, ny):
        rate_copy(d).wait_recv()
    lane = iota((8, 128), 1)
    for tile in range(4):
        owned = jnp.where(lane < 64, rate_in[2 * tile], rate_in[2 * tile + 1])
        for block in range(8):
            rates[block, tile] = jnp.broadcast_to(owned[block : block + 1], (8, 128))

    def edge_copy(side, place):
        return pltpu.make_async_remote_copy(
            src_ref=edge_out.at[side, place],
            dst_ref=moved.at[LEAVE_X[side][place], 1 if side == 0 else 16],
            send_sem=edge_send.at[side, place],
            recv_sem=edge_recv.at[side, place],
            device_id=(right if side == 0 else left, gy),
            device_id_type=MESH,
        )

    def corner_copy(slot):
        index, step_x, step_y = CORNERS[slot]
        side = 0 if step_x > 0 else 1
        return pltpu.make_async_remote_copy(
            src_ref=edge_out.at[side, LEAVE_X[side].index(index), 0 if step_y > 0 else 15],
            dst_ref=corner_in.at[slot, 0],
            send_sem=corner_send.at[slot],
            recv_sem=corner_recv.at[slot],
            device_id=(right if step_x > 0 else left, up if step_y > 0 else down),
            device_id_type=MESH,
        )

    def leave(side, place):
        c = velocities[LEAVE_X[side][place]]
        values = []
        for part in range(2):
            rows = slice(8 * part, 8 * part + 8)
            block = (1 - side) * 4 + 1 + part
            tiles = [
                start_out[side, place, rows, TILES[t]]
                + rates[block, t] * gain_out[side, place, rows, TILES[t]]
                for t in range(4)
            ]
            values.append(along_lanes(tiles, c[2]))
        for t in range(4):
            low, high = along_rows(values[0][t], values[1][t], c[1])
            edge_out[side, place, 0:8, TILES[t]] = low
            edge_out[side, place, 8:16, TILES[t]] = high

    for place in (1, 2, 0, 3, 4):
        for side in range(2):
            leave(side, place)
            for slot, corner in enumerate(CORNERS):
                if corner[0] == LEAVE_X[side][place]:
                    corner_copy(slot).start()
            edge_copy(side, place).start()

    for tile in range(4):
        sums_out[tile, 0:4, :] = jnp.sum(heat_acc[:, tile], axis=1)
    sums_in[pl.ds(gy, 1)] = sums_out[pl.ds(gy // 2, 1)]

    def sums_copy(d):
        return pltpu.make_async_remote_copy(
            src_ref=sums_out.at[peers[d] // 2],
            dst_ref=sums_in.at[gy],
            send_sem=sums_send.at[d],
            recv_sem=sums_recv.at[d],
            device_id=(gx, peers[d]),
            device_id_type=MESH,
        )

    for d in range(1, ny):
        sums_copy(d).start()

    def put(index, plane, tile, low, high):
        c = velocities[index]
        place, lanes = plane + 1 + c[0], TILES[tile]
        low, high = along_rows(low, high, c[1])
        moved[index, place, 0:8, lanes] = low
        moved[index, place, 8:16, lanes] = high

    def collide(plane):
        half = plane // 8
        for tile in range(4):
            lanes = TILES[tile]
            found = []
            for part in range(2):
                rows = slice(8 * part, 8 * part + 8)
                rho, ux, uy, uz = [moments[slot, plane, rows, lanes] for slot in range(4)]
                rate = rates[half * 4 + 1 + part, tile]
                terms = equilibrium((rate * 0.125) * rho, ux, uy, uz)
                fluid = solid[plane, rows, lanes] == 0
                kept = 1.0 - rate
                f = [pops[index, plane, rows, lanes] for index in range(19)]
                found.append(
                    [
                        jnp.where(
                            fluid, kept * f[index] + equilibrium_of(index, terms), f[opposite[index]]
                        )
                        for index in range(19)
                    ]
                )
            for index in range(19):
                low, high = found[0][index], found[1][index]
                if index in LEAVE_Z:
                    staged[LEAVE_Z.index(index), 0:8, lanes] = low
                    staged[LEAVE_Z.index(index), 8:16, lanes] = high
                else:
                    put(index, plane, tile, low, high)

    def run_z(plane):
        for place, index in enumerate(LEAVE_Z):
            low = along_lanes([staged[place, 0:8, TILES[t]] for t in range(4)], velocities[index][2])
            high = along_lanes([staged[place, 8:16, TILES[t]] for t in range(4)], velocities[index][2])
            for t in range(4):
                put(index, plane, t, low[t], high[t])

    collide(0)

    def planes(plane, carry):
        run_z(plane - 1)
        collide(plane)
        return carry

    lax.fori_loop(1, 16, planes, 0)
    run_z(15)

    def collide_y(side):
        y_copy(side).wait_recv()
        found = [[[None] * 4 for _ in range(2)] for _ in range(5)]
        for tile in range(4):
            for part in range(2):
                rows = slice(8 * part, 8 * part + 8)
                rate = rates[part * 4 + 3 * side, tile]
                rho, ux, uy, uz = [y_in[side, 5 + n, rows, TILES[tile]] for n in range(4)]
                terms = equilibrium((rate * 0.125) * rho, ux, uy, uz)
                kept = jnp.where(rho == 0.0, 1.0, 1.0 - rate)
                for place, index in enumerate(LEAVE_Y[side]):
                    found[place][part][tile] = kept * y_in[
                        side, place, rows, TILES[tile]
                    ] + equilibrium_of(index, terms)
        for place, index in enumerate(LEAVE_Y[side]):
            c = velocities[index]
            low, high = [along_lanes(found[place][part], c[2]) for part in range(2)]
            for t in range(4):
                first, second = along_rows(low[t], high[t], c[0])
                y_rows[side, place, 0:8, TILES[t]] = first
                y_rows[side, place, 8:16, TILES[t]] = second

    for side in range(2):
        collide_y(side)
    for slot, (index, step_x, step_y) in enumerate(CORNERS):
        corner_copy(slot).wait_recv()
        side, row = (0 if step_y > 0 else 1), (0 if step_x > 0 else 15)
        y_rows[side, LEAVE_Y[side].index(index), row : row + 1, :] = corner_in[slot, 0:1, :]

    for side in range(2):
        for place in range(5):
            edge_copy(side, place).wait_recv()
    for d in range(1, ny):
        sums_copy(d).wait_recv()

    for d in range(1, ny):
        rate_copy(d).wait_send()
        sums_copy(d).wait_send()
    for side in range(2):
        y_copy(side).wait_send()
        for place in range(5):
            edge_copy(side, place).wait_send()
    for slot in range(4):
        corner_copy(slot).wait_send()


def finish_kernel(
    moved,
    y_rows,
    sums_in,
    counts_hbm,
    breakage_hbm,
    selection_hbm,
    read_hbm,
    next_hbm,
    counts,
    breakage,
    selection,
    result,
    small_sem,
    read_sem,
    row_sem,
    next_sem,
):
    copies = [
        pltpu.make_async_copy(moved.at[index, 1:17], read_hbm.at[index], read_sem.at[index])
        for index in LEAVE_Y[0] + LEAVE_Y[1] + FLAT
    ]
    rows = [
        pltpu.make_async_copy(
            y_rows.at[side, place], read_hbm.at[index, :, 15 * side], row_sem.at[side, place]
        )
        for side in range(2)
        for place, index in enumerate(LEAVE_Y[side])
    ]
    loads = [
        pltpu.make_async_copy(counts_hbm, counts, small_sem.at[0]),
        pltpu.make_async_copy(breakage_hbm, breakage, small_sem.at[1]),
        pltpu.make_async_copy(selection_hbm, selection, small_sem.at[2]),
    ]
    for copy in copies + loads:
        copy.start()
    for copy in loads:
        copy.wait()

    gy = lax.axis_index("gy")
    current = counts[...]
    tau = relax_time(class_load(current, 128))
    factor = (tau - 0.5) / (3.0 * tau * tau)
    row, slot = iota((256, 64), 0), iota((256, 64), 1)
    wanted = ((row // 8) % 16 // 2) * 8 + (row // 128) * 2 + (row // 8) % 2
    pick = jnp.where(slot == wanted, 1.0, 0.0)
    sums = jnp.dot(
        pick, sums_in[...].reshape(64, 128), precision=HIGH, preferred_element_type=F32
    )
    row, lane = iota((256, 128), 0), iota((256, 128), 1)
    sums = jnp.where(lane // 8 == row % 8 + 8 * lax.rem(gy, 2), sums, 0.0)
    sums = jnp.dot(sums, jnp.ones((128, 128), F32), precision=HIGH, preferred_element_type=F32)
    eps = sums * (4.5 / 512.0) * factor
    strength = jnp.sqrt(50.0 * eps + 1e-06)
    gain = strength / (1.0 + strength)
    rate = gain[:, :64] * selection[...][None, :]
    for step in range(SUB):
        lost = rate * current
        born = lax.dot_general(
            lost,
            breakage[...],
            (((1,), (1,)), ((), ())),
            precision=HIGH,
            preferred_element_type=F32,
        )
        current = current + 0.25 * (born - lost)
    for copy in copies[:10]:
        copy.wait()
    for copy in rows:
        copy.start()
    result[...] = current
    last = pltpu.make_async_copy(result, next_hbm, next_sem)
    last.start()
    last.wait()
    for copy in copies[10:] + rows:
        copy.wait()


def per_device(nx, ny, populations, solid, counts, breakage, selection):
    cells = counts.transpose(1, 2, 3, 0).reshape(256, 64)
    any_space = pl.BlockSpec(memory_space=pl.ANY)
    vmem = pl.BlockSpec(memory_space=pltpu.VMEM)
    dma = pltpu.SemaphoreType.DMA
    moved, rows, sums = pl.pallas_call(
        functools.partial(step_kernel, nx, ny),
        out_shape=(
            pltpu.VMEM((19, 18, 16, 512), F32),
            pltpu.VMEM((2, 5, 16, 512), F32),
            pltpu.VMEM((8, 8, 128), F32),
        ),
        in_specs=[any_space] * 3,
        out_specs=(vmem, vmem, vmem),
        scratch_shapes=[
            pltpu.VMEM((19, 16, 16, 512), F32),
            pltpu.VMEM((16, 16, 512), jnp.int32),
            pltpu.VMEM((256, 64), F32),
            pltpu.VMEM((4, 16, 16, 512), F32),
            pltpu.VMEM((4, 4, 8, 128), F32),
            pltpu.VMEM((4, 8, 128), F32),
            pltpu.VMEM((8, 8, 128), F32),
            pltpu.VMEM((8, 8, 128), F32),
            pltpu.VMEM((8, 4, 8, 128), F32),
            pltpu.VMEM((10, 16, 512), F32),
            pltpu.VMEM((2, 19, 16, 512), F32),
            pltpu.VMEM((2, 16, 512), jnp.int32),
            pltpu.VMEM((2, 5, 16, 512), F32),
            pltpu.VMEM((2, 5, 16, 512), F32),
            pltpu.VMEM((2, 5, 16, 512), F32),
            pltpu.VMEM((2, 9, 16, 512), F32),
            pltpu.VMEM((2, 9, 16, 512), F32),
            pltpu.VMEM((4, 8, 512), F32),
            dma((8,)),
            dma,
            dma,
            dma((2, 2)),
            dma((8,)),
            dma((8,)),
            dma((8,)),
            dma((8,)),
            dma((2, 5)),
            dma((2, 5)),
            dma((2,)),
            dma((2,)),
            dma((4,)),
            dma((4,)),
        ],
        compiler_params=pltpu.CompilerParams(
            collective_id=0, has_side_effects=True, vmem_limit_bytes=40 * 1024 * 1024
        ),
        name="collide",
    )(*[pltpu.with_memory_space_constraint(x, pltpu.HBM) for x in (populations, solid, cells)])
    read, after = pl.pallas_call(
        finish_kernel,
        out_shape=(
            jax.ShapeDtypeStruct(populations.shape, F32),
            jax.ShapeDtypeStruct(cells.shape, F32),
        ),
        in_specs=[vmem] * 3 + [any_space] * 3,
        out_specs=(any_space, any_space),
        scratch_shapes=[
            pltpu.VMEM((256, 64), F32),
            pltpu.VMEM((64, 64), F32),
            pltpu.VMEM((64,), F32),
            pltpu.VMEM((256, 64), F32),
            dma((3,)),
            dma((19,)),
            dma((2, 5)),
            dma,
        ],
        compiler_params=pltpu.CompilerParams(vmem_limit_bytes=24 * 1024 * 1024),
        name="finish",
    )(moved, rows, sums, cells, breakage, selection)
    return (read, after.reshape(2, 16, 8, 64).transpose(3, 0, 1, 2))


def solution(mesh):
    in_specs = (P(None, "gx", "gy", None), P("gx", "gy", None), P(None, "gx", None, "gy"), P(), P())
    out_specs = (P(None, "gx", "gy", None), P(None, "gx", None, "gy"))
    return jax.shard_map(
        functools.partial(per_device, mesh.shape["gx"], mesh.shape["gy"]),
        mesh=mesh,
        in_specs=in_specs,
        out_specs=out_specs,
        check_vma=False,
    )
```

```python
import functools

import jax
import jax.numpy as jnp
from jax import lax
from jax.experimental import pallas as pl
from jax.experimental.pallas import tpu as pltpu
from jax.sharding import PartitionSpec as P

SUB = 4
MESH = pl.DeviceIdType.MESH
F32 = jnp.float32
HIGH = lax.Precision.HIGHEST

velocities = (
    (0, 0, 0),
    (1, 0, 0),
    (-1, 0, 0),
    (0, 1, 0),
    (0, -1, 0),
    (0, 0, 1),
    (0, 0, -1),
    (1, 1, 0),
    (-1, -1, 0),
    (1, -1, 0),
    (-1, 1, 0),
    (1, 0, 1),
    (-1, 0, -1),
    (1, 0, -1),
    (-1, 0, 1),
    (0, 1, 1),
    (0, -1, -1),
    (0, 1, -1),
    (0, -1, 1),
)
opposite = (0, 2, 1, 4, 3, 6, 5, 8, 7, 10, 9, 12, 11, 14, 13, 16, 15, 18, 17)

LEAVE_X = ((1, 7, 9, 11, 13), (2, 8, 10, 12, 14))
LEAVE_Y = ((3, 7, 10, 15, 17), (4, 8, 9, 16, 18))
LEAVE_Z = (5, 6, 11, 12, 13, 14, 15, 16, 17, 18)
CORNERS = {7: (0, 0), 10: (0, 1), 9: (1, 0), 8: (1, 1)}
FLAT = tuple(i for i in range(19) if velocities[i][1] == 0)
TILES = tuple(slice(128 * t, 128 * t + 128) for t in range(4))


def iota(shape, axis):
    return lax.broadcasted_iota(jnp.int32, shape, axis)


def class_load(counts, lanes):
    volume = (iota((64, lanes), 0).astype(F32) + 1.0) / 64.0
    return jnp.dot(counts, volume, precision=HIGH, preferred_element_type=F32)


def relax_time(load):
    packed = 0.5 * load / (1.0 + load)
    thinned = 1.0 - packed / 0.64
    return 0.5 + 3.0 * (0.04 / (thinned * thinned))


def moments_of(f):
    even = {i: f[i] + f[i + 1] for i in range(1, 19, 2)}
    odd = {i: f[i] - f[i + 1] for i in range(1, 19, 2)}
    xy, xz, yz = even[7] + even[9], even[11] + even[13], even[15] + even[17]
    rho = f[0] + (even[1] + xy) + (even[3] + yz) + (even[5] + xz)
    jx = odd[1] + (odd[7] + odd[9]) + (odd[11] + odd[13])
    jy = odd[3] + (odd[7] - odd[9]) + (odd[15] + odd[17])
    jz = odd[5] + (odd[11] - odd[13]) + (odd[15] - odd[17])
    return even, (xy, xz, yz), rho, (jx, jy, jz)


def equilibrium(eighth, ux, uy, uz):
    tx, ty, tz = eighth * ux, eighth * uy, eighth * uz
    xx, yy, zz = tx * ux, ty * uy, tz * uz
    tx2, ty2 = tx + tx, ty + ty
    cross = (tx2 * uy, tx2 * uz, ty2 * uz)
    base = eighth * (8.0 / 36.0) - (xx + yy + zz) * (1.0 / 3.0)
    bx, by, bz = base + xx, base + yy, base + zz
    sums = (bx + yy, bx + zz, by + zz)
    return base, (bx, by, bz), sums, cross, (tx * (2.0 / 3.0), ty * (2.0 / 3.0), tz * (2.0 / 3.0))


def equilibrium_of(index, terms):
    base, axes, sums, cross, flow = terms
    c = velocities[index]
    nonzero = [a for a in range(3) if c[a] != 0]
    if not nonzero:
        return 12.0 * base
    if len(nonzero) == 1:
        (a,) = nonzero
        even = axes[a] + axes[a]
        odd = flow[a] + flow[a]
        return even + odd if c[a] > 0 else even - odd
    a, b = nonzero
    slot = {(0, 1): 0, (0, 2): 1, (1, 2): 2}[(a, b)]
    even = sums[slot] + cross[slot] if c[a] * c[b] > 0 else sums[slot] - cross[slot]
    odd = flow[a] + flow[b] if c[a] == c[b] else flow[a] - flow[b]
    return even + odd if c[a] > 0 else even - odd


def along_lanes(tiles, step):
    if step == 0:
        return tiles
    lane = iota((8, 128), 1)
    if step > 0:
        moved = [pltpu.roll(v, 1, 1) for v in tiles]
        return [jnp.where(lane == 0, moved[(t + 3) % 4], moved[t]) for t in range(4)]
    moved = [pltpu.roll(v, 127, 1) for v in tiles]
    return [jnp.where(lane == 127, moved[(t + 1) % 4], moved[t]) for t in range(4)]


def along_rows(low, high, step):
    if step == 0:
        return low, high
    row = iota((8, 128), 0)
    if step > 0:
        low, high = pltpu.roll(low, 1, 0), pltpu.roll(high, 1, 0)
        return jnp.where(row == 0, high, low), jnp.where(row == 0, low, high)
    low, high = pltpu.roll(low, 7, 0), pltpu.roll(high, 7, 0)
    return jnp.where(row == 7, high, low), jnp.where(row == 7, low, high)


def step_kernel(
    nx,
    ny,
    pop_hbm,
    solid_hbm,
    counts_hbm,
    moved,
    y_rows,
    sums_in,
    pops,
    solid,
    counts,
    moments,
    heat_acc,
    sums_out,
    rate_out,
    rate_in,
    rates,
    staged,
    row_pops,
    row_solid,
    start_out,
    gain_out,
    edge_out,
    y_out,
    y_in,
    ends_in,
    pop_sem,
    solid_sem,
    counts_sem,
    row_sem,
    rate_send,
    rate_recv,
    sums_send,
    sums_recv,
    edge_send,
    edge_recv,
    y_send,
    y_recv,
    ends_send,
    ends_recv,
):
    gx = lax.axis_index("gx")
    gy = lax.axis_index("gy")
    right, left = lax.rem(gx + 1, nx), lax.rem(gx + nx - 1, nx)
    up, down = lax.rem(gy + 1, ny), lax.rem(gy + ny - 1, ny)
    peers = [lax.rem(gy + d, ny) for d in range(ny)]

    counts_copy = pltpu.make_async_copy(counts_hbm, counts, counts_sem)
    counts_copy.start()
    barrier = pltpu.get_barrier_semaphore()
    partners = [(gx, peers[d]) for d in range(1, ny)]
    partners += [(left, gy), (right, gy)]
    for partner in partners:
        pl.semaphore_signal(barrier, inc=1, device_id=partner, device_id_type=MESH)

    def chunk_copy(chunk):
        rows = pl.ds(2 * chunk, 2)
        return pltpu.make_async_copy(pop_hbm.at[:, rows], pops.at[:, rows], pop_sem.at[chunk])

    def row_copies(side):
        y = 15 if side == 0 else 0
        return (
            pltpu.make_async_copy(solid_hbm.at[:, y], row_solid.at[side], row_sem.at[side, 0]),
            pltpu.make_async_copy(pop_hbm.at[:, :, y], row_pops.at[side], row_sem.at[side, 1]),
        )

    solid_copy = pltpu.make_async_copy(solid_hbm, solid, solid_sem)
    for side in range(2):
        for copy in row_copies(side):
            copy.start()
    solid_copy.start()
    for chunk in (0, 7, 1, 2):
        chunk_copy(chunk).start()

    counts_copy.wait()
    row, lane = iota((256, 128), 0), iota((256, 128), 1)
    load = class_load(counts[...], 128)
    load = jnp.where(row % 8 == (lane % 64) // 8, load, 0.0)
    slot, cell = iota((64, 256), 0), iota((64, 256), 1)
    wanted = ((slot % 8) // 4) * 16 + (2 * (slot // 8) + 15 + slot % 4) % 16
    pick = jnp.where(cell // 8 == wanted, 1.0, 0.0)
    load = jnp.dot(pick, load, precision=HIGH, preferred_element_type=F32)
    rate_out[...] = (1.0 / relax_time(load)).reshape(8, 8, 128)
    rate_in[pl.ds(gy, 1)] = rate_out[pl.ds(gy, 1)]

    heat_acc[...] = jnp.zeros_like(heat_acc)
    sums_out[...] = jnp.zeros_like(sums_out)

    def prepare_y(tile, carry):
        lanes = pl.ds(pl.multiple_of(tile * 128, 128), 128)
        for side in range(2):
            for part in range(2):
                rows = slice(8 * part, 8 * part + 8)
                f = [row_pops[side, index, rows, lanes] for index in range(19)]
                fluid = row_solid[side, rows, lanes] == 0
                _, _, rho, flow = moments_of(f)
                inverse = 1.0 / rho
                for place, index in enumerate(LEAVE_Y[side]):
                    y_out[side, place, rows, lanes] = jnp.where(fluid, f[index], f[opposite[index]])
                y_out[side, 5, rows, lanes] = jnp.where(fluid, rho, 0.0)
                for axis in range(3):
                    y_out[side, 6 + axis, rows, lanes] = flow[axis] * inverse
        return carry

    def y_copy(side):
        return pltpu.make_async_remote_copy(
            src_ref=y_out.at[side],
            dst_ref=y_in.at[side],
            send_sem=y_send.at[side],
            recv_sem=y_recv.at[side],
            device_id=(gx, up if side == 0 else down),
            device_id_type=MESH,
        )

    for side in range(2):
        for copy in row_copies(side):
            copy.wait()
    lax.fori_loop(0, 4, prepare_y, 0)

    pl.semaphore_wait(barrier, len(partners))

    def rate_copy(d):
        return pltpu.make_async_remote_copy(
            src_ref=rate_out.at[peers[d]],
            dst_ref=rate_in.at[gy],
            send_sem=rate_send.at[d],
            recv_sem=rate_recv.at[d],
            device_id=(gx, peers[d]),
            device_id_type=MESH,
        )

    for d in range(1, ny):
        rate_copy(d).start()

    def ends_copy(side, end):
        return pltpu.make_async_remote_copy(
            src_ref=y_out.at[side, :, 15 - 15 * end],
            dst_ref=ends_in.at[side, end],
            send_sem=ends_send.at[side, end],
            recv_sem=ends_recv.at[side, end],
            device_id=(gx, up if side == 0 else down),
            device_id_type=MESH,
        )

    for side in range(2):
        for end in range(2):
            ends_copy(side, end).start()
    for side in range(2):
        y_copy(side).start()

    def prepare_x(tile, carry):
        lanes = pl.ds(pl.multiple_of(tile * 128, 128), 128)
        for side in range(2):
            plane = 15 if side == 0 else 0
            for part in range(2):
                rows = slice(8 * part, 8 * part + 8)
                f = [pops[index, plane, rows, lanes] for index in range(19)]
                fluid = solid[plane, rows, lanes] == 0
                _, _, rho, (jx, jy, jz) = moments_of(f)
                inverse = 1.0 / rho
                terms = equilibrium(rho * 0.125, jx * inverse, jy * inverse, jz * inverse)
                for place, index in enumerate(LEAVE_X[side]):
                    start_out[side, place, rows, lanes] = jnp.where(
                        fluid, f[index], f[opposite[index]]
                    )
                    gain_out[side, place, rows, lanes] = jnp.where(
                        fluid, equilibrium_of(index, terms) - f[index], 0.0
                    )
        return carry

    solid_copy.wait()
    for chunk in (0, 7):
        chunk_copy(chunk).wait()

    lax.fori_loop(0, 4, prepare_x, 0)

    def first_pass(chunk):
        half = chunk // 4

        def one_tile(tile, carry):
            lanes = pl.ds(pl.multiple_of(tile * 128, 128), 128)
            heats = []
            for part in range(4):
                plane, rows = 2 * chunk + part // 2, slice(8 * (part % 2), 8 * (part % 2) + 8)
                f = [pops[index, plane, rows, lanes] for index in range(19)]
                even, (xy, xz, yz), rho, (jx, jy, jz) = moments_of(f)
                inverse = 1.0 / rho
                ux, uy, uz = jx * inverse, jy * inverse, jz * inverse
                third = rho * (1.0 / 3.0)
                pxx = even[1] + (xy + xz) - third - jx * ux
                pyy = even[3] + (xy + yz) - third - jy * uy
                pzz = even[5] + (xz + yz) - third - jz * uz
                pxy = even[7] - even[9] - jx * uy
                pxz = even[11] - even[13] - jx * uz
                pyz = even[15] - even[17] - jy * uz
                off = pxy * pxy + pxz * pxz + pyz * pyz
                square = pxx * pxx + pyy * pyy + pzz * pzz + (off + off)
                heat = square * (inverse * inverse)
                heats.append(jnp.where(solid[plane, rows, lanes] == 0, heat, 0.0))
                for slot, value in enumerate((rho, ux, uy, uz)):
                    moments[slot, plane, rows, lanes] = value
            heat_acc[half * 2, tile] += heats[0] + heats[2]
            heat_acc[half * 2 + 1, tile] += heats[1] + heats[3]
            return carry

        lax.fori_loop(0, 4, one_tile, 0)

    def outer_chunks(step, carry):
        first_pass(step * 7)
        return carry

    def inner_chunks(chunk, carry):
        chunk_copy(chunk).wait()

        @pl.when(chunk < 5)
        def _():
            chunk_copy(chunk + 2).start()

        first_pass(chunk)
        return carry

    lax.fori_loop(0, 2, outer_chunks, 0)
    lax.fori_loop(1, 7, inner_chunks, 0)

    for d in range(1, ny):
        rate_copy(d).wait_recv()
    lane = iota((8, 128), 1)
    for tile in range(4):
        owned = jnp.where(lane < 64, rate_in[2 * tile], rate_in[2 * tile + 1])
        for block in range(8):
            rates[block, tile] = jnp.broadcast_to(owned[block : block + 1], (8, 128))

    def edge_copy(side, place):
        return pltpu.make_async_remote_copy(
            src_ref=edge_out.at[side, place],
            dst_ref=moved.at[LEAVE_X[side][place], 1 if side == 0 else 16],
            send_sem=edge_send.at[side, place],
            recv_sem=edge_recv.at[side, place],
            device_id=(right if side == 0 else left, gy),
            device_id_type=MESH,
        )

    def leave(side, place):
        c = velocities[LEAVE_X[side][place]]
        values = []
        for part in range(2):
            rows = slice(8 * part, 8 * part + 8)
            block = (1 - side) * 4 + 1 + part
            tiles = [
                start_out[side, place, rows, TILES[t]]
                + rates[block, t] * gain_out[side, place, rows, TILES[t]]
                for t in range(4)
            ]
            values.append(along_lanes(tiles, c[2]))
        for t in range(4):
            low, high = along_rows(values[0][t], values[1][t], c[1])
            edge_out[side, place, 0:8, TILES[t]] = low
            edge_out[side, place, 8:16, TILES[t]] = high

    def leave_corner(index):
        from_y, side = CORNERS[index]
        ends_copy(from_y, side).wait_recv()
        row = 15 * from_y
        for t in range(4):
            cells = ends_in[from_y, side, :, TILES[t]]
            rate = rates[4 * (1 - side) + 3 * from_y, t, 0:1]
            rho, ux, uy, uz = [cells[n : n + 1] for n in range(5, 9)]
            terms = equilibrium((rate * 0.125) * rho, ux, uy, uz)
            kept = jnp.where(rho == 0.0, 1.0, 1.0 - rate)
            place = LEAVE_Y[from_y].index(index)
            edge_out[side, LEAVE_X[side].index(index), row : row + 1, TILES[t]] = kept * cells[
                place : place + 1
            ] + equilibrium_of(index, terms)

    for place in (0, 3, 4, 1, 2):
        for side in range(2):
            leave(side, place)
            if LEAVE_X[side][place] in CORNERS:
                leave_corner(LEAVE_X[side][place])
            edge_copy(side, place).start()

    for tile in range(4):
        sums_out[tile, 0:4, :] = jnp.sum(heat_acc[:, tile], axis=1)
    sums_in[pl.ds(gy, 1)] = sums_out[pl.ds(gy // 2, 1)]

    def sums_copy(d):
        return pltpu.make_async_remote_copy(
            src_ref=sums_out.at[peers[d] // 2],
            dst_ref=sums_in.at[gy],
            send_sem=sums_send.at[d],
            recv_sem=sums_recv.at[d],
            device_id=(gx, peers[d]),
            device_id_type=MESH,
        )

    for d in range(1, ny):
        sums_copy(d).start()

    def put(index, plane, tile, low, high):
        c = velocities[index]
        place, lanes = plane + 1 + c[0], TILES[tile]
        low, high = along_rows(low, high, c[1])
        moved[index, place, 0:8, lanes] = low
        moved[index, place, 8:16, lanes] = high

    def collide(plane):
        half = plane // 8
        for tile in range(4):
            lanes = TILES[tile]
            found = []
            for part in range(2):
                rows = slice(8 * part, 8 * part + 8)
                rho, ux, uy, uz = [moments[slot, plane, rows, lanes] for slot in range(4)]
                rate = rates[half * 4 + 1 + part, tile]
                terms = equilibrium((rate * 0.125) * rho, ux, uy, uz)
                fluid = solid[plane, rows, lanes] == 0
                kept = 1.0 - rate
                f = [pops[index, plane, rows, lanes] for index in range(19)]
                found.append(
                    [
                        jnp.where(
                            fluid, kept * f[index] + equilibrium_of(index, terms), f[opposite[index]]
                        )
                        for index in range(19)
                    ]
                )
            for index in range(19):
                low, high = found[0][index], found[1][index]
                if index in LEAVE_Z:
                    staged[LEAVE_Z.index(index), 0:8, lanes] = low
                    staged[LEAVE_Z.index(index), 8:16, lanes] = high
                else:
                    put(index, plane, tile, low, high)

    def run_z(plane):
        for place, index in enumerate(LEAVE_Z):
            low = along_lanes([staged[place, 0:8, TILES[t]] for t in range(4)], velocities[index][2])
            high = along_lanes([staged[place, 8:16, TILES[t]] for t in range(4)], velocities[index][2])
            for t in range(4):
                put(index, plane, t, low[t], high[t])

    collide(0)

    def planes(plane, carry):
        run_z(plane - 1)
        collide(plane)
        return carry

    lax.fori_loop(1, 16, planes, 0)
    run_z(15)

    def collide_y(side):
        y_copy(side).wait_recv()
        found = [[[None] * 4 for _ in range(2)] for _ in range(5)]
        for tile in range(4):
            for part in range(2):
                rows = slice(8 * part, 8 * part + 8)
                rate = rates[part * 4 + 3 * side, tile]
                rho, ux, uy, uz = [y_in[side, 5 + n, rows, TILES[tile]] for n in range(4)]
                terms = equilibrium((rate * 0.125) * rho, ux, uy, uz)
                kept = jnp.where(rho == 0.0, 1.0, 1.0 - rate)
                for place, index in enumerate(LEAVE_Y[side]):
                    found[place][part][tile] = kept * y_in[
                        side, place, rows, TILES[tile]
                    ] + equilibrium_of(index, terms)
        for place, index in enumerate(LEAVE_Y[side]):
            c = velocities[index]
            low, high = [along_lanes(found[place][part], c[2]) for part in range(2)]
            for t in range(4):
                first, second = along_rows(low[t], high[t], c[0])
                y_rows[side, place, 0:8, TILES[t]] = first
                y_rows[side, place, 8:16, TILES[t]] = second

    for side in range(2):
        collide_y(side)
    for side in range(2):
        for place in range(5):
            edge_copy(side, place).wait_recv()
    for index, (from_y, side) in CORNERS.items():
        row, end, plane = 15 * from_y, 15 * side, 1 + 15 * side
        y_rows[from_y, LEAVE_Y[from_y].index(index), end : end + 1, :] = moved[
            index, plane, row : row + 1, :
        ]
    for d in range(1, ny):
        sums_copy(d).wait_recv()

    for d in range(1, ny):
        rate_copy(d).wait_send()
        sums_copy(d).wait_send()
    for side in range(2):
        y_copy(side).wait_send()
        for place in range(5):
            edge_copy(side, place).wait_send()
        for end in range(2):
            ends_copy(side, end).wait_send()


def finish_kernel(
    moved,
    y_rows,
    sums_in,
    counts_hbm,
    breakage_hbm,
    selection_hbm,
    read_hbm,
    next_hbm,
    counts,
    breakage,
    selection,
    result,
    small_sem,
    read_sem,
    row_sem,
    next_sem,
):
    copies = [
        pltpu.make_async_copy(moved.at[index, 1:17], read_hbm.at[index], read_sem.at[index])
        for index in LEAVE_Y[0] + LEAVE_Y[1] + FLAT
    ]
    rows = [
        pltpu.make_async_copy(
            y_rows.at[side, place], read_hbm.at[index, :, 15 * side], row_sem.at[side, place]
        )
        for side in range(2)
        for place, index in enumerate(LEAVE_Y[side])
    ]
    loads = [
        pltpu.make_async_copy(counts_hbm, counts, small_sem.at[0]),
        pltpu.make_async_copy(breakage_hbm, breakage, small_sem.at[1]),
        pltpu.make_async_copy(selection_hbm, selection, small_sem.at[2]),
    ]
    for copy in copies + loads:
        copy.start()
    for copy in loads:
        copy.wait()

    gy = lax.axis_index("gy")
    current = counts[...]
    tau = relax_time(class_load(current, 128))
    factor = (tau - 0.5) / (3.0 * tau * tau)
    row, slot = iota((256, 64), 0), iota((256, 64), 1)
    wanted = ((row // 8) % 16 // 2) * 8 + (row // 128) * 2 + (row // 8) % 2
    pick = jnp.where(slot == wanted, 1.0, 0.0)
    sums = jnp.dot(
        pick, sums_in[...].reshape(64, 128), precision=HIGH, preferred_element_type=F32
    )
    row, lane = iota((256, 128), 0), iota((256, 128), 1)
    sums = jnp.where(lane // 8 == row % 8 + 8 * lax.rem(gy, 2), sums, 0.0)
    sums = jnp.dot(sums, jnp.ones((128, 128), F32), precision=HIGH, preferred_element_type=F32)
    eps = sums * (4.5 / 512.0) * factor
    strength = jnp.sqrt(50.0 * eps + 1e-06)
    gain = strength / (1.0 + strength)
    rate = gain[:, :64] * selection[...][None, :]
    for step in range(SUB):
        lost = rate * current
        born = lax.dot_general(
            lost,
            breakage[...],
            (((1,), (1,)), ((), ())),
            precision=HIGH,
            preferred_element_type=F32,
        )
        current = current + 0.25 * (born - lost)
    for copy in copies[:10]:
        copy.wait()
    for copy in rows:
        copy.start()
    result[...] = current
    last = pltpu.make_async_copy(result, next_hbm, next_sem)
    last.start()
    last.wait()
    for copy in copies[10:] + rows:
        copy.wait()


def per_device(nx, ny, populations, solid, counts, breakage, selection):
    cells = counts.transpose(1, 2, 3, 0).reshape(256, 64)
    any_space = pl.BlockSpec(memory_space=pl.ANY)
    vmem = pl.BlockSpec(memory_space=pltpu.VMEM)
    dma = pltpu.SemaphoreType.DMA
    moved, rows, sums = pl.pallas_call(
        functools.partial(step_kernel, nx, ny),
        out_shape=(
            pltpu.VMEM((19, 18, 16, 512), F32),
            pltpu.VMEM((2, 5, 16, 512), F32),
            pltpu.VMEM((8, 8, 128), F32),
        ),
        in_specs=[any_space] * 3,
        out_specs=(vmem, vmem, vmem),
        scratch_shapes=[
            pltpu.VMEM((19, 16, 16, 512), F32),
            pltpu.VMEM((16, 16, 512), jnp.int32),
            pltpu.VMEM((256, 64), F32),
            pltpu.VMEM((4, 16, 16, 512), F32),
            pltpu.VMEM((4, 4, 8, 128), F32),
            pltpu.VMEM((4, 8, 128), F32),
            pltpu.VMEM((8, 8, 128), F32),
            pltpu.VMEM((8, 8, 128), F32),
            pltpu.VMEM((8, 4, 8, 128), F32),
            pltpu.VMEM((10, 16, 512), F32),
            pltpu.VMEM((2, 19, 16, 512), F32),
            pltpu.VMEM((2, 16, 512), jnp.int32),
            pltpu.VMEM((2, 5, 16, 512), F32),
            pltpu.VMEM((2, 5, 16, 512), F32),
            pltpu.VMEM((2, 5, 16, 512), F32),
            pltpu.VMEM((2, 9, 16, 512), F32),
            pltpu.VMEM((2, 9, 16, 512), F32),
            pltpu.VMEM((2, 2, 9, 512), F32),
            dma((8,)),
            dma,
            dma,
            dma((2, 2)),
            dma((8,)),
            dma((8,)),
            dma((8,)),
            dma((8,)),
            dma((2, 5)),
            dma((2, 5)),
            dma((2,)),
            dma((2,)),
            dma((2, 2)),
            dma((2, 2)),
        ],
        compiler_params=pltpu.CompilerParams(
            collective_id=0, has_side_effects=True, vmem_limit_bytes=40 * 1024 * 1024
        ),
        name="collide",
    )(*[pltpu.with_memory_space_constraint(x, pltpu.HBM) for x in (populations, solid, cells)])
    read, after = pl.pallas_call(
        finish_kernel,
        out_shape=(
            jax.ShapeDtypeStruct(populations.shape, F32),
            jax.ShapeDtypeStruct(cells.shape, F32),
        ),
        in_specs=[vmem] * 3 + [any_space] * 3,
        out_specs=(any_space, any_space),
        scratch_shapes=[
            pltpu.VMEM((256, 64), F32),
            pltpu.VMEM((64, 64), F32),
            pltpu.VMEM((64,), F32),
            pltpu.VMEM((256, 64), F32),
            dma((3,)),
            dma((19,)),
            dma((2, 5)),
            dma,
        ],
        compiler_params=pltpu.CompilerParams(vmem_limit_bytes=24 * 1024 * 1024),
        name="finish",
    )(moved, rows, sums, cells, breakage, selection)
    return (read, after.reshape(2, 16, 8, 64).transpose(3, 0, 1, 2))


def solution(mesh):
    in_specs = (P(None, "gx", "gy", None), P("gx", "gy", None), P(None, "gx", None, "gy"), P(), P())
    out_specs = (P(None, "gx", "gy", None), P(None, "gx", None, "gy"))
    return jax.shard_map(
        functools.partial(per_device, mesh.shape["gx"], mesh.shape["gy"]),
        mesh=mesh,
        in_specs=in_specs,
        out_specs=out_specs,
        check_vma=False,
    )
```

```python
import functools

import jax
import jax.numpy as jnp
from jax import lax
from jax.experimental import pallas as pl
from jax.experimental.pallas import tpu as pltpu
from jax.sharding import PartitionSpec as P

SUB = 4
MESH = pl.DeviceIdType.MESH
F32 = jnp.float32
HIGH = lax.Precision.HIGHEST

velocities = (
    (0, 0, 0),
    (1, 0, 0),
    (-1, 0, 0),
    (0, 1, 0),
    (0, -1, 0),
    (0, 0, 1),
    (0, 0, -1),
    (1, 1, 0),
    (-1, -1, 0),
    (1, -1, 0),
    (-1, 1, 0),
    (1, 0, 1),
    (-1, 0, -1),
    (1, 0, -1),
    (-1, 0, 1),
    (0, 1, 1),
    (0, -1, -1),
    (0, 1, -1),
    (0, -1, 1),
)
opposite = (0, 2, 1, 4, 3, 6, 5, 8, 7, 10, 9, 12, 11, 14, 13, 16, 15, 18, 17)

LEAVE_X = ((1, 7, 9, 11, 13), (2, 8, 10, 12, 14))
LEAVE_Y = ((3, 7, 10, 15, 17), (4, 8, 9, 16, 18))
LEAVE_Z = (5, 6, 11, 12, 13, 14, 15, 16, 17, 18)
CORNERS = {7: (0, 0), 10: (0, 1), 9: (1, 0), 8: (1, 1)}
TILES = tuple(slice(128 * t, 128 * t + 128) for t in range(4))


def iota(shape, axis):
    return lax.broadcasted_iota(jnp.int32, shape, axis)


def class_load(counts, lanes):
    volume = (iota((64, lanes), 0).astype(F32) + 1.0) / 64.0
    return jnp.dot(counts, volume, precision=HIGH, preferred_element_type=F32)


def relax_time(load):
    packed = 0.5 * load / (1.0 + load)
    thinned = 1.0 - packed / 0.64
    return 0.5 + 3.0 * (0.04 / (thinned * thinned))


def moments_of(f):
    even = {i: f[i] + f[i + 1] for i in range(1, 19, 2)}
    odd = {i: f[i] - f[i + 1] for i in range(1, 19, 2)}
    xy, xz, yz = even[7] + even[9], even[11] + even[13], even[15] + even[17]
    rho = f[0] + (even[1] + xy) + (even[3] + yz) + (even[5] + xz)
    jx = odd[1] + (odd[7] + odd[9]) + (odd[11] + odd[13])
    jy = odd[3] + (odd[7] - odd[9]) + (odd[15] + odd[17])
    jz = odd[5] + (odd[11] - odd[13]) + (odd[15] - odd[17])
    return even, (xy, xz, yz), rho, (jx, jy, jz)


def equilibrium(eighth, ux, uy, uz):
    tx, ty, tz = eighth * ux, eighth * uy, eighth * uz
    xx, yy, zz = tx * ux, ty * uy, tz * uz
    tx2, ty2 = tx + tx, ty + ty
    cross = (tx2 * uy, tx2 * uz, ty2 * uz)
    base = eighth * (8.0 / 36.0) - (xx + yy + zz) * (1.0 / 3.0)
    bx, by, bz = base + xx, base + yy, base + zz
    sums = (bx + yy, bx + zz, by + zz)
    return base, (bx, by, bz), sums, cross, (tx * (2.0 / 3.0), ty * (2.0 / 3.0), tz * (2.0 / 3.0))


def equilibrium_of(index, terms):
    base, axes, sums, cross, flow = terms
    c = velocities[index]
    nonzero = [a for a in range(3) if c[a] != 0]
    if not nonzero:
        return 12.0 * base
    if len(nonzero) == 1:
        (a,) = nonzero
        even = axes[a] + axes[a]
        odd = flow[a] + flow[a]
        return even + odd if c[a] > 0 else even - odd
    a, b = nonzero
    slot = {(0, 1): 0, (0, 2): 1, (1, 2): 2}[(a, b)]
    even = sums[slot] + cross[slot] if c[a] * c[b] > 0 else sums[slot] - cross[slot]
    odd = flow[a] + flow[b] if c[a] == c[b] else flow[a] - flow[b]
    return even + odd if c[a] > 0 else even - odd


def along_lanes(tiles, step):
    if step == 0:
        return tiles
    lane = iota((8, 128), 1)
    if step > 0:
        moved = [pltpu.roll(v, 1, 1) for v in tiles]
        return [jnp.where(lane == 0, moved[(t + 3) % 4], moved[t]) for t in range(4)]
    moved = [pltpu.roll(v, 127, 1) for v in tiles]
    return [jnp.where(lane == 127, moved[(t + 1) % 4], moved[t]) for t in range(4)]


def along_rows(low, high, step):
    if step == 0:
        return low, high
    row = iota((8, 128), 0)
    if step > 0:
        low, high = pltpu.roll(low, 1, 0), pltpu.roll(high, 1, 0)
        return jnp.where(row == 0, high, low), jnp.where(row == 0, low, high)
    low, high = pltpu.roll(low, 7, 0), pltpu.roll(high, 7, 0)
    return jnp.where(row == 7, high, low), jnp.where(row == 7, low, high)


def break_up(gy, counts, breakage, selection, sums_in, result):
    current = counts[...]
    tau = relax_time(class_load(current, 128))
    factor = (tau - 0.5) / (3.0 * tau * tau)
    row, slot = iota((256, 64), 0), iota((256, 64), 1)
    wanted = ((row // 8) % 16 // 2) * 8 + (row // 128) * 2 + (row // 8) % 2
    pick = jnp.where(slot == wanted, 1.0, 0.0)
    sums = jnp.dot(
        pick, sums_in[...].reshape(64, 128), precision=HIGH, preferred_element_type=F32
    )
    row, lane = iota((256, 128), 0), iota((256, 128), 1)
    sums = jnp.where(lane // 8 == row % 8 + 8 * lax.rem(gy, 2), sums, 0.0)
    sums = jnp.dot(sums, jnp.ones((128, 128), F32), precision=HIGH, preferred_element_type=F32)
    eps = sums * (4.5 / 512.0) * factor
    strength = jnp.sqrt(50.0 * eps + 1e-06)
    gain = strength / (1.0 + strength)
    rate = gain[:, :64] * selection[...][None, :]
    for step in range(SUB):
        lost = rate * current
        born = lax.dot_general(
            lost,
            breakage[...],
            (((1,), (1,)), ((), ())),
            precision=HIGH,
            preferred_element_type=F32,
        )
        current = current + 0.25 * (born - lost)
    result[...] = current


def step_kernel(
    nx,
    ny,
    pop_hbm,
    solid_hbm,
    counts_hbm,
    breakage_hbm,
    selection_hbm,
    moved,
    result,
    pops,
    solid,
    counts,
    breakage,
    selection,
    moments,
    heat_acc,
    sums_out,
    sums_in,
    rate_out,
    rate_in,
    rates,
    staged,
    row_pops,
    row_solid,
    start_out,
    gain_out,
    edge_out,
    y_out,
    ends_in,
    pop_sem,
    solid_sem,
    counts_sem,
    small_sem,
    row_sem,
    rate_send,
    rate_recv,
    sums_send,
    sums_recv,
    edge_send,
    edge_recv,
    ends_send,
    ends_recv,
):
    gx = lax.axis_index("gx")
    gy = lax.axis_index("gy")
    right, left = lax.rem(gx + 1, nx), lax.rem(gx + nx - 1, nx)
    up, down = lax.rem(gy + 1, ny), lax.rem(gy + ny - 1, ny)
    peers = [lax.rem(gy + d, ny) for d in range(ny)]

    counts_copy = pltpu.make_async_copy(counts_hbm, counts, counts_sem)
    counts_copy.start()
    barrier = pltpu.get_barrier_semaphore()
    partners = [(gx, peers[d]) for d in range(1, ny)]
    partners += [(left, gy), (right, gy)]
    for partner in partners:
        pl.semaphore_signal(barrier, inc=1, device_id=partner, device_id_type=MESH)

    def chunk_copy(chunk):
        rows = pl.ds(2 * chunk, 2)
        return pltpu.make_async_copy(pop_hbm.at[:, rows], pops.at[:, rows], pop_sem.at[chunk])

    def row_copies(side):
        y = 15 if side == 0 else 0
        return (
            pltpu.make_async_copy(solid_hbm.at[:, y], row_solid.at[side], row_sem.at[side, 0]),
            pltpu.make_async_copy(pop_hbm.at[:, :, y], row_pops.at[side], row_sem.at[side, 1]),
        )

    solid_copy = pltpu.make_async_copy(solid_hbm, solid, solid_sem)
    for side in range(2):
        for copy in row_copies(side):
            copy.start()
    solid_copy.start()
    for chunk in (0, 7, 1, 2):
        chunk_copy(chunk).start()
    small_copies = (
        pltpu.make_async_copy(breakage_hbm, breakage, small_sem.at[0]),
        pltpu.make_async_copy(selection_hbm, selection, small_sem.at[1]),
    )
    for copy in small_copies:
        copy.start()

    counts_copy.wait()
    row, lane = iota((256, 128), 0), iota((256, 128), 1)
    load = class_load(counts[...], 128)
    load = jnp.where(row % 8 == (lane % 64) // 8, load, 0.0)
    slot, cell = iota((64, 256), 0), iota((64, 256), 1)
    wanted = ((slot % 8) // 4) * 16 + (2 * (slot // 8) + 15 + slot % 4) % 16
    pick = jnp.where(cell // 8 == wanted, 1.0, 0.0)
    load = jnp.dot(pick, load, precision=HIGH, preferred_element_type=F32)
    rate_out[...] = (1.0 / relax_time(load)).reshape(8, 8, 128)
    rate_in[pl.ds(gy, 1)] = rate_out[pl.ds(gy, 1)]

    pl.semaphore_wait(barrier, len(partners))

    def rate_copy(d):
        return pltpu.make_async_remote_copy(
            src_ref=rate_out.at[peers[d]],
            dst_ref=rate_in.at[gy],
            send_sem=rate_send.at[d],
            recv_sem=rate_recv.at[d],
            device_id=(gx, peers[d]),
            device_id_type=MESH,
        )

    for d in range(1, ny):
        rate_copy(d).start()

    heat_acc[...] = jnp.zeros_like(heat_acc)
    sums_out[...] = jnp.zeros_like(sums_out)

    def prepare(kind, side, tile):
        lanes = pl.ds(pl.multiple_of(tile * 128, 128), 128)
        plane = 15 if side == 0 else 0
        for part in range(2):
            rows = slice(8 * part, 8 * part + 8)
            if kind == 0:
                f = [pops[index, plane, rows, lanes] for index in range(19)]
                fluid = solid[plane, rows, lanes] == 0
            else:
                f = [row_pops[side, index, rows, lanes] for index in range(19)]
                fluid = row_solid[side, rows, lanes] == 0
            _, _, rho, flow = moments_of(f)
            inverse = 1.0 / rho
            speed = [component * inverse for component in flow]
            terms = equilibrium(rho * 0.125, *speed)
            for place, index in enumerate((LEAVE_X if kind == 0 else LEAVE_Y)[side]):
                start = jnp.where(fluid, f[index], f[opposite[index]])
                start_out[kind, side, place, rows, lanes] = start
                gain_out[kind, side, place, rows, lanes] = jnp.where(
                    fluid, equilibrium_of(index, terms) - f[index], 0.0
                )
                if kind == 1:
                    y_out[side, place, rows, lanes] = start
            if kind == 1:
                y_out[side, 5, rows, lanes] = jnp.where(fluid, rho, 0.0)
                for axis in range(3):
                    y_out[side, 6 + axis, rows, lanes] = speed[axis]

    def prepare_y(tile, carry):
        for side in range(2):
            prepare(1, side, tile)
        return carry

    def prepare_x(tile, carry):
        for side in range(2):
            prepare(0, side, tile)
        return carry

    for side in range(2):
        for copy in row_copies(side):
            copy.wait()
    lax.fori_loop(0, 4, prepare_y, 0)

    def ends_copy(side, end):
        return pltpu.make_async_remote_copy(
            src_ref=y_out.at[side, :, 15 - 15 * end],
            dst_ref=ends_in.at[side, end],
            send_sem=ends_send.at[side, end],
            recv_sem=ends_recv.at[side, end],
            device_id=(gx, up if side == 0 else down),
            device_id_type=MESH,
        )

    for side in range(2):
        for end in range(2):
            ends_copy(side, end).start()

    solid_copy.wait()
    for chunk in (0, 7):
        chunk_copy(chunk).wait()

    lax.fori_loop(0, 4, prepare_x, 0)

    def first_pass(chunk):
        half = chunk // 4

        def one_tile(tile, carry):
            lanes = pl.ds(pl.multiple_of(tile * 128, 128), 128)
            heats = []
            for part in range(4):
                plane, rows = 2 * chunk + part // 2, slice(8 * (part % 2), 8 * (part % 2) + 8)
                f = [pops[index, plane, rows, lanes] for index in range(19)]
                even, (xy, xz, yz), rho, (jx, jy, jz) = moments_of(f)
                inverse = 1.0 / rho
                ux, uy, uz = jx * inverse, jy * inverse, jz * inverse
                third = rho * (1.0 / 3.0)
                pxx = even[1] + (xy + xz) - third - jx * ux
                pyy = even[3] + (xy + yz) - third - jy * uy
                pzz = even[5] + (xz + yz) - third - jz * uz
                pxy = even[7] - even[9] - jx * uy
                pxz = even[11] - even[13] - jx * uz
                pyz = even[15] - even[17] - jy * uz
                off = pxy * pxy + pxz * pxz + pyz * pyz
                square = pxx * pxx + pyy * pyy + pzz * pzz + (off + off)
                heat = square * (inverse * inverse)
                heats.append(jnp.where(solid[plane, rows, lanes] == 0, heat, 0.0))
                for slot, value in enumerate((rho, ux, uy, uz)):
                    moments[slot, plane, rows, lanes] = value
            heat_acc[half * 2, tile] += heats[0] + heats[2]
            heat_acc[half * 2 + 1, tile] += heats[1] + heats[3]
            return carry

        lax.fori_loop(0, 4, one_tile, 0)

    def outer_chunks(step, carry):
        first_pass(step * 7)
        return carry

    def inner_chunks(chunk, carry):
        chunk_copy(chunk).wait()

        @pl.when(chunk < 5)
        def _():
            chunk_copy(chunk + 2).start()

        first_pass(chunk)
        return carry

    lax.fori_loop(0, 2, outer_chunks, 0)
    lax.fori_loop(1, 7, inner_chunks, 0)

    for tile in range(4):
        sums_out[tile, 0:4, :] = jnp.sum(heat_acc[:, tile], axis=1)
    sums_in[pl.ds(gy, 1)] = sums_out[pl.ds(gy // 2, 1)]

    def sums_copy(d):
        return pltpu.make_async_remote_copy(
            src_ref=sums_out.at[peers[d] // 2],
            dst_ref=sums_in.at[gy],
            send_sem=sums_send.at[d],
            recv_sem=sums_recv.at[d],
            device_id=(gx, peers[d]),
            device_id_type=MESH,
        )

    for d in range(1, ny):
        sums_copy(d).start()

    for d in range(1, ny):
        rate_copy(d).wait_recv()
    lane = iota((8, 128), 1)
    for tile in range(4):
        owned = jnp.where(lane < 64, rate_in[2 * tile], rate_in[2 * tile + 1])
        for block in range(8):
            rates[block, tile] = jnp.broadcast_to(owned[block : block + 1], (8, 128))

    def edge_copy(kind, side, place):
        index = (LEAVE_X if kind == 0 else LEAVE_Y)[side][place]
        if kind == 0:
            target = moved.at[index, 1 if side == 0 else 16]
            device = (right if side == 0 else left, gy)
        else:
            first = 1 + velocities[index][0]
            target = moved.at[index, first : first + 16, 0 if side == 0 else 15]
            device = (gx, up if side == 0 else down)
        return pltpu.make_async_remote_copy(
            src_ref=edge_out.at[kind, side, place],
            dst_ref=target,
            send_sem=edge_send.at[kind, side, place],
            recv_sem=edge_recv.at[kind, side, place],
            device_id=device,
            device_id_type=MESH,
        )

    def leave(kind, side, place):
        c = velocities[(LEAVE_X if kind == 0 else LEAVE_Y)[side][place]]
        far = 1 - side
        values = []
        for part in range(2):
            rows = slice(8 * part, 8 * part + 8)
            block = far * 4 + 1 + part if kind == 0 else part * 4 + 1 + far
            tiles = [
                start_out[kind, side, place, rows, TILES[t]]
                + rates[block, t] * gain_out[kind, side, place, rows, TILES[t]]
                for t in range(4)
            ]
            values.append(along_lanes(tiles, c[2]))
        for t in range(4):
            low, high = along_rows(values[0][t], values[1][t], c[1] if kind == 0 else 0)
            edge_out[kind, side, place, 0:8, TILES[t]] = low
            edge_out[kind, side, place, 8:16, TILES[t]] = high

    def leave_corner(index):
        from_y, side = CORNERS[index]
        ends_copy(from_y, side).wait_recv()
        row = 15 * from_y
        for t in range(4):
            cells = ends_in[from_y, side, :, TILES[t]]
            rate = rates[4 * (1 - side) + 3 * from_y, t, 0:1]
            rho, ux, uy, uz = [cells[n : n + 1] for n in range(5, 9)]
            terms = equilibrium((rate * 0.125) * rho, ux, uy, uz)
            kept = jnp.where(rho == 0.0, 1.0, 1.0 - rate)
            place = LEAVE_Y[from_y].index(index)
            edge_out[0, side, LEAVE_X[side].index(index), row : row + 1, TILES[t]] = kept * cells[
                place : place + 1
            ] + equilibrium_of(index, terms)

    for place in (0, 3, 4, 1, 2):
        for side in range(2):
            leave(0, side, place)
            if LEAVE_X[side][place] in CORNERS:
                leave_corner(LEAVE_X[side][place])
            edge_copy(0, side, place).start()
    for place in range(5):
        for side in range(2):
            leave(1, side, place)
            edge_copy(1, side, place).start()

    def put(index, plane, tile, low, high):
        c = velocities[index]
        place, lanes = plane + 1 + c[0], TILES[tile]
        low, high = along_rows(low, high, c[1])
        if c[1] > 0:
            moved[index, place, 1:8, lanes] = low[1:8]
        else:
            moved[index, place, 0:8, lanes] = low
        if c[1] < 0:
            moved[index, place, 8:15, lanes] = high[0:7]
        else:
            moved[index, place, 8:16, lanes] = high

    def collide(plane):
        half = plane // 8
        for tile in range(4):
            lanes = TILES[tile]
            found = []
            for part in range(2):
                rows = slice(8 * part, 8 * part + 8)
                rho, ux, uy, uz = [moments[slot, plane, rows, lanes] for slot in range(4)]
                rate = rates[half * 4 + 1 + part, tile]
                terms = equilibrium((rate * 0.125) * rho, ux, uy, uz)
                fluid = solid[plane, rows, lanes] == 0
                kept = 1.0 - rate
                f = [pops[index, plane, rows, lanes] for index in range(19)]
                found.append(
                    [
                        jnp.where(
                            fluid, kept * f[index] + equilibrium_of(index, terms), f[opposite[index]]
                        )
                        for index in range(19)
                    ]
                )
            for index in range(19):
                low, high = found[0][index], found[1][index]
                if index in LEAVE_Z:
                    staged[LEAVE_Z.index(index), 0:8, lanes] = low
                    staged[LEAVE_Z.index(index), 8:16, lanes] = high
                else:
                    put(index, plane, tile, low, high)

    def run_z(plane):
        for place, index in enumerate(LEAVE_Z):
            low = along_lanes([staged[place, 0:8, TILES[t]] for t in range(4)], velocities[index][2])
            high = along_lanes([staged[place, 8:16, TILES[t]] for t in range(4)], velocities[index][2])
            for t in range(4):
                put(index, plane, t, low[t], high[t])

    collide(0)

    def planes(plane, carry):
        run_z(plane - 1)
        collide(plane)
        return carry

    lax.fori_loop(1, 16, planes, 0)
    run_z(15)

    for copy in small_copies:
        copy.wait()
    for d in range(1, ny):
        sums_copy(d).wait_recv()
    break_up(gy, counts, breakage, selection, sums_in, result)

    for kind in range(2):
        for side in range(2):
            for place in range(5):
                edge_copy(kind, side, place).wait_recv()

    for d in range(1, ny):
        rate_copy(d).wait_send()
        sums_copy(d).wait_send()
    for side in range(2):
        for place in range(5):
            for kind in range(2):
                edge_copy(kind, side, place).wait_send()
        for end in range(2):
            ends_copy(side, end).wait_send()


def finish_kernel(moved, result, read_hbm, next_hbm, read_sem, next_sem):
    copies = [
        pltpu.make_async_copy(moved.at[index, 1:17], read_hbm.at[index], read_sem.at[index])
        for index in range(19)
    ]
    copies.append(pltpu.make_async_copy(result, next_hbm, next_sem))
    for copy in copies:
        copy.start()
    for copy in copies:
        copy.wait()


def per_device(nx, ny, populations, solid, counts, breakage, selection):
    cells = counts.transpose(1, 2, 3, 0).reshape(256, 64)
    any_space = pl.BlockSpec(memory_space=pl.ANY)
    vmem = pl.BlockSpec(memory_space=pltpu.VMEM)
    dma = pltpu.SemaphoreType.DMA
    moved, result = pl.pallas_call(
        functools.partial(step_kernel, nx, ny),
        out_shape=(
            pltpu.VMEM((19, 18, 16, 512), F32),
            pltpu.VMEM((256, 64), F32),
        ),
        in_specs=[any_space] * 5,
        out_specs=(vmem, vmem),
        scratch_shapes=[
            pltpu.VMEM((19, 16, 16, 512), F32),
            pltpu.VMEM((16, 16, 512), jnp.int32),
            pltpu.VMEM((256, 64), F32),
            pltpu.VMEM((64, 64), F32),
            pltpu.VMEM((64,), F32),
            pltpu.VMEM((4, 16, 16, 512), F32),
            pltpu.VMEM((4, 4, 8, 128), F32),
            pltpu.VMEM((4, 8, 128), F32),
            pltpu.VMEM((8, 8, 128), F32),
            pltpu.VMEM((8, 8, 128), F32),
            pltpu.VMEM((8, 8, 128), F32),
            pltpu.VMEM((8, 4, 8, 128), F32),
            pltpu.VMEM((10, 16, 512), F32),
            pltpu.VMEM((2, 19, 16, 512), F32),
            pltpu.VMEM((2, 16, 512), jnp.int32),
            pltpu.VMEM((2, 2, 5, 16, 512), F32),
            pltpu.VMEM((2, 2, 5, 16, 512), F32),
            pltpu.VMEM((2, 2, 5, 16, 512), F32),
            pltpu.VMEM((2, 9, 16, 512), F32),
            pltpu.VMEM((2, 2, 9, 512), F32),
            dma((8,)),
            dma,
            dma,
            dma((2,)),
            dma((2, 2)),
            dma((8,)),
            dma((8,)),
            dma((8,)),
            dma((8,)),
            dma((2, 2, 5)),
            dma((2, 2, 5)),
            dma((2, 2)),
            dma((2, 2)),
        ],
        compiler_params=pltpu.CompilerParams(
            collective_id=0, has_side_effects=True, vmem_limit_bytes=40 * 1024 * 1024
        ),
        name="collide",
    )(
        *[
            pltpu.with_memory_space_constraint(x, pltpu.HBM)
            for x in (populations, solid, cells, breakage, selection)
        ]
    )
    read, after = pl.pallas_call(
        finish_kernel,
        out_shape=(
            jax.ShapeDtypeStruct(populations.shape, F32),
            jax.ShapeDtypeStruct(cells.shape, F32),
        ),
        in_specs=[vmem] * 2,
        out_specs=(any_space, any_space),
        scratch_shapes=[dma((19,)), dma],
        compiler_params=pltpu.CompilerParams(vmem_limit_bytes=24 * 1024 * 1024),
        name="finish",
    )(moved, result)
    return (read, after.reshape(2, 16, 8, 64).transpose(3, 0, 1, 2))


def solution(mesh):
    in_specs = (P(None, "gx", "gy", None), P("gx", "gy", None), P(None, "gx", None, "gy"), P(), P())
    out_specs = (P(None, "gx", "gy", None), P(None, "gx", None, "gy"))
    return jax.shard_map(
        functools.partial(per_device, mesh.shape["gx"], mesh.shape["gy"]),
        mesh=mesh,
        in_specs=in_specs,
        out_specs=out_specs,
        check_vma=False,
    )
```

```python
import functools

import jax
import jax.numpy as jnp
from jax import lax
from jax.experimental import pallas as pl
from jax.experimental.pallas import tpu as pltpu
from jax.sharding import PartitionSpec as P

SUB = 4
MESH = pl.DeviceIdType.MESH
F32 = jnp.float32
HIGH = lax.Precision.HIGHEST

velocities = (
    (0, 0, 0),
    (1, 0, 0),
    (-1, 0, 0),
    (0, 1, 0),
    (0, -1, 0),
    (0, 0, 1),
    (0, 0, -1),
    (1, 1, 0),
    (-1, -1, 0),
    (1, -1, 0),
    (-1, 1, 0),
    (1, 0, 1),
    (-1, 0, -1),
    (1, 0, -1),
    (-1, 0, 1),
    (0, 1, 1),
    (0, -1, -1),
    (0, 1, -1),
    (0, -1, 1),
)
opposite = (0, 2, 1, 4, 3, 6, 5, 8, 7, 10, 9, 12, 11, 14, 13, 16, 15, 18, 17)

LEAVE_X = ((1, 7, 9, 11, 13), (2, 8, 10, 12, 14))
LEAVE_Y = ((3, 7, 10, 15, 17), (4, 8, 9, 16, 18))
LEAVE_Z = (5, 6, 11, 12, 13, 14, 15, 16, 17, 18)
CORNERS = {7: (0, 0), 10: (0, 1), 9: (1, 0), 8: (1, 1)}
EARLY = 5
TILES = tuple(slice(128 * t, 128 * t + 128) for t in range(4))


def iota(shape, axis):
    return lax.broadcasted_iota(jnp.int32, shape, axis)


def class_load(counts, lanes):
    volume = (iota((64, lanes), 0).astype(F32) + 1.0) / 64.0
    return jnp.dot(counts, volume, precision=HIGH, preferred_element_type=F32)


def relax_time(load):
    packed = 0.5 * load / (1.0 + load)
    thinned = 1.0 - packed / 0.64
    return 0.5 + 3.0 * (0.04 / (thinned * thinned))


def moments_of(f):
    even = {i: f[i] + f[i + 1] for i in range(1, 19, 2)}
    odd = {i: f[i] - f[i + 1] for i in range(1, 19, 2)}
    xy, xz, yz = even[7] + even[9], even[11] + even[13], even[15] + even[17]
    rho = f[0] + (even[1] + xy) + (even[3] + yz) + (even[5] + xz)
    jx = odd[1] + (odd[7] + odd[9]) + (odd[11] + odd[13])
    jy = odd[3] + (odd[7] - odd[9]) + (odd[15] + odd[17])
    jz = odd[5] + (odd[11] - odd[13]) + (odd[15] - odd[17])
    return even, (xy, xz, yz), rho, (jx, jy, jz)


def equilibrium(eighth, ux, uy, uz):
    tx, ty, tz = eighth * ux, eighth * uy, eighth * uz
    xx, yy, zz = tx * ux, ty * uy, tz * uz
    tx2, ty2 = tx + tx, ty + ty
    cross = (tx2 * uy, tx2 * uz, ty2 * uz)
    base = eighth * (8.0 / 36.0) - (xx + yy + zz) * (1.0 / 3.0)
    bx, by, bz = base + xx, base + yy, base + zz
    sums = (bx + yy, bx + zz, by + zz)
    return base, (bx, by, bz), sums, cross, (tx * (2.0 / 3.0), ty * (2.0 / 3.0), tz * (2.0 / 3.0))


def equilibrium_of(index, terms):
    base, axes, sums, cross, flow = terms
    c = velocities[index]
    nonzero = [a for a in range(3) if c[a] != 0]
    if not nonzero:
        return 12.0 * base
    if len(nonzero) == 1:
        (a,) = nonzero
        even = axes[a] + axes[a]
        odd = flow[a] + flow[a]
        return even + odd if c[a] > 0 else even - odd
    a, b = nonzero
    slot = {(0, 1): 0, (0, 2): 1, (1, 2): 2}[(a, b)]
    even = sums[slot] + cross[slot] if c[a] * c[b] > 0 else sums[slot] - cross[slot]
    odd = flow[a] + flow[b] if c[a] == c[b] else flow[a] - flow[b]
    return even + odd if c[a] > 0 else even - odd


def along_lanes(tiles, step):
    if step == 0:
        return tiles
    lane = iota((8, 128), 1)
    if step > 0:
        moved = [pltpu.roll(v, 1, 1) for v in tiles]
        return [jnp.where(lane == 0, moved[(t + 3) % 4], moved[t]) for t in range(4)]
    moved = [pltpu.roll(v, 127, 1) for v in tiles]
    return [jnp.where(lane == 127, moved[(t + 1) % 4], moved[t]) for t in range(4)]


def along_rows(low, high, step):
    if step == 0:
        return low, high
    row = iota((8, 128), 0)
    if step > 0:
        low, high = pltpu.roll(low, 1, 0), pltpu.roll(high, 1, 0)
        return jnp.where(row == 0, high, low), jnp.where(row == 0, low, high)
    low, high = pltpu.roll(low, 7, 0), pltpu.roll(high, 7, 0)
    return jnp.where(row == 7, high, low), jnp.where(row == 7, low, high)


def break_up(gy, counts, breakage, selection, sums_in, result):
    current = counts[...]
    tau = relax_time(class_load(current, 128))
    factor = (tau - 0.5) / (3.0 * tau * tau)
    row, slot = iota((256, 64), 0), iota((256, 64), 1)
    wanted = ((row // 8) % 16 // 2) * 8 + (row // 128) * 2 + (row // 8) % 2
    pick = jnp.where(slot == wanted, 1.0, 0.0)
    sums = jnp.dot(
        pick, sums_in[...].reshape(64, 128), precision=HIGH, preferred_element_type=F32
    )
    row, lane = iota((256, 128), 0), iota((256, 128), 1)
    sums = jnp.where(lane // 8 == row % 8 + 8 * lax.rem(gy, 2), sums, 0.0)
    sums = jnp.dot(sums, jnp.ones((128, 128), F32), precision=HIGH, preferred_element_type=F32)
    eps = sums * (4.5 / 512.0) * factor
    strength = jnp.sqrt(50.0 * eps + 1e-06)
    gain = strength / (1.0 + strength)
    rate = gain[:, :64] * selection[...][None, :]
    for step in range(SUB):
        lost = rate * current
        born = lax.dot_general(
            lost,
            breakage[...],
            (((1,), (1,)), ((), ())),
            precision=HIGH,
            preferred_element_type=F32,
        )
        current = current + 0.25 * (born - lost)
    result[...] = current


def step_kernel(
    nx,
    ny,
    pop_hbm,
    solid_hbm,
    counts_hbm,
    breakage_hbm,
    selection_hbm,
    moved,
    result,
    pops,
    solid,
    counts,
    breakage,
    selection,
    moments,
    heat_acc,
    sums_out,
    sums_in,
    rate_out,
    rate_in,
    rates,
    staged,
    row_pops,
    row_solid,
    start_out,
    gain_out,
    edge_out,
    y_out,
    ends_in,
    pop_sem,
    solid_sem,
    counts_sem,
    small_sem,
    row_solid_sem,
    row_sem,
    rate_send,
    rate_recv,
    sums_send,
    sums_recv,
    edge_send,
    edge_recv,
    ends_send,
    ends_recv,
):
    gx = lax.axis_index("gx")
    gy = lax.axis_index("gy")
    right, left = lax.rem(gx + 1, nx), lax.rem(gx + nx - 1, nx)
    up, down = lax.rem(gy + 1, ny), lax.rem(gy + ny - 1, ny)
    peers = [lax.rem(gy + d, ny) for d in range(ny)]

    counts_copy = pltpu.make_async_copy(counts_hbm, counts, counts_sem)
    counts_copy.start()
    barrier = pltpu.get_barrier_semaphore()
    partners = [(gx, peers[d]) for d in range(1, ny)]
    partners += [(left, gy), (right, gy)]
    for partner in partners:
        pl.semaphore_signal(barrier, inc=1, device_id=partner, device_id_type=MESH)

    def lanes_of(tile):
        return pl.ds(pl.multiple_of(tile * 128, 128), 128)

    def chunk_copy(chunk, tile):
        rows, lanes = pl.ds(2 * chunk, 2), lanes_of(tile)
        return pltpu.make_async_copy(
            pop_hbm.at[:, rows, :, lanes], pops.at[:, rows, :, lanes], pop_sem.at[chunk, tile]
        )

    def row_solid_copy(side):
        y = 15 if side == 0 else 0
        return pltpu.make_async_copy(
            solid_hbm.at[:, y], row_solid.at[side], row_solid_sem.at[side]
        )

    def row_copy(side, tile):
        y, lanes = 15 if side == 0 else 0, lanes_of(tile)
        return pltpu.make_async_copy(
            pop_hbm.at[:, :, y, lanes], row_pops.at[side, :, :, lanes], row_sem.at[side, tile]
        )

    solid_copy = pltpu.make_async_copy(solid_hbm, solid, solid_sem)
    for side in range(2):
        row_solid_copy(side).start()
    for tile in range(4):
        for side in range(2):
            row_copy(side, tile).start()
    solid_copy.start()
    for chunk in (0, 7, 1, 2, 3, 4, 5, 6):
        for tile in range(4):
            chunk_copy(chunk, tile).start()
    small_copies = (
        pltpu.make_async_copy(breakage_hbm, breakage, small_sem.at[0]),
        pltpu.make_async_copy(selection_hbm, selection, small_sem.at[1]),
    )
    for copy in small_copies:
        copy.start()

    counts_copy.wait()
    row, lane = iota((256, 128), 0), iota((256, 128), 1)
    load = class_load(counts[...], 128)
    load = jnp.where(row % 8 == (lane % 64) // 8, load, 0.0)
    slot, cell = iota((64, 256), 0), iota((64, 256), 1)
    wanted = ((slot % 8) // 4) * 16 + (2 * (slot // 8) + 15 + slot % 4) % 16
    pick = jnp.where(cell // 8 == wanted, 1.0, 0.0)
    load = jnp.dot(pick, load, precision=HIGH, preferred_element_type=F32)
    rate_out[...] = (1.0 / relax_time(load)).reshape(8, 8, 128)
    rate_in[pl.ds(gy, 1)] = rate_out[pl.ds(gy, 1)]

    pl.semaphore_wait(barrier, len(partners))

    def rate_copy(d):
        return pltpu.make_async_remote_copy(
            src_ref=rate_out.at[peers[d]],
            dst_ref=rate_in.at[gy],
            send_sem=rate_send.at[d],
            recv_sem=rate_recv.at[d],
            device_id=(gx, peers[d]),
            device_id_type=MESH,
        )

    for d in range(1, ny):
        rate_copy(d).start()

    heat_acc[...] = jnp.zeros_like(heat_acc)
    sums_out[...] = jnp.zeros_like(sums_out)

    def prepare(kind, side, tile):
        lanes = pl.ds(pl.multiple_of(tile * 128, 128), 128)
        plane = 15 if side == 0 else 0
        for part in range(2):
            rows = slice(8 * part, 8 * part + 8)
            if kind == 0:
                f = [pops[index, plane, rows, lanes] for index in range(19)]
                fluid = solid[plane, rows, lanes] == 0
            else:
                f = [row_pops[side, index, rows, lanes] for index in range(19)]
                fluid = row_solid[side, rows, lanes] == 0
            _, _, rho, flow = moments_of(f)
            inverse = 1.0 / rho
            speed = [component * inverse for component in flow]
            terms = equilibrium(rho * 0.125, *speed)
            for place, index in enumerate((LEAVE_X if kind == 0 else LEAVE_Y)[side]):
                start = jnp.where(fluid, f[index], f[opposite[index]])
                start_out[kind, side, place, rows, lanes] = start
                gain_out[kind, side, place, rows, lanes] = jnp.where(
                    fluid, equilibrium_of(index, terms) - f[index], 0.0
                )
                if kind == 1:
                    y_out[side, place, rows, lanes] = start
            if kind == 1:
                y_out[side, 5, rows, lanes] = jnp.where(fluid, rho, 0.0)
                for axis in range(3):
                    y_out[side, 6 + axis, rows, lanes] = speed[axis]

    def prepare_y(tile, carry):
        for side in range(2):
            row_copy(side, tile).wait()
            prepare(1, side, tile)
        return carry

    def prepare_x(tile, carry):
        for side in range(2):
            chunk_copy(7 * (1 - side), tile).wait()
            prepare(0, side, tile)
        return carry

    for side in range(2):
        row_solid_copy(side).wait()
    lax.fori_loop(0, 4, prepare_y, 0)

    def ends_copy(side, end):
        return pltpu.make_async_remote_copy(
            src_ref=y_out.at[side, :, 15 - 15 * end],
            dst_ref=ends_in.at[side, end],
            send_sem=ends_send.at[side, end],
            recv_sem=ends_recv.at[side, end],
            device_id=(gx, up if side == 0 else down),
            device_id_type=MESH,
        )

    for side in range(2):
        for end in range(2):
            ends_copy(side, end).start()

    solid_copy.wait()

    lax.fori_loop(0, 4, prepare_x, 0)

    def first_pass(chunk, loaded):
        half = chunk // 4

        def one_tile(tile, carry):
            if not loaded:
                chunk_copy(chunk, tile).wait()
            lanes = lanes_of(tile)
            heats = []
            for part in range(4):
                plane, rows = 2 * chunk + part // 2, slice(8 * (part % 2), 8 * (part % 2) + 8)
                f = [pops[index, plane, rows, lanes] for index in range(19)]
                even, (xy, xz, yz), rho, (jx, jy, jz) = moments_of(f)
                inverse = 1.0 / rho
                ux, uy, uz = jx * inverse, jy * inverse, jz * inverse
                third = rho * (1.0 / 3.0)
                pxx = even[1] + (xy + xz) - third - jx * ux
                pyy = even[3] + (xy + yz) - third - jy * uy
                pzz = even[5] + (xz + yz) - third - jz * uz
                pxy = even[7] - even[9] - jx * uy
                pxz = even[11] - even[13] - jx * uz
                pyz = even[15] - even[17] - jy * uz
                off = pxy * pxy + pxz * pxz + pyz * pyz
                square = pxx * pxx + pyy * pyy + pzz * pzz + (off + off)
                heat = square * (inverse * inverse)
                heats.append(jnp.where(solid[plane, rows, lanes] == 0, heat, 0.0))
                for slot, value in enumerate((rho, ux, uy, uz)):
                    moments[slot, plane, rows, lanes] = value
            heat_acc[half * 2, tile] += heats[0] + heats[2]
            heat_acc[half * 2 + 1, tile] += heats[1] + heats[3]
            return carry

        lax.fori_loop(0, 4, one_tile, 0)

    def outer_chunks(step, carry):
        first_pass(step * 7, True)
        return carry

    def inner_chunks(chunk, carry):
        first_pass(chunk, False)
        return carry

    lax.fori_loop(0, 2, outer_chunks, 0)
    lax.fori_loop(1, EARLY, inner_chunks, 0)

    for d in range(1, ny):
        rate_copy(d).wait_recv()
    lane = iota((8, 128), 1)
    for tile in range(4):
        owned = jnp.where(lane < 64, rate_in[2 * tile], rate_in[2 * tile + 1])
        for block in range(8):
            rates[block, tile] = jnp.broadcast_to(owned[block : block + 1], (8, 128))

    def edge_copy(kind, side, place):
        index = (LEAVE_X if kind == 0 else LEAVE_Y)[side][place]
        if kind == 0:
            target = moved.at[index, 1 if side == 0 else 16]
            device = (right if side == 0 else left, gy)
        else:
            first = 1 + velocities[index][0]
            target = moved.at[index, first : first + 16, 0 if side == 0 else 15]
            device = (gx, up if side == 0 else down)
        return pltpu.make_async_remote_copy(
            src_ref=edge_out.at[kind, side, place],
            dst_ref=target,
            send_sem=edge_send.at[kind, side, place],
            recv_sem=edge_recv.at[kind, side, place],
            device_id=device,
            device_id_type=MESH,
        )

    def leave(kind, side, place):
        c = velocities[(LEAVE_X if kind == 0 else LEAVE_Y)[side][place]]
        far = 1 - side
        values = []
        for part in range(2):
            rows = slice(8 * part, 8 * part + 8)
            block = far * 4 + 1 + part if kind == 0 else part * 4 + 1 + far
            tiles = [
                start_out[kind, side, place, rows, TILES[t]]
                + rates[block, t] * gain_out[kind, side, place, rows, TILES[t]]
                for t in range(4)
            ]
            values.append(along_lanes(tiles, c[2]))
        for t in range(4):
            low, high = along_rows(values[0][t], values[1][t], c[1] if kind == 0 else 0)
            edge_out[kind, side, place, 0:8, TILES[t]] = low
            edge_out[kind, side, place, 8:16, TILES[t]] = high

    def leave_corner(index):
        from_y, side = CORNERS[index]
        ends_copy(from_y, side).wait_recv()
        row = 15 * from_y
        for t in range(4):
            cells = ends_in[from_y, side, :, TILES[t]]
            rate = rates[4 * (1 - side) + 3 * from_y, t, 0:1]
            rho, ux, uy, uz = [cells[n : n + 1] for n in range(5, 9)]
            terms = equilibrium((rate * 0.125) * rho, ux, uy, uz)
            kept = jnp.where(rho == 0.0, 1.0, 1.0 - rate)
            place = LEAVE_Y[from_y].index(index)
            edge_out[0, side, LEAVE_X[side].index(index), row : row + 1, TILES[t]] = kept * cells[
                place : place + 1
            ] + equilibrium_of(index, terms)

    for side in range(2):
        for place in (0, 3, 4):
            leave(0, side, place)
            edge_copy(0, side, place).start()

    lax.fori_loop(EARLY, 7, inner_chunks, 0)

    for side in range(2):
        for place in (1, 2):
            leave(0, side, place)
            leave_corner(LEAVE_X[side][place])
            edge_copy(0, side, place).start()
    for place in range(5):
        for side in range(2):
            leave(1, side, place)
            edge_copy(1, side, place).start()

    for tile in range(4):
        sums_out[tile, 0:4, :] = jnp.sum(heat_acc[:, tile], axis=1)
    sums_in[pl.ds(gy, 1)] = sums_out[pl.ds(gy // 2, 1)]

    def sums_copy(d):
        return pltpu.make_async_remote_copy(
            src_ref=sums_out.at[peers[d] // 2],
            dst_ref=sums_in.at[gy],
            send_sem=sums_send.at[d],
            recv_sem=sums_recv.at[d],
            device_id=(gx, peers[d]),
            device_id_type=MESH,
        )

    for d in range(1, ny):
        sums_copy(d).start()

    def put(index, plane, tile, low, high):
        c = velocities[index]
        place, lanes = plane + 1 + c[0], TILES[tile]
        low, high = along_rows(low, high, c[1])
        if c[1] > 0:
            moved[index, place, 1:8, lanes] = low[1:8]
        else:
            moved[index, place, 0:8, lanes] = low
        if c[1] < 0:
            moved[index, place, 8:15, lanes] = high[0:7]
        else:
            moved[index, place, 8:16, lanes] = high

    def collide(plane):
        half = plane // 8
        for tile in range(4):
            lanes = TILES[tile]
            found = []
            for part in range(2):
                rows = slice(8 * part, 8 * part + 8)
                rho, ux, uy, uz = [moments[slot, plane, rows, lanes] for slot in range(4)]
                rate = rates[half * 4 + 1 + part, tile]
                terms = equilibrium((rate * 0.125) * rho, ux, uy, uz)
                fluid = solid[plane, rows, lanes] == 0
                kept = 1.0 - rate
                f = [pops[index, plane, rows, lanes] for index in range(19)]
                found.append(
                    [
                        jnp.where(
                            fluid, kept * f[index] + equilibrium_of(index, terms), f[opposite[index]]
                        )
                        for index in range(19)
                    ]
                )
            for index in range(19):
                low, high = found[0][index], found[1][index]
                if index in LEAVE_Z:
                    staged[LEAVE_Z.index(index), 0:8, lanes] = low
                    staged[LEAVE_Z.index(index), 8:16, lanes] = high
                else:
                    put(index, plane, tile, low, high)

    def run_z(plane):
        for place, index in enumerate(LEAVE_Z):
            low = along_lanes([staged[place, 0:8, TILES[t]] for t in range(4)], velocities[index][2])
            high = along_lanes([staged[place, 8:16, TILES[t]] for t in range(4)], velocities[index][2])
            for t in range(4):
                put(index, plane, t, low[t], high[t])

    collide(0)

    def planes(plane, carry):
        run_z(plane - 1)
        collide(plane)
        return carry

    lax.fori_loop(1, 16, planes, 0)
    run_z(15)

    for copy in small_copies:
        copy.wait()
    for d in range(1, ny):
        sums_copy(d).wait_recv()
    break_up(gy, counts, breakage, selection, sums_in, result)

    for kind in range(2):
        for side in range(2):
            for place in range(5):
                edge_copy(kind, side, place).wait_recv()

    for d in range(1, ny):
        rate_copy(d).wait_send()
        sums_copy(d).wait_send()
    for side in range(2):
        for place in range(5):
            for kind in range(2):
                edge_copy(kind, side, place).wait_send()
        for end in range(2):
            ends_copy(side, end).wait_send()


def finish_kernel(moved, result, read_hbm, next_hbm, read_sem, next_sem):
    copies = [
        pltpu.make_async_copy(moved.at[index, 1:17], read_hbm.at[index], read_sem.at[index])
        for index in range(19)
    ]
    copies.append(pltpu.make_async_copy(result, next_hbm, next_sem))
    for copy in copies:
        copy.start()
    for copy in copies:
        copy.wait()


def per_device(nx, ny, populations, solid, counts, breakage, selection):
    cells = counts.transpose(1, 2, 3, 0).reshape(256, 64)
    any_space = pl.BlockSpec(memory_space=pl.ANY)
    vmem = pl.BlockSpec(memory_space=pltpu.VMEM)
    dma = pltpu.SemaphoreType.DMA
    moved, result = pl.pallas_call(
        functools.partial(step_kernel, nx, ny),
        out_shape=(
            pltpu.VMEM((19, 18, 16, 512), F32),
            pltpu.VMEM((256, 64), F32),
        ),
        in_specs=[any_space] * 5,
        out_specs=(vmem, vmem),
        scratch_shapes=[
            pltpu.VMEM((19, 16, 16, 512), F32),
            pltpu.VMEM((16, 16, 512), jnp.int32),
            pltpu.VMEM((256, 64), F32),
            pltpu.VMEM((64, 64), F32),
            pltpu.VMEM((64,), F32),
            pltpu.VMEM((4, 16, 16, 512), F32),
            pltpu.VMEM((4, 4, 8, 128), F32),
            pltpu.VMEM((4, 8, 128), F32),
            pltpu.VMEM((8, 8, 128), F32),
            pltpu.VMEM((8, 8, 128), F32),
            pltpu.VMEM((8, 8, 128), F32),
            pltpu.VMEM((8, 4, 8, 128), F32),
            pltpu.VMEM((10, 16, 512), F32),
            pltpu.VMEM((2, 19, 16, 512), F32),
            pltpu.VMEM((2, 16, 512), jnp.int32),
            pltpu.VMEM((2, 2, 5, 16, 512), F32),
            pltpu.VMEM((2, 2, 5, 16, 512), F32),
            pltpu.VMEM((2, 2, 5, 16, 512), F32),
            pltpu.VMEM((2, 9, 16, 512), F32),
            pltpu.VMEM((2, 2, 9, 512), F32),
            dma((8, 4)),
            dma,
            dma,
            dma((2,)),
            dma((2,)),
            dma((2, 4)),
            dma((8,)),
            dma((8,)),
            dma((8,)),
            dma((8,)),
            dma((2, 2, 5)),
            dma((2, 2, 5)),
            dma((2, 2)),
            dma((2, 2)),
        ],
        compiler_params=pltpu.CompilerParams(
            collective_id=0, has_side_effects=True, vmem_limit_bytes=40 * 1024 * 1024
        ),
        name="collide",
    )(
        *[
            pltpu.with_memory_space_constraint(x, pltpu.HBM)
            for x in (populations, solid, cells, breakage, selection)
        ]
    )
    read, after = pl.pallas_call(
        finish_kernel,
        out_shape=(
            jax.ShapeDtypeStruct(populations.shape, F32),
            jax.ShapeDtypeStruct(cells.shape, F32),
        ),
        in_specs=[vmem] * 2,
        out_specs=(any_space, any_space),
        scratch_shapes=[dma((19,)), dma],
        compiler_params=pltpu.CompilerParams(vmem_limit_bytes=24 * 1024 * 1024),
        name="finish",
    )(moved, result)
    return (read, after.reshape(2, 16, 8, 64).transpose(3, 0, 1, 2))


def solution(mesh):
    in_specs = (P(None, "gx", "gy", None), P("gx", "gy", None), P(None, "gx", None, "gy"), P(), P())
    out_specs = (P(None, "gx", "gy", None), P(None, "gx", None, "gy"))
    return jax.shard_map(
        functools.partial(per_device, mesh.shape["gx"], mesh.shape["gy"]),
        mesh=mesh,
        in_specs=in_specs,
        out_specs=out_specs,
        check_vma=False,
    )
```

```python
import functools

import jax
import jax.numpy as jnp
from jax import lax
from jax.experimental import pallas as pl
from jax.experimental.pallas import tpu as pltpu
from jax.sharding import PartitionSpec as P

SUB = 4
MESH = pl.DeviceIdType.MESH
F32 = jnp.float32
HIGH = lax.Precision.HIGHEST

velocities = (
    (0, 0, 0),
    (1, 0, 0),
    (-1, 0, 0),
    (0, 1, 0),
    (0, -1, 0),
    (0, 0, 1),
    (0, 0, -1),
    (1, 1, 0),
    (-1, -1, 0),
    (1, -1, 0),
    (-1, 1, 0),
    (1, 0, 1),
    (-1, 0, -1),
    (1, 0, -1),
    (-1, 0, 1),
    (0, 1, 1),
    (0, -1, -1),
    (0, 1, -1),
    (0, -1, 1),
)
opposite = (0, 2, 1, 4, 3, 6, 5, 8, 7, 10, 9, 12, 11, 14, 13, 16, 15, 18, 17)

LEAVE_X = ((1, 7, 9, 11, 13), (2, 8, 10, 12, 14))
LEAVE_Y = ((3, 7, 10, 15, 17), (4, 8, 9, 16, 18))
LEAVE_Z = (5, 6, 11, 12, 13, 14, 15, 16, 17, 18)
CORNERS = {7: (0, 0), 10: (0, 1), 9: (1, 0), 8: (1, 1)}
EARLY = 5
TILES = tuple(slice(128 * t, 128 * t + 128) for t in range(4))


def iota(shape, axis):
    return lax.broadcasted_iota(jnp.int32, shape, axis)


def class_load(counts, lanes):
    volume = (iota((64, lanes), 0).astype(F32) + 1.0) / 64.0
    return jnp.dot(counts, volume, precision=HIGH, preferred_element_type=F32)


def relax_time(load):
    packed = 0.5 * load / (1.0 + load)
    thinned = 1.0 - packed / 0.64
    return 0.5 + 3.0 * (0.04 / (thinned * thinned))


def moments_of(f):
    even = {i: f[i] + f[i + 1] for i in range(1, 19, 2)}
    odd = {i: f[i] - f[i + 1] for i in range(1, 19, 2)}
    xy, xz, yz = even[7] + even[9], even[11] + even[13], even[15] + even[17]
    rho = f[0] + (even[1] + xy) + (even[3] + yz) + (even[5] + xz)
    jx = odd[1] + (odd[7] + odd[9]) + (odd[11] + odd[13])
    jy = odd[3] + (odd[7] - odd[9]) + (odd[15] + odd[17])
    jz = odd[5] + (odd[11] - odd[13]) + (odd[15] - odd[17])
    return even, (xy, xz, yz), rho, (jx, jy, jz)


def equilibrium(eighth, ux, uy, uz):
    tx, ty, tz = eighth * ux, eighth * uy, eighth * uz
    xx, yy, zz = tx * ux, ty * uy, tz * uz
    tx2, ty2 = tx + tx, ty + ty
    cross = (tx2 * uy, tx2 * uz, ty2 * uz)
    base = eighth * (8.0 / 36.0) - (xx + yy + zz) * (1.0 / 3.0)
    bx, by, bz = base + xx, base + yy, base + zz
    sums = (bx + yy, bx + zz, by + zz)
    return base, (bx, by, bz), sums, cross, (tx * (2.0 / 3.0), ty * (2.0 / 3.0), tz * (2.0 / 3.0))


def equilibrium_of(index, terms):
    base, axes, sums, cross, flow = terms
    c = velocities[index]
    nonzero = [a for a in range(3) if c[a] != 0]
    if not nonzero:
        return 12.0 * base
    if len(nonzero) == 1:
        (a,) = nonzero
        even = axes[a] + axes[a]
        odd = flow[a] + flow[a]
        return even + odd if c[a] > 0 else even - odd
    a, b = nonzero
    slot = {(0, 1): 0, (0, 2): 1, (1, 2): 2}[(a, b)]
    even = sums[slot] + cross[slot] if c[a] * c[b] > 0 else sums[slot] - cross[slot]
    odd = flow[a] + flow[b] if c[a] == c[b] else flow[a] - flow[b]
    return even + odd if c[a] > 0 else even - odd


def along_lanes(tiles, step):
    if step == 0:
        return tiles
    lane = iota((8, 128), 1)
    if step > 0:
        moved = [pltpu.roll(v, 1, 1) for v in tiles]
        return [jnp.where(lane == 0, moved[(t + 3) % 4], moved[t]) for t in range(4)]
    moved = [pltpu.roll(v, 127, 1) for v in tiles]
    return [jnp.where(lane == 127, moved[(t + 1) % 4], moved[t]) for t in range(4)]


def along_rows(low, high, step):
    if step == 0:
        return low, high
    row = iota((8, 128), 0)
    if step > 0:
        low, high = pltpu.roll(low, 1, 0), pltpu.roll(high, 1, 0)
        return jnp.where(row == 0, high, low), jnp.where(row == 0, low, high)
    low, high = pltpu.roll(low, 7, 0), pltpu.roll(high, 7, 0)
    return jnp.where(row == 7, high, low), jnp.where(row == 7, low, high)


def break_up(gy, counts, breakage, selection, sums_in, result):
    current = counts[...]
    tau = relax_time(class_load(current, 128))
    factor = (tau - 0.5) / (3.0 * tau * tau)
    row, slot = iota((256, 64), 0), iota((256, 64), 1)
    wanted = ((row // 8) % 16 // 2) * 8 + (row // 128) * 2 + (row // 8) % 2
    pick = jnp.where(slot == wanted, 1.0, 0.0)
    sums = jnp.dot(
        pick, sums_in[...].reshape(64, 128), precision=HIGH, preferred_element_type=F32
    )
    row, lane = iota((256, 128), 0), iota((256, 128), 1)
    sums = jnp.where(lane // 8 == row % 8 + 8 * lax.rem(gy, 2), sums, 0.0)
    sums = jnp.dot(sums, jnp.ones((128, 128), F32), precision=HIGH, preferred_element_type=F32)
    eps = sums * (4.5 / 512.0) * factor
    strength = jnp.sqrt(50.0 * eps + 1e-06)
    gain = strength / (1.0 + strength)
    rate = gain[:, :64] * selection[...][None, :]
    for step in range(SUB):
        lost = rate * current
        born = lax.dot_general(
            lost,
            breakage[...],
            (((1,), (1,)), ((), ())),
            precision=HIGH,
            preferred_element_type=F32,
        )
        current = current + 0.25 * (born - lost)
    result[...] = current


def step_kernel(
    nx,
    ny,
    pop_hbm,
    solid_hbm,
    counts_hbm,
    breakage_hbm,
    selection_hbm,
    moved,
    result,
    pops,
    solid,
    counts,
    breakage,
    selection,
    moments,
    heat_acc,
    sums_out,
    sums_in,
    rate_out,
    rate_in,
    rates,
    staged,
    row_pops,
    row_solid,
    start_out,
    gain_out,
    edge_out,
    y_out,
    ends_in,
    pop_sem,
    solid_sem,
    counts_sem,
    small_sem,
    row_solid_sem,
    row_sem,
    rate_send,
    rate_recv,
    sums_send,
    sums_recv,
    edge_send,
    edge_recv,
    ends_send,
    ends_recv,
):
    gx = lax.axis_index("gx")
    gy = lax.axis_index("gy")
    right, left = lax.rem(gx + 1, nx), lax.rem(gx + nx - 1, nx)
    up, down = lax.rem(gy + 1, ny), lax.rem(gy + ny - 1, ny)
    peers = [lax.rem(gy + d, ny) for d in range(ny)]

    counts_copy = pltpu.make_async_copy(counts_hbm, counts, counts_sem)
    counts_copy.start()
    barrier = pltpu.get_barrier_semaphore()
    partners = [(gx, peers[d]) for d in range(1, ny)]
    partners += [(left, gy), (right, gy)]
    for partner in partners:
        pl.semaphore_signal(barrier, inc=1, device_id=partner, device_id_type=MESH)

    def lanes_of(tile):
        return pl.ds(pl.multiple_of(tile * 128, 128), 128)

    def chunk_copy(chunk, tile):
        rows, lanes = pl.ds(2 * chunk, 2), lanes_of(tile)
        return pltpu.make_async_copy(
            pop_hbm.at[:, rows, :, lanes], pops.at[:, rows, :, lanes], pop_sem.at[chunk, tile]
        )

    def row_solid_copy(side):
        y = 15 if side == 0 else 0
        return pltpu.make_async_copy(
            solid_hbm.at[:, y], row_solid.at[side], row_solid_sem.at[side]
        )

    def row_copy(side, tile):
        y, lanes = 15 if side == 0 else 0, lanes_of(tile)
        return pltpu.make_async_copy(
            pop_hbm.at[:, :, y, lanes], row_pops.at[side, :, :, lanes], row_sem.at[side, tile]
        )

    solid_copy = pltpu.make_async_copy(solid_hbm, solid, solid_sem)
    for side in range(2):
        row_solid_copy(side).start()
    for tile in range(4):
        for side in range(2):
            row_copy(side, tile).start()
    solid_copy.start()
    for chunk in (0, 7, 1, 2, 3, 4, 5, 6):
        for tile in range(4):
            chunk_copy(chunk, tile).start()
    small_copies = (
        pltpu.make_async_copy(breakage_hbm, breakage, small_sem.at[0]),
        pltpu.make_async_copy(selection_hbm, selection, small_sem.at[1]),
    )
    for copy in small_copies:
        copy.start()

    counts_copy.wait()
    row, lane = iota((256, 128), 0), iota((256, 128), 1)
    load = class_load(counts[...], 128)
    load = jnp.where(row % 8 == (lane % 64) // 8, load, 0.0)
    slot, cell = iota((64, 256), 0), iota((64, 256), 1)
    wanted = ((slot % 8) // 4) * 16 + (2 * (slot // 8) + 15 + slot % 4) % 16
    pick = jnp.where(cell // 8 == wanted, 1.0, 0.0)
    load = jnp.dot(pick, load, precision=HIGH, preferred_element_type=F32)
    rate_out[...] = (1.0 / relax_time(load)).reshape(8, 8, 128)
    rate_in[pl.ds(gy, 1)] = rate_out[pl.ds(gy, 1)]

    pl.semaphore_wait(barrier, len(partners))

    def rate_copy(d):
        return pltpu.make_async_remote_copy(
            src_ref=rate_out.at[peers[d]],
            dst_ref=rate_in.at[gy],
            send_sem=rate_send.at[d],
            recv_sem=rate_recv.at[d],
            device_id=(gx, peers[d]),
            device_id_type=MESH,
        )

    for d in range(1, ny):
        rate_copy(d).start()

    heat_acc[...] = jnp.zeros_like(heat_acc)
    sums_out[...] = jnp.zeros_like(sums_out)

    def prepare(kind, side, tile):
        lanes = pl.ds(pl.multiple_of(tile * 128, 128), 128)
        plane = 15 if side == 0 else 0
        for part in range(2):
            rows = slice(8 * part, 8 * part + 8)
            if kind == 0:
                f = [pops[index, plane, rows, lanes] for index in range(19)]
                fluid = solid[plane, rows, lanes] == 0
            else:
                f = [row_pops[side, index, rows, lanes] for index in range(19)]
                fluid = row_solid[side, rows, lanes] == 0
            _, _, rho, flow = moments_of(f)
            inverse = 1.0 / rho
            speed = [component * inverse for component in flow]
            terms = equilibrium(rho * 0.125, *speed)
            for place, index in enumerate((LEAVE_X if kind == 0 else LEAVE_Y)[side]):
                start = jnp.where(fluid, f[index], f[opposite[index]])
                start_out[kind, side, place, rows, lanes] = start
                gain_out[kind, side, place, rows, lanes] = jnp.where(
                    fluid, equilibrium_of(index, terms) - f[index], 0.0
                )
                if kind == 1:
                    y_out[side, place, rows, lanes] = start
            if kind == 1:
                y_out[side, 5, rows, lanes] = jnp.where(fluid, rho, 0.0)
                for axis in range(3):
                    y_out[side, 6 + axis, rows, lanes] = speed[axis]

    def prepare_y(tile, carry):
        for side in range(2):
            row_copy(side, tile).wait()
            prepare(1, side, tile)
        return carry

    def prepare_x(tile, carry):
        for side in range(2):
            chunk_copy(7 * (1 - side), tile).wait()
            prepare(0, side, tile)
        return carry

    for side in range(2):
        row_solid_copy(side).wait()
    lax.fori_loop(0, 4, prepare_y, 0)

    def ends_copy(side, end):
        return pltpu.make_async_remote_copy(
            src_ref=y_out.at[side, :, 15 - 15 * end],
            dst_ref=ends_in.at[side, end],
            send_sem=ends_send.at[side, end],
            recv_sem=ends_recv.at[side, end],
            device_id=(gx, up if side == 0 else down),
            device_id_type=MESH,
        )

    for side in range(2):
        for end in range(2):
            ends_copy(side, end).start()

    solid_copy.wait()

    lax.fori_loop(0, 4, prepare_x, 0)

    def first_pass(chunk, loaded):
        half = chunk // 4

        def one_tile(tile, carry):
            if not loaded:
                chunk_copy(chunk, tile).wait()
            lanes = lanes_of(tile)
            heats = []
            for part in range(4):
                plane, rows = 2 * chunk + part // 2, slice(8 * (part % 2), 8 * (part % 2) + 8)
                f = [pops[index, plane, rows, lanes] for index in range(19)]
                even, (xy, xz, yz), rho, (jx, jy, jz) = moments_of(f)
                inverse = 1.0 / rho
                ux, uy, uz = jx * inverse, jy * inverse, jz * inverse
                third = rho * (1.0 / 3.0)
                pxx = even[1] + (xy + xz) - third - jx * ux
                pyy = even[3] + (xy + yz) - third - jy * uy
                pzz = even[5] + (xz + yz) - third - jz * uz
                pxy = even[7] - even[9] - jx * uy
                pxz = even[11] - even[13] - jx * uz
                pyz = even[15] - even[17] - jy * uz
                off = pxy * pxy + pxz * pxz + pyz * pyz
                square = pxx * pxx + pyy * pyy + pzz * pzz + (off + off)
                heat = square * (inverse * inverse)
                heats.append(jnp.where(solid[plane, rows, lanes] == 0, heat, 0.0))
                for slot, value in enumerate((rho, ux, uy, uz)):
                    moments[slot, plane, rows, lanes] = value
            heat_acc[half * 2, tile] += heats[0] + heats[2]
            heat_acc[half * 2 + 1, tile] += heats[1] + heats[3]
            return carry

        lax.fori_loop(0, 4, one_tile, 0)

    def outer_chunks(step, carry):
        first_pass(step * 7, True)
        return carry

    def inner_chunks(chunk, carry):
        first_pass(chunk, False)
        return carry

    lax.fori_loop(0, 2, outer_chunks, 0)
    lax.fori_loop(1, EARLY, inner_chunks, 0)

    for d in range(1, ny):
        rate_copy(d).wait_recv()
    lane = iota((8, 128), 1)
    for tile in range(4):
        owned = jnp.where(lane < 64, rate_in[2 * tile], rate_in[2 * tile + 1])
        for block in range(8):
            rates[block, tile] = jnp.broadcast_to(owned[block : block + 1], (8, 128))

    def edge_copy(kind, side, place):
        index = (LEAVE_X if kind == 0 else LEAVE_Y)[side][place]
        if kind == 0:
            target = moved.at[index, 1 if side == 0 else 16]
            device = (right if side == 0 else left, gy)
        else:
            first = 1 + velocities[index][0]
            target = moved.at[index, first : first + 16, 0 if side == 0 else 15]
            device = (gx, up if side == 0 else down)
        return pltpu.make_async_remote_copy(
            src_ref=edge_out.at[kind, side, place],
            dst_ref=target,
            send_sem=edge_send.at[kind, side, place],
            recv_sem=edge_recv.at[kind, side, place],
            device_id=device,
            device_id_type=MESH,
        )

    def leave(kind, side, place):
        c = velocities[(LEAVE_X if kind == 0 else LEAVE_Y)[side][place]]
        far = 1 - side
        values = []
        for part in range(2):
            rows = slice(8 * part, 8 * part + 8)
            block = far * 4 + 1 + part if kind == 0 else part * 4 + 1 + far
            tiles = [
                start_out[kind, side, place, rows, TILES[t]]
                + rates[block, t] * gain_out[kind, side, place, rows, TILES[t]]
                for t in range(4)
            ]
            values.append(along_lanes(tiles, c[2]))
        for t in range(4):
            low, high = along_rows(values[0][t], values[1][t], c[1] if kind == 0 else 0)
            edge_out[kind, side, place, 0:8, TILES[t]] = low
            edge_out[kind, side, place, 8:16, TILES[t]] = high

    def leave_corner(index):
        from_y, side = CORNERS[index]
        ends_copy(from_y, side).wait_recv()
        row = 15 * from_y
        for t in range(4):
            cells = ends_in[from_y, side, :, TILES[t]]
            rate = rates[4 * (1 - side) + 3 * from_y, t, 0:1]
            rho, ux, uy, uz = [cells[n : n + 1] for n in range(5, 9)]
            terms = equilibrium((rate * 0.125) * rho, ux, uy, uz)
            kept = jnp.where(rho == 0.0, 1.0, 1.0 - rate)
            place = LEAVE_Y[from_y].index(index)
            edge_out[0, side, LEAVE_X[side].index(index), row : row + 1, TILES[t]] = kept * cells[
                place : place + 1
            ] + equilibrium_of(index, terms)

    for side in range(2):
        for place in (0, 3, 4):
            leave(0, side, place)
            edge_copy(0, side, place).start()

    lax.fori_loop(EARLY, 7, inner_chunks, 0)

    for tile in range(4):
        sums_out[tile, 0:4, :] = jnp.sum(heat_acc[:, tile], axis=1)
    sums_in[pl.ds(gy, 1)] = sums_out[pl.ds(gy // 2, 1)]

    def sums_copy(d):
        return pltpu.make_async_remote_copy(
            src_ref=sums_out.at[peers[d] // 2],
            dst_ref=sums_in.at[gy],
            send_sem=sums_send.at[d],
            recv_sem=sums_recv.at[d],
            device_id=(gx, peers[d]),
            device_id_type=MESH,
        )

    for d in range(1, ny):
        sums_copy(d).start()

    for side in range(2):
        for place in (1, 2):
            leave(0, side, place)
            leave_corner(LEAVE_X[side][place])
            edge_copy(0, side, place).start()
    for place in range(5):
        for side in range(2):
            leave(1, side, place)
            edge_copy(1, side, place).start()

    def put(index, plane, tile, low, high):
        c = velocities[index]
        place, lanes = plane + 1 + c[0], TILES[tile]
        low, high = along_rows(low, high, c[1])
        if c[1] > 0:
            moved[index, place, 1:8, lanes] = low[1:8]
        else:
            moved[index, place, 0:8, lanes] = low
        if c[1] < 0:
            moved[index, place, 8:15, lanes] = high[0:7]
        else:
            moved[index, place, 8:16, lanes] = high

    def collide(plane):
        half = plane // 8
        for tile in range(4):
            lanes = TILES[tile]
            found = []
            for part in range(2):
                rows = slice(8 * part, 8 * part + 8)
                rho, ux, uy, uz = [moments[slot, plane, rows, lanes] for slot in range(4)]
                rate = rates[half * 4 + 1 + part, tile]
                terms = equilibrium((rate * 0.125) * rho, ux, uy, uz)
                fluid = solid[plane, rows, lanes] == 0
                kept = 1.0 - rate
                f = [pops[index, plane, rows, lanes] for index in range(19)]
                found.append(
                    [
                        jnp.where(
                            fluid, kept * f[index] + equilibrium_of(index, terms), f[opposite[index]]
                        )
                        for index in range(19)
                    ]
                )
            for index in range(19):
                low, high = found[0][index], found[1][index]
                if index in LEAVE_Z:
                    staged[LEAVE_Z.index(index), 0:8, lanes] = low
                    staged[LEAVE_Z.index(index), 8:16, lanes] = high
                else:
                    put(index, plane, tile, low, high)

    def run_z(plane):
        for place, index in enumerate(LEAVE_Z):
            low = along_lanes([staged[place, 0:8, TILES[t]] for t in range(4)], velocities[index][2])
            high = along_lanes([staged[place, 8:16, TILES[t]] for t in range(4)], velocities[index][2])
            for t in range(4):
                put(index, plane, t, low[t], high[t])

    collide(0)

    def planes(plane, carry):
        run_z(plane - 1)
        collide(plane)
        return carry

    lax.fori_loop(1, 16, planes, 0)
    run_z(15)

    for copy in small_copies:
        copy.wait()
    for d in range(1, ny):
        sums_copy(d).wait_recv()
    break_up(gy, counts, breakage, selection, sums_in, result)

    for kind in range(2):
        for side in range(2):
            for place in range(5):
                edge_copy(kind, side, place).wait_recv()

    for d in range(1, ny):
        rate_copy(d).wait_send()
        sums_copy(d).wait_send()
    for side in range(2):
        for place in range(5):
            for kind in range(2):
                edge_copy(kind, side, place).wait_send()
        for end in range(2):
            ends_copy(side, end).wait_send()


def finish_kernel(moved, result, read_hbm, next_hbm, read_sem, next_sem):
    copies = [
        pltpu.make_async_copy(moved.at[index, 1:17], read_hbm.at[index], read_sem.at[index])
        for index in range(19)
    ]
    copies.append(pltpu.make_async_copy(result, next_hbm, next_sem))
    for copy in copies:
        copy.start()
    for copy in copies:
        copy.wait()


def per_device(nx, ny, populations, solid, counts, breakage, selection):
    cells = counts.transpose(1, 2, 3, 0).reshape(256, 64)
    any_space = pl.BlockSpec(memory_space=pl.ANY)
    vmem = pl.BlockSpec(memory_space=pltpu.VMEM)
    dma = pltpu.SemaphoreType.DMA
    moved, result = pl.pallas_call(
        functools.partial(step_kernel, nx, ny),
        out_shape=(
            pltpu.VMEM((19, 18, 16, 512), F32),
            pltpu.VMEM((256, 64), F32),
        ),
        in_specs=[any_space] * 5,
        out_specs=(vmem, vmem),
        scratch_shapes=[
            pltpu.VMEM((19, 16, 16, 512), F32),
            pltpu.VMEM((16, 16, 512), jnp.int32),
            pltpu.VMEM((256, 64), F32),
            pltpu.VMEM((64, 64), F32),
            pltpu.VMEM((64,), F32),
            pltpu.VMEM((4, 16, 16, 512), F32),
            pltpu.VMEM((4, 4, 8, 128), F32),
            pltpu.VMEM((4, 8, 128), F32),
            pltpu.VMEM((8, 8, 128), F32),
            pltpu.VMEM((8, 8, 128), F32),
            pltpu.VMEM((8, 8, 128), F32),
            pltpu.VMEM((8, 4, 8, 128), F32),
            pltpu.VMEM((10, 16, 512), F32),
            pltpu.VMEM((2, 19, 16, 512), F32),
            pltpu.VMEM((2, 16, 512), jnp.int32),
            pltpu.VMEM((2, 2, 5, 16, 512), F32),
            pltpu.VMEM((2, 2, 5, 16, 512), F32),
            pltpu.VMEM((2, 2, 5, 16, 512), F32),
            pltpu.VMEM((2, 9, 16, 512), F32),
            pltpu.VMEM((2, 2, 9, 512), F32),
            dma((8, 4)),
            dma,
            dma,
            dma((2,)),
            dma((2,)),
            dma((2, 4)),
            dma((8,)),
            dma((8,)),
            dma((8,)),
            dma((8,)),
            dma((2, 2, 5)),
            dma((2, 2, 5)),
            dma((2, 2)),
            dma((2, 2)),
        ],
        compiler_params=pltpu.CompilerParams(
            collective_id=0, has_side_effects=True, vmem_limit_bytes=40 * 1024 * 1024
        ),
        name="collide",
    )(
        *[
            pltpu.with_memory_space_constraint(x, pltpu.HBM)
            for x in (populations, solid, cells, breakage, selection)
        ]
    )
    read, after = pl.pallas_call(
        finish_kernel,
        out_shape=(
            jax.ShapeDtypeStruct(populations.shape, F32),
            jax.ShapeDtypeStruct(cells.shape, F32),
        ),
        in_specs=[vmem] * 2,
        out_specs=(any_space, any_space),
        scratch_shapes=[dma((19,)), dma],
        compiler_params=pltpu.CompilerParams(vmem_limit_bytes=24 * 1024 * 1024),
        name="finish",
    )(moved, result)
    return (read, after.reshape(2, 16, 8, 64).transpose(3, 0, 1, 2))


def solution(mesh):
    in_specs = (P(None, "gx", "gy", None), P("gx", "gy", None), P(None, "gx", None, "gy"), P(), P())
    out_specs = (P(None, "gx", "gy", None), P(None, "gx", None, "gy"))
    return jax.shard_map(
        functools.partial(per_device, mesh.shape["gx"], mesh.shape["gy"]),
        mesh=mesh,
        in_specs=in_specs,
        out_specs=out_specs,
        check_vma=False,
    )
```

```python
import functools

import jax
import jax.numpy as jnp
from jax import lax
from jax.experimental import pallas as pl
from jax.experimental.pallas import tpu as pltpu
from jax.sharding import PartitionSpec as P

SUB = 4
MESH = pl.DeviceIdType.MESH
F32 = jnp.float32
HIGH = lax.Precision.HIGHEST

velocities = (
    (0, 0, 0),
    (1, 0, 0),
    (-1, 0, 0),
    (0, 1, 0),
    (0, -1, 0),
    (0, 0, 1),
    (0, 0, -1),
    (1, 1, 0),
    (-1, -1, 0),
    (1, -1, 0),
    (-1, 1, 0),
    (1, 0, 1),
    (-1, 0, -1),
    (1, 0, -1),
    (-1, 0, 1),
    (0, 1, 1),
    (0, -1, -1),
    (0, 1, -1),
    (0, -1, 1),
)
opposite = (0, 2, 1, 4, 3, 6, 5, 8, 7, 10, 9, 12, 11, 14, 13, 16, 15, 18, 17)

LEAVE_X = ((1, 7, 9, 11, 13), (2, 8, 10, 12, 14))
LEAVE_Y = ((3, 7, 10, 15, 17), (4, 8, 9, 16, 18))
LEAVE_Z = (5, 6, 11, 12, 13, 14, 15, 16, 17, 18)
CORNERS = {7: (0, 0), 10: (0, 1), 9: (1, 0), 8: (1, 1)}
FLAT = tuple(i for i in range(19) if velocities[i][1] == 0)
TILES = tuple(slice(128 * t, 128 * t + 128) for t in range(4))


def iota(shape, axis):
    return lax.broadcasted_iota(jnp.int32, shape, axis)


def class_load(counts, lanes):
    volume = (iota((64, lanes), 0).astype(F32) + 1.0) / 64.0
    return jnp.dot(counts, volume, precision=HIGH, preferred_element_type=F32)


def relax_time(load):
    packed = 0.5 * load / (1.0 + load)
    thinned = 1.0 - packed / 0.64
    return 0.5 + 3.0 * (0.04 / (thinned * thinned))


def moments_of(f):
    even = {i: f[i] + f[i + 1] for i in range(1, 19, 2)}
    odd = {i: f[i] - f[i + 1] for i in range(1, 19, 2)}
    xy, xz, yz = even[7] + even[9], even[11] + even[13], even[15] + even[17]
    rho = f[0] + (even[1] + xy) + (even[3] + yz) + (even[5] + xz)
    jx = odd[1] + (odd[7] + odd[9]) + (odd[11] + odd[13])
    jy = odd[3] + (odd[7] - odd[9]) + (odd[15] + odd[17])
    jz = odd[5] + (odd[11] - odd[13]) + (odd[15] - odd[17])
    return even, (xy, xz, yz), rho, (jx, jy, jz)


def equilibrium(eighth, ux, uy, uz):
    tx, ty, tz = eighth * ux, eighth * uy, eighth * uz
    xx, yy, zz = tx * ux, ty * uy, tz * uz
    tx2, ty2 = tx + tx, ty + ty
    cross = (tx2 * uy, tx2 * uz, ty2 * uz)
    base = eighth * (8.0 / 36.0) - (xx + yy + zz) * (1.0 / 3.0)
    bx, by, bz = base + xx, base + yy, base + zz
    sums = (bx + yy, bx + zz, by + zz)
    return base, (bx, by, bz), sums, cross, (tx * (2.0 / 3.0), ty * (2.0 / 3.0), tz * (2.0 / 3.0))


def equilibrium_of(index, terms):
    base, axes, sums, cross, flow = terms
    c = velocities[index]
    nonzero = [a for a in range(3) if c[a] != 0]
    if not nonzero:
        return 12.0 * base
    if len(nonzero) == 1:
        (a,) = nonzero
        even = axes[a] + axes[a]
        odd = flow[a] + flow[a]
        return even + odd if c[a] > 0 else even - odd
    a, b = nonzero
    slot = {(0, 1): 0, (0, 2): 1, (1, 2): 2}[(a, b)]
    even = sums[slot] + cross[slot] if c[a] * c[b] > 0 else sums[slot] - cross[slot]
    odd = flow[a] + flow[b] if c[a] == c[b] else flow[a] - flow[b]
    return even + odd if c[a] > 0 else even - odd


def along_lanes(tiles, step):
    if step == 0:
        return tiles
    lane = iota((8, 128), 1)
    if step > 0:
        moved = [pltpu.roll(v, 1, 1) for v in tiles]
        return [jnp.where(lane == 0, moved[(t + 3) % 4], moved[t]) for t in range(4)]
    moved = [pltpu.roll(v, 127, 1) for v in tiles]
    return [jnp.where(lane == 127, moved[(t + 1) % 4], moved[t]) for t in range(4)]


def along_rows(low, high, step):
    if step == 0:
        return low, high
    row = iota((8, 128), 0)
    if step > 0:
        low, high = pltpu.roll(low, 1, 0), pltpu.roll(high, 1, 0)
        return jnp.where(row == 0, high, low), jnp.where(row == 0, low, high)
    low, high = pltpu.roll(low, 7, 0), pltpu.roll(high, 7, 0)
    return jnp.where(row == 7, high, low), jnp.where(row == 7, low, high)


def step_kernel(
    nx,
    ny,
    pop_hbm,
    solid_hbm,
    counts_hbm,
    moved,
    y_rows,
    sums_in,
    pops,
    solid,
    counts,
    moments,
    heat_acc,
    sums_out,
    rate_out,
    rate_in,
    rates,
    staged,
    row_pops,
    row_solid,
    start_out,
    gain_out,
    edge_out,
    y_out,
    y_in,
    ends_in,
    pop_sem,
    solid_sem,
    counts_sem,
    row_solid_sem,
    row_sem,
    rate_send,
    rate_recv,
    sums_send,
    sums_recv,
    edge_send,
    edge_recv,
    y_send,
    y_recv,
    ends_send,
    ends_recv,
):
    gx = lax.axis_index("gx")
    gy = lax.axis_index("gy")
    right, left = lax.rem(gx + 1, nx), lax.rem(gx + nx - 1, nx)
    up, down = lax.rem(gy + 1, ny), lax.rem(gy + ny - 1, ny)
    peers = [lax.rem(gy + d, ny) for d in range(ny)]

    counts_copy = pltpu.make_async_copy(counts_hbm, counts, counts_sem)
    counts_copy.start()
    barrier = pltpu.get_barrier_semaphore()
    partners = [(gx, peers[d]) for d in range(1, ny)]
    partners += [(left, gy), (right, gy)]
    for partner in partners:
        pl.semaphore_signal(barrier, inc=1, device_id=partner, device_id_type=MESH)

    def lanes_of(tile):
        return pl.ds(pl.multiple_of(tile * 128, 128), 128)

    def chunk_copy(chunk, tile):
        rows, lanes = pl.ds(2 * chunk, 2), lanes_of(tile)
        return pltpu.make_async_copy(
            pop_hbm.at[:, rows, :, lanes], pops.at[:, rows, :, lanes], pop_sem.at[chunk, tile]
        )

    def row_solid_copy(side):
        y = 15 if side == 0 else 0
        return pltpu.make_async_copy(
            solid_hbm.at[:, y], row_solid.at[side], row_solid_sem.at[side]
        )

    def row_copy(side, tile):
        y, lanes = 15 if side == 0 else 0, lanes_of(tile)
        return pltpu.make_async_copy(
            pop_hbm.at[:, :, y, lanes], row_pops.at[side, :, :, lanes], row_sem.at[side, tile]
        )

    solid_copy = pltpu.make_async_copy(solid_hbm, solid, solid_sem)
    for side in range(2):
        row_solid_copy(side).start()
    for tile in range(4):
        for side in range(2):
            row_copy(side, tile).start()
    solid_copy.start()
    for chunk in (0, 7, 1, 2, 3, 4, 5, 6):
        for tile in range(4):
            chunk_copy(chunk, tile).start()

    counts_copy.wait()
    row, lane = iota((256, 128), 0), iota((256, 128), 1)
    load = class_load(counts[...], 128)
    load = jnp.where(row % 8 == (lane % 64) // 8, load, 0.0)
    slot, cell = iota((64, 256), 0), iota((64, 256), 1)
    wanted = ((slot % 8) // 4) * 16 + (2 * (slot // 8) + 15 + slot % 4) % 16
    pick = jnp.where(cell // 8 == wanted, 1.0, 0.0)
    load = jnp.dot(pick, load, precision=HIGH, preferred_element_type=F32)
    rate_out[...] = (1.0 / relax_time(load)).reshape(8, 8, 128)
    rate_in[pl.ds(gy, 1)] = rate_out[pl.ds(gy, 1)]

    pl.semaphore_wait(barrier, len(partners))

    def rate_copy(d):
        return pltpu.make_async_remote_copy(
            src_ref=rate_out.at[peers[d]],
            dst_ref=rate_in.at[gy],
            send_sem=rate_send.at[d],
            recv_sem=rate_recv.at[d],
            device_id=(gx, peers[d]),
            device_id_type=MESH,
        )

    for d in range(1, ny):
        rate_copy(d).start()

    heat_acc[...] = jnp.zeros_like(heat_acc)
    sums_out[...] = jnp.zeros_like(sums_out)

    def prepare_y(tile, carry):
        lanes = lanes_of(tile)
        for side in range(2):
            row_copy(side, tile).wait()
            for part in range(2):
                rows = slice(8 * part, 8 * part + 8)
                f = [row_pops[side, index, rows, lanes] for index in range(19)]
                fluid = row_solid[side, rows, lanes] == 0
                _, _, rho, flow = moments_of(f)
                inverse = 1.0 / rho
                for place, index in enumerate(LEAVE_Y[side]):
                    y_out[side, place, rows, lanes] = jnp.where(fluid, f[index], f[opposite[index]])
                y_out[side, 5, rows, lanes] = jnp.where(fluid, rho, 0.0)
                for axis in range(3):
                    y_out[side, 6 + axis, rows, lanes] = flow[axis] * inverse
        return carry

    def y_copy(side):
        return pltpu.make_async_remote_copy(
            src_ref=y_out.at[side],
            dst_ref=y_in.at[side],
            send_sem=y_send.at[side],
            recv_sem=y_recv.at[side],
            device_id=(gx, up if side == 0 else down),
            device_id_type=MESH,
        )

    for side in range(2):
        row_solid_copy(side).wait()
    lax.fori_loop(0, 4, prepare_y, 0)

    def ends_copy(side, end):
        return pltpu.make_async_remote_copy(
            src_ref=y_out.at[side, :, 15 - 15 * end],
            dst_ref=ends_in.at[side, end],
            send_sem=ends_send.at[side, end],
            recv_sem=ends_recv.at[side, end],
            device_id=(gx, up if side == 0 else down),
            device_id_type=MESH,
        )

    for side in range(2):
        for end in range(2):
            ends_copy(side, end).start()
    for side in range(2):
        y_copy(side).start()

    def prepare_x(tile, carry):
        lanes = pl.ds(pl.multiple_of(tile * 128, 128), 128)
        for side in range(2):
            chunk_copy(7 * (1 - side), tile).wait()
            plane = 15 if side == 0 else 0
            for part in range(2):
                rows = slice(8 * part, 8 * part + 8)
                f = [pops[index, plane, rows, lanes] for index in range(19)]
                fluid = solid[plane, rows, lanes] == 0
                _, _, rho, (jx, jy, jz) = moments_of(f)
                inverse = 1.0 / rho
                terms = equilibrium(rho * 0.125, jx * inverse, jy * inverse, jz * inverse)
                for place, index in enumerate(LEAVE_X[side]):
                    start_out[side, place, rows, lanes] = jnp.where(
                        fluid, f[index], f[opposite[index]]
                    )
                    gain_out[side, place, rows, lanes] = jnp.where(
                        fluid, equilibrium_of(index, terms) - f[index], 0.0
                    )
        return carry

    solid_copy.wait()

    lax.fori_loop(0, 4, prepare_x, 0)

    def first_pass(chunk, loaded):
        half = chunk // 4

        def one_tile(tile, carry):
            if not loaded:
                chunk_copy(chunk, tile).wait()
            lanes = lanes_of(tile)
            heats = []
            for part in range(4):
                plane, rows = 2 * chunk + part // 2, slice(8 * (part % 2), 8 * (part % 2) + 8)
                f = [pops[index, plane, rows, lanes] for index in range(19)]
                even, (xy, xz, yz), rho, (jx, jy, jz) = moments_of(f)
                inverse = 1.0 / rho
                ux, uy, uz = jx * inverse, jy * inverse, jz * inverse
                third = rho * (1.0 / 3.0)
                pxx = even[1] + (xy + xz) - third - jx * ux
                pyy = even[3] + (xy + yz) - third - jy * uy
                pzz = even[5] + (xz + yz) - third - jz * uz
                pxy = even[7] - even[9] - jx * uy
                pxz = even[11] - even[13] - jx * uz
                pyz = even[15] - even[17] - jy * uz
                off = pxy * pxy + pxz * pxz + pyz * pyz
                square = pxx * pxx + pyy * pyy + pzz * pzz + (off + off)
                heat = square * (inverse * inverse)
                heats.append(jnp.where(solid[plane, rows, lanes] == 0, heat, 0.0))
                for slot, value in enumerate((rho, ux, uy, uz)):
                    moments[slot, plane, rows, lanes] = value
            heat_acc[half * 2, tile] += heats[0] + heats[2]
            heat_acc[half * 2 + 1, tile] += heats[1] + heats[3]
            return carry

        lax.fori_loop(0, 4, one_tile, 0)

    def outer_chunks(step, carry):
        first_pass(step * 7, True)
        return carry

    def inner_chunks(chunk, carry):
        first_pass(chunk, False)
        return carry

    lax.fori_loop(0, 2, outer_chunks, 0)
    lax.fori_loop(1, 7, inner_chunks, 0)

    for d in range(1, ny):
        rate_copy(d).wait_recv()
    lane = iota((8, 128), 1)
    for tile in range(4):
        owned = jnp.where(lane < 64, rate_in[2 * tile], rate_in[2 * tile + 1])
        for block in range(8):
            rates[block, tile] = jnp.broadcast_to(owned[block : block + 1], (8, 128))

    def edge_copy(side, place):
        return pltpu.make_async_remote_copy(
            src_ref=edge_out.at[side, place],
            dst_ref=moved.at[LEAVE_X[side][place], 1 if side == 0 else 16],
            send_sem=edge_send.at[side, place],
            recv_sem=edge_recv.at[side, place],
            device_id=(right if side == 0 else left, gy),
            device_id_type=MESH,
        )

    def leave(side, place):
        c = velocities[LEAVE_X[side][place]]
        values = []
        for part in range(2):
            rows = slice(8 * part, 8 * part + 8)
            block = (1 - side) * 4 + 1 + part
            tiles = [
                start_out[side, place, rows, TILES[t]]
                + rates[block, t] * gain_out[side, place, rows, TILES[t]]
                for t in range(4)
            ]
            values.append(along_lanes(tiles, c[2]))
        for t in range(4):
            low, high = along_rows(values[0][t], values[1][t], c[1])
            edge_out[side, place, 0:8, TILES[t]] = low
            edge_out[side, place, 8:16, TILES[t]] = high

    def leave_corner(index):
        from_y, side = CORNERS[index]
        ends_copy(from_y, side).wait_recv()
        row = 15 * from_y
        for t in range(4):
            cells = ends_in[from_y, side, :, TILES[t]]
            rate = rates[4 * (1 - side) + 3 * from_y, t, 0:1]
            rho, ux, uy, uz = [cells[n : n + 1] for n in range(5, 9)]
            terms = equilibrium((rate * 0.125) * rho, ux, uy, uz)
            kept = jnp.where(rho == 0.0, 1.0, 1.0 - rate)
            place = LEAVE_Y[from_y].index(index)
            edge_out[side, LEAVE_X[side].index(index), row : row + 1, TILES[t]] = kept * cells[
                place : place + 1
            ] + equilibrium_of(index, terms)

    for place in (0, 3, 4, 1, 2):
        for side in range(2):
            leave(side, place)
            if LEAVE_X[side][place] in CORNERS:
                leave_corner(LEAVE_X[side][place])
            edge_copy(side, place).start()

    for tile in range(4):
        sums_out[tile, 0:4, :] = jnp.sum(heat_acc[:, tile], axis=1)
    sums_in[pl.ds(gy, 1)] = sums_out[pl.ds(gy // 2, 1)]

    def sums_copy(d):
        return pltpu.make_async_remote_copy(
            src_ref=sums_out.at[peers[d] // 2],
            dst_ref=sums_in.at[gy],
            send_sem=sums_send.at[d],
            recv_sem=sums_recv.at[d],
            device_id=(gx, peers[d]),
            device_id_type=MESH,
        )

    for d in range(1, ny):
        sums_copy(d).start()

    def put(index, plane, tile, low, high):
        c = velocities[index]
        place, lanes = plane + 1 + c[0], TILES[tile]
        low, high = along_rows(low, high, c[1])
        moved[index, place, 0:8, lanes] = low
        moved[index, place, 8:16, lanes] = high

    def collide(plane):
        half = plane // 8
        for tile in range(4):
            lanes = TILES[tile]
            found = []
            for part in range(2):
                rows = slice(8 * part, 8 * part + 8)
                rho, ux, uy, uz = [moments[slot, plane, rows, lanes] for slot in range(4)]
                rate = rates[half * 4 + 1 + part, tile]
                terms = equilibrium((rate * 0.125) * rho, ux, uy, uz)
                fluid = solid[plane, rows, lanes] == 0
                kept = 1.0 - rate
                f = [pops[index, plane, rows, lanes] for index in range(19)]
                found.append(
                    [
                        jnp.where(
                            fluid, kept * f[index] + equilibrium_of(index, terms), f[opposite[index]]
                        )
                        for index in range(19)
                    ]
                )
            for index in range(19):
                low, high = found[0][index], found[1][index]
                if index in LEAVE_Z:
                    staged[LEAVE_Z.index(index), 0:8, lanes] = low
                    staged[LEAVE_Z.index(index), 8:16, lanes] = high
                else:
                    put(index, plane, tile, low, high)

    def run_z(plane):
        for place, index in enumerate(LEAVE_Z):
            low = along_lanes([staged[place, 0:8, TILES[t]] for t in range(4)], velocities[index][2])
            high = along_lanes([staged[place, 8:16, TILES[t]] for t in range(4)], velocities[index][2])
            for t in range(4):
                put(index, plane, t, low[t], high[t])

    collide(0)

    def planes(plane, carry):
        run_z(plane - 1)
        collide(plane)
        return carry

    lax.fori_loop(1, 16, planes, 0)
    run_z(15)

    def collide_y(side):
        y_copy(side).wait_recv()
        found = [[[None] * 4 for _ in range(2)] for _ in range(5)]
        for tile in range(4):
            for part in range(2):
                rows = slice(8 * part, 8 * part + 8)
                rate = rates[part * 4 + 3 * side, tile]
                rho, ux, uy, uz = [y_in[side, 5 + n, rows, TILES[tile]] for n in range(4)]
                terms = equilibrium((rate * 0.125) * rho, ux, uy, uz)
                kept = jnp.where(rho == 0.0, 1.0, 1.0 - rate)
                for place, index in enumerate(LEAVE_Y[side]):
                    found[place][part][tile] = kept * y_in[
                        side, place, rows, TILES[tile]
                    ] + equilibrium_of(index, terms)
        for place, index in enumerate(LEAVE_Y[side]):
            c = velocities[index]
            low, high = [along_lanes(found[place][part], c[2]) for part in range(2)]
            for t in range(4):
                first, second = along_rows(low[t], high[t], c[0])
                y_rows[side, place, 0:8, TILES[t]] = first
                y_rows[side, place, 8:16, TILES[t]] = second

    for side in range(2):
        collide_y(side)
    for side in range(2):
        for place in range(5):
            edge_copy(side, place).wait_recv()
    for index, (from_y, side) in CORNERS.items():
        row, end, plane = 15 * from_y, 15 * side, 1 + 15 * side
        y_rows[from_y, LEAVE_Y[from_y].index(index), end : end + 1, :] = moved[
            index, plane, row : row + 1, :
        ]
    for d in range(1, ny):
        sums_copy(d).wait_recv()

    for d in range(1, ny):
        rate_copy(d).wait_send()
        sums_copy(d).wait_send()
    for side in range(2):
        y_copy(side).wait_send()
        for place in range(5):
            edge_copy(side, place).wait_send()
        for end in range(2):
            ends_copy(side, end).wait_send()


def finish_kernel(
    moved,
    y_rows,
    sums_in,
    counts_hbm,
    breakage_hbm,
    selection_hbm,
    read_hbm,
    next_hbm,
    counts,
    breakage,
    selection,
    result,
    small_sem,
    read_sem,
    row_sem,
    next_sem,
):
    copies = [
        pltpu.make_async_copy(moved.at[index, 1:17], read_hbm.at[index], read_sem.at[index])
        for index in LEAVE_Y[0] + LEAVE_Y[1] + FLAT
    ]
    rows = [
        pltpu.make_async_copy(
            y_rows.at[side, place], read_hbm.at[index, :, 15 * side], row_sem.at[side, place]
        )
        for side in range(2)
        for place, index in enumerate(LEAVE_Y[side])
    ]
    loads = [
        pltpu.make_async_copy(counts_hbm, counts, small_sem.at[0]),
        pltpu.make_async_copy(breakage_hbm, breakage, small_sem.at[1]),
        pltpu.make_async_copy(selection_hbm, selection, small_sem.at[2]),
    ]
    for copy in copies + loads:
        copy.start()
    for copy in loads:
        copy.wait()

    gy = lax.axis_index("gy")
    current = counts[...]
    tau = relax_time(class_load(current, 128))
    factor = (tau - 0.5) / (3.0 * tau * tau)
    row, slot = iota((256, 64), 0), iota((256, 64), 1)
    wanted = ((row // 8) % 16 // 2) * 8 + (row // 128) * 2 + (row // 8) % 2
    pick = jnp.where(slot == wanted, 1.0, 0.0)
    sums = jnp.dot(
        pick, sums_in[...].reshape(64, 128), precision=HIGH, preferred_element_type=F32
    )
    row, lane = iota((256, 128), 0), iota((256, 128), 1)
    sums = jnp.where(lane // 8 == row % 8 + 8 * lax.rem(gy, 2), sums, 0.0)
    sums = jnp.dot(sums, jnp.ones((128, 128), F32), precision=HIGH, preferred_element_type=F32)
    eps = sums * (4.5 / 512.0) * factor
    strength = jnp.sqrt(50.0 * eps + 1e-06)
    gain = strength / (1.0 + strength)
    rate = gain[:, :64] * selection[...][None, :]
    for step in range(SUB):
        lost = rate * current
        born = lax.dot_general(
            lost,
            breakage[...],
            (((1,), (1,)), ((), ())),
            precision=HIGH,
            preferred_element_type=F32,
        )
        current = current + 0.25 * (born - lost)
    for copy in copies[:10]:
        copy.wait()
    for copy in rows:
        copy.start()
    result[...] = current
    last = pltpu.make_async_copy(result, next_hbm, next_sem)
    last.start()
    last.wait()
    for copy in copies[10:] + rows:
        copy.wait()


def per_device(nx, ny, populations, solid, counts, breakage, selection):
    cells = counts.transpose(1, 2, 3, 0).reshape(256, 64)
    any_space = pl.BlockSpec(memory_space=pl.ANY)
    vmem = pl.BlockSpec(memory_space=pltpu.VMEM)
    dma = pltpu.SemaphoreType.DMA
    moved, rows, sums = pl.pallas_call(
        functools.partial(step_kernel, nx, ny),
        out_shape=(
            pltpu.VMEM((19, 18, 16, 512), F32),
            pltpu.VMEM((2, 5, 16, 512), F32),
            pltpu.VMEM((8, 8, 128), F32),
        ),
        in_specs=[any_space] * 3,
        out_specs=(vmem, vmem, vmem),
        scratch_shapes=[
            pltpu.VMEM((19, 16, 16, 512), F32),
            pltpu.VMEM((16, 16, 512), jnp.int32),
            pltpu.VMEM((256, 64), F32),
            pltpu.VMEM((4, 16, 16, 512), F32),
            pltpu.VMEM((4, 4, 8, 128), F32),
            pltpu.VMEM((4, 8, 128), F32),
            pltpu.VMEM((8, 8, 128), F32),
            pltpu.VMEM((8, 8, 128), F32),
            pltpu.VMEM((8, 4, 8, 128), F32),
            pltpu.VMEM((10, 16, 512), F32),
            pltpu.VMEM((2, 19, 16, 512), F32),
            pltpu.VMEM((2, 16, 512), jnp.int32),
            pltpu.VMEM((2, 5, 16, 512), F32),
            pltpu.VMEM((2, 5, 16, 512), F32),
            pltpu.VMEM((2, 5, 16, 512), F32),
            pltpu.VMEM((2, 9, 16, 512), F32),
            pltpu.VMEM((2, 9, 16, 512), F32),
            pltpu.VMEM((2, 2, 9, 512), F32),
            dma((8, 4)),
            dma,
            dma,
            dma((2,)),
            dma((2, 4)),
            dma((8,)),
            dma((8,)),
            dma((8,)),
            dma((8,)),
            dma((2, 5)),
            dma((2, 5)),
            dma((2,)),
            dma((2,)),
            dma((2, 2)),
            dma((2, 2)),
        ],
        compiler_params=pltpu.CompilerParams(
            collective_id=0, has_side_effects=True, vmem_limit_bytes=40 * 1024 * 1024
        ),
        name="collide",
    )(*[pltpu.with_memory_space_constraint(x, pltpu.HBM) for x in (populations, solid, cells)])
    read, after = pl.pallas_call(
        finish_kernel,
        out_shape=(
            jax.ShapeDtypeStruct(populations.shape, F32),
            jax.ShapeDtypeStruct(cells.shape, F32),
        ),
        in_specs=[vmem] * 3 + [any_space] * 3,
        out_specs=(any_space, any_space),
        scratch_shapes=[
            pltpu.VMEM((256, 64), F32),
            pltpu.VMEM((64, 64), F32),
            pltpu.VMEM((64,), F32),
            pltpu.VMEM((256, 64), F32),
            dma((3,)),
            dma((19,)),
            dma((2, 5)),
            dma,
        ],
        compiler_params=pltpu.CompilerParams(vmem_limit_bytes=24 * 1024 * 1024),
        name="finish",
    )(moved, rows, sums, cells, breakage, selection)
    return (read, after.reshape(2, 16, 8, 64).transpose(3, 0, 1, 2))


def solution(mesh):
    in_specs = (P(None, "gx", "gy", None), P("gx", "gy", None), P(None, "gx", None, "gy"), P(), P())
    out_specs = (P(None, "gx", "gy", None), P(None, "gx", None, "gy"))
    return jax.shard_map(
        functools.partial(per_device, mesh.shape["gx"], mesh.shape["gy"]),
        mesh=mesh,
        in_specs=in_specs,
        out_specs=out_specs,
        check_vma=False,
    )
```

```python
import functools

import jax
import jax.numpy as jnp
from jax import lax
from jax.experimental import pallas as pl
from jax.experimental.pallas import tpu as pltpu
from jax.sharding import PartitionSpec as P

SUB = 4
MESH = pl.DeviceIdType.MESH
F32 = jnp.float32
HIGH = lax.Precision.HIGHEST

velocities = (
    (0, 0, 0),
    (1, 0, 0),
    (-1, 0, 0),
    (0, 1, 0),
    (0, -1, 0),
    (0, 0, 1),
    (0, 0, -1),
    (1, 1, 0),
    (-1, -1, 0),
    (1, -1, 0),
    (-1, 1, 0),
    (1, 0, 1),
    (-1, 0, -1),
    (1, 0, -1),
    (-1, 0, 1),
    (0, 1, 1),
    (0, -1, -1),
    (0, 1, -1),
    (0, -1, 1),
)
opposite = (0, 2, 1, 4, 3, 6, 5, 8, 7, 10, 9, 12, 11, 14, 13, 16, 15, 18, 17)

LEAVE_X = ((1, 7, 9, 11, 13), (2, 8, 10, 12, 14))
LEAVE_Y = ((3, 7, 10, 15, 17), (4, 8, 9, 16, 18))
LEAVE_Z = (5, 6, 11, 12, 13, 14, 15, 16, 17, 18)
CORNERS = ((7, 1, 1), (10, -1, 1), (9, 1, -1), (8, -1, -1))
FLAT = tuple(i for i in range(19) if velocities[i][1] == 0)
TILES = tuple(slice(128 * t, 128 * t + 128) for t in range(4))


def iota(shape, axis):
    return lax.broadcasted_iota(jnp.int32, shape, axis)


def class_load(counts, lanes):
    volume = (iota((64, lanes), 0).astype(F32) + 1.0) / 64.0
    return jnp.dot(counts, volume, precision=HIGH, preferred_element_type=F32)


def relax_time(load):
    packed = 0.5 * load / (1.0 + load)
    thinned = 1.0 - packed / 0.64
    return 0.5 + 3.0 * (0.04 / (thinned * thinned))


def moments_of(f):
    even = {i: f[i] + f[i + 1] for i in range(1, 19, 2)}
    odd = {i: f[i] - f[i + 1] for i in range(1, 19, 2)}
    xy, xz, yz = even[7] + even[9], even[11] + even[13], even[15] + even[17]
    rho = f[0] + (even[1] + xy) + (even[3] + yz) + (even[5] + xz)
    jx = odd[1] + (odd[7] + odd[9]) + (odd[11] + odd[13])
    jy = odd[3] + (odd[7] - odd[9]) + (odd[15] + odd[17])
    jz = odd[5] + (odd[11] - odd[13]) + (odd[15] - odd[17])
    return even, (xy, xz, yz), rho, (jx, jy, jz)


def equilibrium(eighth, ux, uy, uz):
    tx, ty, tz = eighth * ux, eighth * uy, eighth * uz
    xx, yy, zz = tx * ux, ty * uy, tz * uz
    tx2, ty2 = tx + tx, ty + ty
    cross = (tx2 * uy, tx2 * uz, ty2 * uz)
    base = eighth * (8.0 / 36.0) - (xx + yy + zz) * (1.0 / 3.0)
    bx, by, bz = base + xx, base + yy, base + zz
    sums = (bx + yy, bx + zz, by + zz)
    return base, (bx, by, bz), sums, cross, (tx * (2.0 / 3.0), ty * (2.0 / 3.0), tz * (2.0 / 3.0))


def equilibrium_of(index, terms):
    base, axes, sums, cross, flow = terms
    c = velocities[index]
    nonzero = [a for a in range(3) if c[a] != 0]
    if not nonzero:
        return 12.0 * base
    if len(nonzero) == 1:
        (a,) = nonzero
        even = axes[a] + axes[a]
        odd = flow[a] + flow[a]
        return even + odd if c[a] > 0 else even - odd
    a, b = nonzero
    slot = {(0, 1): 0, (0, 2): 1, (1, 2): 2}[(a, b)]
    even = sums[slot] + cross[slot] if c[a] * c[b] > 0 else sums[slot] - cross[slot]
    odd = flow[a] + flow[b] if c[a] == c[b] else flow[a] - flow[b]
    return even + odd if c[a] > 0 else even - odd


def along_lanes(tiles, step):
    if step == 0:
        return tiles
    lane = iota((8, 128), 1)
    if step > 0:
        moved = [pltpu.roll(v, 1, 1) for v in tiles]
        return [jnp.where(lane == 0, moved[(t + 3) % 4], moved[t]) for t in range(4)]
    moved = [pltpu.roll(v, 127, 1) for v in tiles]
    return [jnp.where(lane == 127, moved[(t + 1) % 4], moved[t]) for t in range(4)]


def along_rows(low, high, step):
    if step == 0:
        return low, high
    row = iota((8, 128), 0)
    if step > 0:
        low, high = pltpu.roll(low, 1, 0), pltpu.roll(high, 1, 0)
        return jnp.where(row == 0, high, low), jnp.where(row == 0, low, high)
    low, high = pltpu.roll(low, 7, 0), pltpu.roll(high, 7, 0)
    return jnp.where(row == 7, high, low), jnp.where(row == 7, low, high)


def step_kernel(
    nx,
    ny,
    pop_hbm,
    solid_hbm,
    counts_hbm,
    moved,
    y_rows,
    sums_in,
    pops,
    solid,
    counts,
    moments,
    heat_acc,
    sums_out,
    rate_out,
    rate_in,
    rates,
    staged,
    row_pops,
    row_solid,
    start_out,
    gain_out,
    edge_out,
    y_out,
    y_in,
    corner_in,
    pop_sem,
    solid_sem,
    counts_sem,
    row_sem,
    rate_send,
    rate_recv,
    sums_send,
    sums_recv,
    edge_send,
    edge_recv,
    y_send,
    y_recv,
    corner_send,
    corner_recv,
):
    gx = lax.axis_index("gx")
    gy = lax.axis_index("gy")
    right, left = lax.rem(gx + 1, nx), lax.rem(gx + nx - 1, nx)
    up, down = lax.rem(gy + 1, ny), lax.rem(gy + ny - 1, ny)
    peers = [lax.rem(gy + d, ny) for d in range(ny)]

    counts_copy = pltpu.make_async_copy(counts_hbm, counts, counts_sem)
    counts_copy.start()
    barrier = pltpu.get_barrier_semaphore()
    partners = [(gx, peers[d]) for d in range(1, ny)]
    partners += [(x, y) for x in (left, right) for y in (gy, up, down)]
    for partner in partners:
        pl.semaphore_signal(barrier, inc=1, device_id=partner, device_id_type=MESH)

    def chunk_copy(chunk):
        rows = pl.ds(2 * chunk, 2)
        return pltpu.make_async_copy(pop_hbm.at[:, rows], pops.at[:, rows], pop_sem.at[chunk])

    def row_copies(side):
        y = 15 if side == 0 else 0
        return (
            pltpu.make_async_copy(solid_hbm.at[:, y], row_solid.at[side], row_sem.at[side, 0]),
            pltpu.make_async_copy(pop_hbm.at[:, :, y], row_pops.at[side], row_sem.at[side, 1]),
        )

    solid_copy = pltpu.make_async_copy(solid_hbm, solid, solid_sem)
    for side in range(2):
        for copy in row_copies(side):
            copy.start()
    solid_copy.start()
    for chunk in (0, 7, 1, 2):
        chunk_copy(chunk).start()

    counts_copy.wait()
    row, lane = iota((256, 128), 0), iota((256, 128), 1)
    load = class_load(counts[...], 128)
    load = jnp.where(row % 8 == (lane % 64) // 8, load, 0.0)
    slot, cell = iota((64, 256), 0), iota((64, 256), 1)
    wanted = ((slot % 8) // 4) * 16 + (2 * (slot // 8) + 15 + slot % 4) % 16
    pick = jnp.where(cell // 8 == wanted, 1.0, 0.0)
    load = jnp.dot(pick, load, precision=HIGH, preferred_element_type=F32)
    rate_out[...] = (1.0 / relax_time(load)).reshape(8, 8, 128)
    rate_in[pl.ds(gy, 1)] = rate_out[pl.ds(gy, 1)]

    pl.semaphore_wait(barrier, len(partners))

    def rate_copy(d):
        return pltpu.make_async_remote_copy(
            src_ref=rate_out.at[peers[d]],
            dst_ref=rate_in.at[gy],
            send_sem=rate_send.at[d],
            recv_sem=rate_recv.at[d],
            device_id=(gx, peers[d]),
            device_id_type=MESH,
        )

    for d in range(1, ny):
        rate_copy(d).start()

    heat_acc[...] = jnp.zeros_like(heat_acc)
    sums_out[...] = jnp.zeros_like(sums_out)

    def prepare_y(tile, carry):
        lanes = pl.ds(pl.multiple_of(tile * 128, 128), 128)
        for side in range(2):
            for part in range(2):
                rows = slice(8 * part, 8 * part + 8)
                f = [row_pops[side, index, rows, lanes] for index in range(19)]
                fluid = row_solid[side, rows, lanes] == 0
                _, _, rho, flow = moments_of(f)
                inverse = 1.0 / rho
                for place, index in enumerate(LEAVE_Y[side]):
                    y_out[side, place, rows, lanes] = jnp.where(fluid, f[index], f[opposite[index]])
                y_out[side, 5, rows, lanes] = jnp.where(fluid, rho, 0.0)
                for axis in range(3):
                    y_out[side, 6 + axis, rows, lanes] = flow[axis] * inverse
        return carry

    def y_copy(side):
        return pltpu.make_async_remote_copy(
            src_ref=y_out.at[side],
            dst_ref=y_in.at[side],
            send_sem=y_send.at[side],
            recv_sem=y_recv.at[side],
            device_id=(gx, up if side == 0 else down),
            device_id_type=MESH,
        )

    for side in range(2):
        for copy in row_copies(side):
            copy.wait()
    lax.fori_loop(0, 4, prepare_y, 0)
    for side in range(2):
        y_copy(side).start()

    def prepare_x(tile, carry):
        lanes = pl.ds(pl.multiple_of(tile * 128, 128), 128)
        for side in range(2):
            plane = 15 if side == 0 else 0
            for part in range(2):
                rows = slice(8 * part, 8 * part + 8)
                f = [pops[index, plane, rows, lanes] for index in range(19)]
                fluid = solid[plane, rows, lanes] == 0
                _, _, rho, (jx, jy, jz) = moments_of(f)
                inverse = 1.0 / rho
                terms = equilibrium(rho * 0.125, jx * inverse, jy * inverse, jz * inverse)
                for place, index in enumerate(LEAVE_X[side]):
                    start_out[side, place, rows, lanes] = jnp.where(
                        fluid, f[index], f[opposite[index]]
                    )
                    gain_out[side, place, rows, lanes] = jnp.where(
                        fluid, equilibrium_of(index, terms) - f[index], 0.0
                    )
        return carry

    solid_copy.wait()
    for chunk in (0, 7):
        chunk_copy(chunk).wait()

    lax.fori_loop(0, 4, prepare_x, 0)

    def first_pass(chunk):
        half = chunk // 4

        def one_tile(tile, carry):
            lanes = pl.ds(pl.multiple_of(tile * 128, 128), 128)
            heats = []
            for part in range(4):
                plane, rows = 2 * chunk + part // 2, slice(8 * (part % 2), 8 * (part % 2) + 8)
                f = [pops[index, plane, rows, lanes] for index in range(19)]
                even, (xy, xz, yz), rho, (jx, jy, jz) = moments_of(f)
                inverse = 1.0 / rho
                ux, uy, uz = jx * inverse, jy * inverse, jz * inverse
                third = rho * (1.0 / 3.0)
                pxx = even[1] + (xy + xz) - third - jx * ux
                pyy = even[3] + (xy + yz) - third - jy * uy
                pzz = even[5] + (xz + yz) - third - jz * uz
                pxy = even[7] - even[9] - jx * uy
                pxz = even[11] - even[13] - jx * uz
                pyz = even[15] - even[17] - jy * uz
                off = pxy * pxy + pxz * pxz + pyz * pyz
                square = pxx * pxx + pyy * pyy + pzz * pzz + (off + off)
                heat = square * (inverse * inverse)
                heats.append(jnp.where(solid[plane, rows, lanes] == 0, heat, 0.0))
                for slot, value in enumerate((rho, ux, uy, uz)):
                    moments[slot, plane, rows, lanes] = value
            heat_acc[half * 2, tile] += heats[0] + heats[2]
            heat_acc[half * 2 + 1, tile] += heats[1] + heats[3]
            return carry

        lax.fori_loop(0, 4, one_tile, 0)

    def outer_chunks(step, carry):
        first_pass(step * 7)
        return carry

    def inner_chunks(chunk, carry):
        chunk_copy(chunk).wait()

        @pl.when(chunk < 5)
        def _():
            chunk_copy(chunk + 2).start()

        first_pass(chunk)
        return carry

    lax.fori_loop(0, 2, outer_chunks, 0)
    lax.fori_loop(1, 7, inner_chunks, 0)

    for tile in range(4):
        sums_out[tile, 0:4, :] = jnp.sum(heat_acc[:, tile], axis=1)
    sums_in[pl.ds(gy, 1)] = sums_out[pl.ds(gy // 2, 1)]

    def sums_copy(d):
        return pltpu.make_async_remote_copy(
            src_ref=sums_out.at[peers[d] // 2],
            dst_ref=sums_in.at[gy],
            send_sem=sums_send.at[d],
            recv_sem=sums_recv.at[d],
            device_id=(gx, peers[d]),
            device_id_type=MESH,
        )

    for d in range(1, ny):
        sums_copy(d).start()

    for d in range(1, ny):
        rate_copy(d).wait_recv()
    lane = iota((8, 128), 1)
    for tile in range(4):
        owned = jnp.where(lane < 64, rate_in[2 * tile], rate_in[2 * tile + 1])
        for block in range(8):
            rates[block, tile] = jnp.broadcast_to(owned[block : block + 1], (8, 128))

    def edge_copy(side, place):
        return pltpu.make_async_remote_copy(
            src_ref=edge_out.at[side, place],
            dst_ref=moved.at[LEAVE_X[side][place], 1 if side == 0 else 16],
            send_sem=edge_send.at[side, place],
            recv_sem=edge_recv.at[side, place],
            device_id=(right if side == 0 else left, gy),
            device_id_type=MESH,
        )

    def corner_copy(slot):
        index, step_x, step_y = CORNERS[slot]
        side = 0 if step_x > 0 else 1
        return pltpu.make_async_remote_copy(
            src_ref=edge_out.at[side, LEAVE_X[side].index(index), 0 if step_y > 0 else 15],
            dst_ref=corner_in.at[slot, 0],
            send_sem=corner_send.at[slot],
            recv_sem=corner_recv.at[slot],
            device_id=(right if step_x > 0 else left, up if step_y > 0 else down),
            device_id_type=MESH,
        )

    def leave(side, place):
        c = velocities[LEAVE_X[side][place]]
        values = []
        for part in range(2):
            rows = slice(8 * part, 8 * part + 8)
            block = (1 - side) * 4 + 1 + part
            tiles = [
                start_out[side, place, rows, TILES[t]]
                + rates[block, t] * gain_out[side, place, rows, TILES[t]]
                for t in range(4)
            ]
            values.append(along_lanes(tiles, c[2]))
        for t in range(4):
            low, high = along_rows(values[0][t], values[1][t], c[1])
            edge_out[side, place, 0:8, TILES[t]] = low
            edge_out[side, place, 8:16, TILES[t]] = high

    for place in (1, 2, 0, 3, 4):
        for side in range(2):
            leave(side, place)
            for slot, corner in enumerate(CORNERS):
                if corner[0] == LEAVE_X[side][place]:
                    corner_copy(slot).start()
            edge_copy(side, place).start()

    def put(index, plane, tile, low, high):
        c = velocities[index]
        place, lanes = plane + 1 + c[0], TILES[tile]
        low, high = along_rows(low, high, c[1])
        moved[index, place, 0:8, lanes] = low
        moved[index, place, 8:16, lanes] = high

    def collide(plane):
        half = plane // 8
        for tile in range(4):
            lanes = TILES[tile]
            found = []
            for part in range(2):
                rows = slice(8 * part, 8 * part + 8)
                rho, ux, uy, uz = [moments[slot, plane, rows, lanes] for slot in range(4)]
                rate = rates[half * 4 + 1 + part, tile]
                terms = equilibrium((rate * 0.125) * rho, ux, uy, uz)
                fluid = solid[plane, rows, lanes] == 0
                kept = 1.0 - rate
                f = [pops[index, plane, rows, lanes] for index in range(19)]
                found.append(
                    [
                        jnp.where(
                            fluid, kept * f[index] + equilibrium_of(index, terms), f[opposite[index]]
                        )
                        for index in range(19)
                    ]
                )
            for index in range(19):
                low, high = found[0][index], found[1][index]
                if index in LEAVE_Z:
                    staged[LEAVE_Z.index(index), 0:8, lanes] = low
                    staged[LEAVE_Z.index(index), 8:16, lanes] = high
                else:
                    put(index, plane, tile, low, high)

    def run_z(plane):
        for place, index in enumerate(LEAVE_Z):
            low = along_lanes([staged[place, 0:8, TILES[t]] for t in range(4)], velocities[index][2])
            high = along_lanes([staged[place, 8:16, TILES[t]] for t in range(4)], velocities[index][2])
            for t in range(4):
                put(index, plane, t, low[t], high[t])

    collide(0)

    def planes(plane, carry):
        run_z(plane - 1)
        collide(plane)
        return carry

    lax.fori_loop(1, 16, planes, 0)
    run_z(15)

    def collide_y(side):
        y_copy(side).wait_recv()
        found = [[[None] * 4 for _ in range(2)] for _ in range(5)]
        for tile in range(4):
            for part in range(2):
                rows = slice(8 * part, 8 * part + 8)
                rate = rates[part * 4 + 3 * side, tile]
                rho, ux, uy, uz = [y_in[side, 5 + n, rows, TILES[tile]] for n in range(4)]
                terms = equilibrium((rate * 0.125) * rho, ux, uy, uz)
                kept = jnp.where(rho == 0.0, 1.0, 1.0 - rate)
                for place, index in enumerate(LEAVE_Y[side]):
                    found[place][part][tile] = kept * y_in[
                        side, place, rows, TILES[tile]
                    ] + equilibrium_of(index, terms)
        for place, index in enumerate(LEAVE_Y[side]):
            c = velocities[index]
            low, high = [along_lanes(found[place][part], c[2]) for part in range(2)]
            for t in range(4):
                first, second = along_rows(low[t], high[t], c[0])
                y_rows[side, place, 0:8, TILES[t]] = first
                y_rows[side, place, 8:16, TILES[t]] = second

    for side in range(2):
        collide_y(side)
    for slot, (index, step_x, step_y) in enumerate(CORNERS):
        corner_copy(slot).wait_recv()
        side, row = (0 if step_y > 0 else 1), (0 if step_x > 0 else 15)
        y_rows[side, LEAVE_Y[side].index(index), row : row + 1, :] = corner_in[slot, 0:1, :]

    for side in range(2):
        for place in range(5):
            edge_copy(side, place).wait_recv()
    for d in range(1, ny):
        sums_copy(d).wait_recv()

    for d in range(1, ny):
        rate_copy(d).wait_send()
        sums_copy(d).wait_send()
    for side in range(2):
        y_copy(side).wait_send()
        for place in range(5):
            edge_copy(side, place).wait_send()
    for slot in range(4):
        corner_copy(slot).wait_send()


def finish_kernel(
    moved,
    y_rows,
    sums_in,
    counts_hbm,
    breakage_hbm,
    selection_hbm,
    read_hbm,
    next_hbm,
    counts,
    breakage,
    selection,
    result,
    small_sem,
    read_sem,
    row_sem,
    next_sem,
):
    copies = [
        pltpu.make_async_copy(moved.at[index, 1:17], read_hbm.at[index], read_sem.at[index])
        for index in LEAVE_Y[0] + LEAVE_Y[1] + FLAT
    ]
    rows = [
        pltpu.make_async_copy(
            y_rows.at[side, place], read_hbm.at[index, :, 15 * side], row_sem.at[side, place]
        )
        for side in range(2)
        for place, index in enumerate(LEAVE_Y[side])
    ]
    loads = [
        pltpu.make_async_copy(counts_hbm, counts, small_sem.at[0]),
        pltpu.make_async_copy(breakage_hbm, breakage, small_sem.at[1]),
        pltpu.make_async_copy(selection_hbm, selection, small_sem.at[2]),
    ]
    for copy in copies + loads:
        copy.start()
    for copy in loads:
        copy.wait()

    gy = lax.axis_index("gy")
    current = counts[...]
    tau = relax_time(class_load(current, 128))
    factor = (tau - 0.5) / (3.0 * tau * tau)
    row, slot = iota((256, 64), 0), iota((256, 64), 1)
    wanted = ((row // 8) % 16 // 2) * 8 + (row // 128) * 2 + (row // 8) % 2
    pick = jnp.where(slot == wanted, 1.0, 0.0)
    sums = jnp.dot(
        pick, sums_in[...].reshape(64, 128), precision=HIGH, preferred_element_type=F32
    )
    row, lane = iota((256, 128), 0), iota((256, 128), 1)
    sums = jnp.where(lane // 8 == row % 8 + 8 * lax.rem(gy, 2), sums, 0.0)
    sums = jnp.dot(sums, jnp.ones((128, 128), F32), precision=HIGH, preferred_element_type=F32)
    eps = sums * (4.5 / 512.0) * factor
    strength = jnp.sqrt(50.0 * eps + 1e-06)
    gain = strength / (1.0 + strength)
    rate = gain[:, :64] * selection[...][None, :]
    for step in range(SUB):
        lost = rate * current
        born = lax.dot_general(
            lost,
            breakage[...],
            (((1,), (1,)), ((), ())),
            precision=HIGH,
            preferred_element_type=F32,
        )
        current = current + 0.25 * (born - lost)
    for copy in copies[:10]:
        copy.wait()
    for copy in rows:
        copy.start()
    result[...] = current
    last = pltpu.make_async_copy(result, next_hbm, next_sem)
    last.start()
    last.wait()
    for copy in copies[10:] + rows:
        copy.wait()


def per_device(nx, ny, populations, solid, counts, breakage, selection):
    cells = counts.transpose(1, 2, 3, 0).reshape(256, 64)
    any_space = pl.BlockSpec(memory_space=pl.ANY)
    vmem = pl.BlockSpec(memory_space=pltpu.VMEM)
    dma = pltpu.SemaphoreType.DMA
    moved, rows, sums = pl.pallas_call(
        functools.partial(step_kernel, nx, ny),
        out_shape=(
            pltpu.VMEM((19, 18, 16, 512), F32),
            pltpu.VMEM((2, 5, 16, 512), F32),
            pltpu.VMEM((8, 8, 128), F32),
        ),
        in_specs=[any_space] * 3,
        out_specs=(vmem, vmem, vmem),
        scratch_shapes=[
            pltpu.VMEM((19, 16, 16, 512), F32),
            pltpu.VMEM((16, 16, 512), jnp.int32),
            pltpu.VMEM((256, 64), F32),
            pltpu.VMEM((4, 16, 16, 512), F32),
            pltpu.VMEM((4, 4, 8, 128), F32),
            pltpu.VMEM((4, 8, 128), F32),
            pltpu.VMEM((8, 8, 128), F32),
            pltpu.VMEM((8, 8, 128), F32),
            pltpu.VMEM((8, 4, 8, 128), F32),
            pltpu.VMEM((10, 16, 512), F32),
            pltpu.VMEM((2, 19, 16, 512), F32),
            pltpu.VMEM((2, 16, 512), jnp.int32),
            pltpu.VMEM((2, 5, 16, 512), F32),
            pltpu.VMEM((2, 5, 16, 512), F32),
            pltpu.VMEM((2, 5, 16, 512), F32),
            pltpu.VMEM((2, 9, 16, 512), F32),
            pltpu.VMEM((2, 9, 16, 512), F32),
            pltpu.VMEM((4, 8, 512), F32),
            dma((8,)),
            dma,
            dma,
            dma((2, 2)),
            dma((8,)),
            dma((8,)),
            dma((8,)),
            dma((8,)),
            dma((2, 5)),
            dma((2, 5)),
            dma((2,)),
            dma((2,)),
            dma((4,)),
            dma((4,)),
        ],
        compiler_params=pltpu.CompilerParams(
            collective_id=0, has_side_effects=True, vmem_limit_bytes=40 * 1024 * 1024
        ),
        name="collide",
    )(*[pltpu.with_memory_space_constraint(x, pltpu.HBM) for x in (populations, solid, cells)])
    read, after = pl.pallas_call(
        finish_kernel,
        out_shape=(
            jax.ShapeDtypeStruct(populations.shape, F32),
            jax.ShapeDtypeStruct(cells.shape, F32),
        ),
        in_specs=[vmem] * 3 + [any_space] * 3,
        out_specs=(any_space, any_space),
        scratch_shapes=[
            pltpu.VMEM((256, 64), F32),
            pltpu.VMEM((64, 64), F32),
            pltpu.VMEM((64,), F32),
            pltpu.VMEM((256, 64), F32),
            dma((3,)),
            dma((19,)),
            dma((2, 5)),
            dma,
        ],
        compiler_params=pltpu.CompilerParams(vmem_limit_bytes=24 * 1024 * 1024),
        name="finish",
    )(moved, rows, sums, cells, breakage, selection)
    return (read, after.reshape(2, 16, 8, 64).transpose(3, 0, 1, 2))


def solution(mesh):
    in_specs = (P(None, "gx", "gy", None), P("gx", "gy", None), P(None, "gx", None, "gy"), P(), P())
    out_specs = (P(None, "gx", "gy", None), P(None, "gx", None, "gy"))
    return jax.shard_map(
        functools.partial(per_device, mesh.shape["gx"], mesh.shape["gy"]),
        mesh=mesh,
        in_specs=in_specs,
        out_specs=out_specs,
        check_vma=False,
    )
```
